128 devices in a mesh: ctx: 16 (over z, x_lo, core), tp: 8 (over x_hi, y).
Axes of the slice: x: 4 (x_hi: 2, x_lo: 2; x = x_hi * 2 + x_lo), y: 4, z: 4, core: 2. Of those that a mesh axis runs over, the one named last changes fastest.
Arguments:
- prefill_query: bfloat16 [4096, 12288], P('ctx', 'tp'), may hold values from -400 to 400
- span_latent: bfloat16 [4096, 576], P('ctx'), may hold values from -8 to 8
- prompt_lengths: int32 [8], replicated, may hold values from 1 to 2560, 4096 in all
- key_weight: bfloat16 [512, 8192], P(None, 'tp'), may hold values from -0.25 to 0.25
- value_weight: bfloat16 [512, 8192], P(None, 'tp'), may hold values from -0.25 to 0.25
- placement: int32 [8], replicated, may hold values from 0 to 255, as said below
- resident_cache: bfloat16 [256, 256, 576], P('ctx'), may hold values from -6 to 6
- resident_lengths: int32 [256], P('ctx'), may hold values from 1 to 256, 32768 in all
- decode_query: bfloat16 [256, 2, 12288], P('ctx', None, 'tp'), may hold values from -400 to 400
- decode_latent: bfloat16 [256, 2, 576], P('ctx'), may hold values from -8 to 8
- out_weight: bfloat16 [8192, 7168], P('tp'), may hold values from -0.0625 to 0.0625
Outputs:
- prefill_out: bfloat16 [4096, 8192], P('ctx', 'tp')
- decode_out: bfloat16 [256, 2, 7168], P(('ctx', 'tp'))
The draws below stay inside these ranges and needn't reach their ends.
Inputs may be any that keep to these rules, and one draw needn't show every extreme that they name: `placement`: 8 distinct decode rows, one for each request of the span; row r belongs to decode group r // 16; exactly one group takes 2 requests and every other group at most one; row 0 and row 255 always take a request.
All inputs are finite; a program needn't handle non-finite values. No bound on the sum of `resident_lengths` on one device may be relied on, other than what follows from the above.
Results may differ from the reference program's by a relative error of at most 0.019.
Values may be sent and summed in bfloat16 or wider, within the bound.
A program may use at most 192 MiB of HBM per device.

```python
import math
import jax
import jax.numpy as jnp
import numpy as np
from jax import lax

D = 7168
HEADS = 64
NOPE = 128
ROPE = 64
VHEAD = 128
LATENT = 512
TOK_DEV = 256
ROWS_DEV = 16
CTX_RES = 256
NREQ = 8
STEPS = 2
TOKENS = 4096
PROMPT_MAX = 2560
ROWS = 256
N_CTX = 16


def span_parts(key):
    pick_key = jax.random.fold_in(key, 0)
    latent_key = jax.random.fold_in(key, 1)
    latent = jax.random.normal(latent_key, (TOKENS, LATENT + ROPE), jnp.float32)
    positions = jnp.arange(TOKENS)
    picked = (jax.random.randint(pick_key, (TOKENS,), 0, 64) == 0) & (positions > 0)
    rope_part = latent[:, LATENT:]
    before_pick = jnp.concatenate([picked[1:], jnp.zeros((1,), jnp.bool_)], axis=0)
    rope_part = jnp.where(before_pick[:, None], rope_part, rope_part)
    return jnp.concatenate([latent[:, :LATENT], rope_part], axis=1)


def fresh_parts(key):
    pick_key = jax.random.fold_in(key, 0)
    latent_key = jax.random.fold_in(key, 1)
    latent = jax.random.normal(latent_key, (ROWS, STEPS, LATENT + ROPE), jnp.float32)
    picked = jax.random.randint(pick_key, (ROWS,), 0, 8) == 0
    first_rope = latent[:, 0:1, LATENT:]
    later = jnp.where(picked[:, None, None], latent[:, 1:, LATENT:], latent[:, 1:, LATENT:])
    rope_part = jnp.concatenate([first_rope, later], axis=1)
    return jnp.concatenate([latent[:, :, :LATENT], rope_part], axis=2)


def draw_span_latent(key, part):
    latent = span_parts(key)
    return latent.astype(jnp.bfloat16)


def draw_prefill_query(key, part):
    key = jax.random.fold_in(key, 2)
    queries = 2.0 * jax.random.normal(key, (TOKENS, HEADS, NOPE + ROPE), jnp.float32)
    return queries.reshape(TOKENS, HEADS * (NOPE + ROPE)).astype(jnp.bfloat16)


def draw_decode_latent(key, part):
    latent = fresh_parts(key)
    return latent.astype(jnp.bfloat16)


def draw_decode_query(key, part):
    key = jax.random.fold_in(key, 4)
    queries = 2.0 * jax.random.normal(key, (ROWS, STEPS, HEADS, NOPE + ROPE), jnp.float32)
    return queries.reshape(ROWS, STEPS, HEADS * (NOPE + ROPE)).astype(jnp.bfloat16)


def draw_placement(key, part):
    key = jax.random.fold_in(key, 7)
    group_key, slot_key, second_key, order_key = jax.random.split(key, 4)
    group_count = ROWS // ROWS_DEV
    middle = jax.random.permutation(group_key, group_count - 2) + 1
    chosen_groups = jnp.concatenate([middle[0:1], middle[0:NREQ - 3], jnp.zeros((1,), middle.dtype), jnp.full((1,), group_count - 1, middle.dtype)], axis=0)
    slots = jax.random.randint(slot_key, (NREQ,), 0, ROWS_DEV)
    second = (slots[0] + 1 + jax.random.randint(second_key, (), 0, ROWS_DEV - 1)) % ROWS_DEV
    slots = jnp.concatenate([slots[0:1], second[None], slots[2:NREQ - 2], jnp.zeros((1,), slots.dtype), jnp.full((1,), ROWS_DEV - 1, slots.dtype)], axis=0)
    targets = chosen_groups * ROWS_DEV + slots
    order = jax.random.permutation(order_key, NREQ)
    return targets[order].astype(jnp.int32)


def shard_levels(own_key, extent, pieces, low, largest):
    def one(dim, parts):
        draws = jax.random.uniform(jax.random.fold_in(jax.random.fold_in(own_key, 6), dim), (parts,), jnp.float32, low / len(pieces), largest / len(pieces))
        return jnp.repeat(jnp.exp(draws), extent[dim] // parts).reshape((-1,) + (1,) * (len(extent) - dim - 1))

    gain = one(*pieces[0])
    for cut in pieces[1:]:
        gain = gain * one(*cut)
    return gain


def split_up(count, total, limit, skew):
    portions = [(1 << 20) // math.isqrt(grade ** skew) + 1 for grade in range(2, count + 1)]
    surplus, counts = total - limit - (count - 1), [1] * (count - 1)
    while surplus > 0:
        free = [i for i in range(count - 1) if counts[i] < limit]
        whole, budget = sum([portions[i] for i in free]), surplus
        for i in free:
            extra = min(limit - counts[i], max(1, budget * portions[i] // whole), surplus)
            counts[i] = counts[i] + extra
            surplus = surplus - extra
    return np.array([limit] + counts)


def ragged(rng, count, total, limit, skew):
    if count == 2:
        one = jax.random.randint(rng, (), max(1, total - limit), min(limit, total - 1) + 1)
        return jnp.stack([one, total - one])
    tallies = jnp.asarray(split_up(count, total, limit, skew), jnp.int32)
    pairs = (count - 1) // 2
    source_of, sink = tallies[1:1 + 2 * pairs:2], tallies[2:2 + 2 * pairs:2]
    room = jnp.minimum(source_of - 1, limit - sink)
    shifted = jax.random.randint(jax.random.fold_in(rng, 1), (pairs,), 0, 1 << 20) % (room + 1)
    tallies = tallies.at[1:1 + 2 * pairs:2].set(source_of - shifted).at[2:2 + 2 * pairs:2].set(sink + shifted)
    return tallies[jax.random.permutation(jax.random.fold_in(rng, 2), count)]


def bell_draw(rng, shape, spread, most, shards=(), kind=jnp.bfloat16):
    values = jax.random.normal(rng, shape, jnp.float32) * spread
    if len(shards) > 0:
        values = shard_levels(rng, shape, shards, -0.22, 0.18) * values
    return jnp.clip(values, min=-most, max=most).astype(kind)


def setup_inputs(seed: int = 0) -> dict:
    key_of = jax.random.split(jax.random.key(seed), 12)
    return {
        "prefill_query": draw_prefill_query(jax.random.fold_in(key_of[11], 71), 0),
        "span_latent": draw_span_latent(jax.random.fold_in(key_of[11], 71), 0),
        "prompt_lengths": ragged(key_of[2], NREQ, TOKENS, PROMPT_MAX, 2).astype(jnp.int32),
        "key_weight": bell_draw(key_of[3], (LATENT, HEADS * NOPE), LATENT ** -0.5, 0.25, ((1, 8),)),
        "value_weight": bell_draw(key_of[4], (LATENT, HEADS * VHEAD), LATENT ** -0.5, 0.25, ((1, 8),)),
        "placement": draw_placement(jax.random.fold_in(key_of[11], 71), 0),
        "resident_cache": bell_draw(key_of[6], (ROWS, CTX_RES, LATENT + ROPE), 1.0, 6.0, ((0, 16),)),
        "resident_lengths": ragged(key_of[7], ROWS, ROWS * CTX_RES // 2, CTX_RES, 2).astype(jnp.int32),
        "decode_query": draw_decode_query(jax.random.fold_in(key_of[11], 71), 0),
        "decode_latent": draw_decode_latent(jax.random.fold_in(key_of[11], 71), 0),
        "out_weight": bell_draw(key_of[10], (HEADS * VHEAD, D), (HEADS * VHEAD) ** -0.5, 0.0625, ((0, 8),)),
    }


def product(form, left, right):
    return jnp.einsum(form, lax.optimization_barrier(left).astype(jnp.float32), lax.optimization_barrier(right).astype(jnp.float32))

def segment_ids(positions, request_ends):
    return lax.optimization_barrier(jnp.sum((positions[:, None] >= request_ends[None, :]).astype(jnp.int32), axis=1))

def decode_core(absorbed, query_rope, resident, resident_valid, prompts, prompt_valid, slot_row, fresh_keys, fresh_valid, value_heads, score_scale):
    latent_dim = value_heads.shape[0]
    row_count = absorbed.shape[0]
    onehot = slot_row[:, None] == jnp.arange(row_count, dtype=jnp.int32)[None, :]
    picker = onehot.astype(jnp.bfloat16)
    slot_latent = product('kr,rhl->khl', picker, absorbed).astype(jnp.bfloat16)
    slot_rope = product('kr,rhe->khe', picker, query_rope).astype(jnp.bfloat16)
    res_scores = (product('rhl,rcl->rhc', absorbed, resident[..., :latent_dim]) + product('rhe,rce->rhc', query_rope, resident[..., latent_dim:])) * score_scale
    fresh_scores = (product('rhl,rtl->rht', absorbed, fresh_keys[..., :latent_dim]) + product('rhe,rte->rht', query_rope, fresh_keys[..., latent_dim:])) * score_scale
    slot_scores = (product('khl,kpl->khp', slot_latent, prompts[..., :latent_dim]) + product('khe,kpe->khp', slot_rope, prompts[..., latent_dim:])) * score_scale
    res_mask = resident_valid[:, None, :]
    fresh_mask = fresh_valid[:, None, :]
    slot_mask = prompt_valid[:, None, :]
    res_best = lax.optimization_barrier(jnp.max(jnp.where(res_mask, res_scores, -jnp.inf), axis=2))
    fresh_best = lax.optimization_barrier(jnp.max(jnp.where(fresh_mask, fresh_scores, -jnp.inf), axis=2))
    slot_best = lax.optimization_barrier(jnp.max(jnp.where(slot_mask, slot_scores, -jnp.inf), axis=2))
    routed = onehot[:, :, None]
    slot_best_rows = lax.optimization_barrier(jnp.max(jnp.where(routed, slot_best[:, None, :], -jnp.inf), axis=0))
    row_best = jnp.maximum(jnp.maximum(res_best, fresh_best), slot_best_rows)
    occupied = jnp.any(onehot, axis=1)[:, None]
    slot_shift = jnp.where(occupied, lax.optimization_barrier(jnp.max(jnp.where(routed, row_best[None, :, :], -jnp.inf), axis=1)), 0.0)
    res_weights = jnp.where(res_mask, jnp.exp(res_scores - row_best[:, :, None]), 0.0)
    fresh_weights = jnp.where(fresh_mask, jnp.exp(fresh_scores - row_best[:, :, None]), 0.0)
    slot_weights = jnp.where(slot_mask, jnp.exp(slot_scores - slot_shift[:, :, None]), 0.0)
    slot_total = lax.optimization_barrier(jnp.sum(jnp.where(routed, lax.optimization_barrier(jnp.sum(slot_weights, axis=2))[:, None, :], 0.0), axis=0))
    weight_sum = lax.optimization_barrier(jnp.sum(res_weights, axis=2)) + lax.optimization_barrier(jnp.sum(fresh_weights, axis=2)) + slot_total
    slot_accum = product('khp,kpl->khl', slot_weights.astype(jnp.bfloat16), prompts[..., :latent_dim])
    accumulated = product('rhc,rcl->rhl', res_weights.astype(jnp.bfloat16), resident[..., :latent_dim])
    accumulated = accumulated + product('rht,rtl->rhl', fresh_weights.astype(jnp.bfloat16), fresh_keys[..., :latent_dim])
    accumulated = accumulated + lax.optimization_barrier(jnp.sum(jnp.where(routed[..., None], slot_accum[:, None], 0.0), axis=0))
    latent_out = (accumulated / weight_sum[:, :, None]).astype(jnp.bfloat16)
    return product('rhl,lhv->rhv', latent_out, value_heads).astype(jnp.bfloat16).reshape(row_count, -1)

def reference(prefill_query, span_latent, prompt_lengths, key_weight, value_weight, placement, resident_cache, resident_lengths, decode_query, decode_latent, out_weight):
    score_scale = 1.0 / math.sqrt(NOPE + ROPE)
    key_plain = jnp.dot(span_latent[:, :LATENT], key_weight, preferred_element_type=jnp.float32).astype(jnp.bfloat16).reshape(TOKENS, HEADS, NOPE)
    value_rows = jnp.dot(span_latent[:, :LATENT], value_weight, preferred_element_type=jnp.float32).astype(jnp.bfloat16).reshape(TOKENS, HEADS, VHEAD)
    key_rope = span_latent[:, LATENT:]
    queries = prefill_query.reshape(TOKENS, HEADS, NOPE + ROPE)
    request_ends = jnp.cumsum(prompt_lengths).astype(jnp.int32)
    positions = jnp.arange(TOKENS, dtype=jnp.int32)
    request_id = segment_ids(positions, request_ends)

    def query_block(block_index):
        first_row = (block_index * TOK_DEV).astype(jnp.int32)
        block_query = lax.dynamic_slice_in_dim(queries, first_row, TOK_DEV, 0)
        block_pos = first_row + jnp.arange(TOK_DEV, dtype=jnp.int32)
        block_seg = lax.dynamic_slice_in_dim(request_id, first_row, TOK_DEV, 0)
        scores = (product('qhn,khn->qhk', block_query[:, :, :NOPE], key_plain) + product('qhe,ke->qhk', block_query[:, :, NOPE:], key_rope)) * score_scale
        visible = ((block_seg[:, None] == request_id[None, :]) & (positions[None, :] <= block_pos[:, None]))[:, None, :]
        row_best = lax.optimization_barrier(jnp.max(jnp.where(visible, scores, -jnp.inf), axis=2))
        weights = jnp.where(visible, jnp.exp(scores - row_best[:, :, None]), 0.0)
        weight_sum = lax.optimization_barrier(jnp.sum(weights, axis=2))
        accumulated = product('qhk,khv->qhv', weights.astype(jnp.bfloat16), value_rows)
        return (accumulated / weight_sum[:, :, None]).astype(jnp.bfloat16).reshape(TOK_DEV, HEADS * VHEAD)
    prefill_out = lax.map(query_block, jnp.arange(N_CTX, dtype=jnp.int32)).reshape(TOKENS, HEADS * VHEAD)
    request_starts = (request_ends - prompt_lengths).astype(jnp.int32)
    padded = jnp.concatenate([span_latent, jnp.zeros((PROMPT_MAX, LATENT + ROPE), jnp.bfloat16)], axis=0)
    prompts = jax.vmap(lambda begin: lax.dynamic_slice_in_dim(padded, begin.astype(jnp.int32), PROMPT_MAX, 0))(request_starts)
    offsets = jnp.arange(PROMPT_MAX, dtype=jnp.int32)
    prompt_valid = offsets[None, :] < prompt_lengths[:, None]
    all_rows = jnp.arange(ROWS, dtype=jnp.int32)
    replaced = jnp.any(placement[None, :] == all_rows[:, None], axis=1)
    resident_valid = (jnp.arange(CTX_RES, dtype=jnp.int32)[None, :] < resident_lengths[:, None]) & jnp.logical_not(replaced)[:, None]
    decode_heads = decode_query.reshape(ROWS, STEPS, HEADS, NOPE + ROPE)
    absorbed = product('rshn,lhn->rshl', decode_heads[..., :NOPE], key_weight.reshape(LATENT, HEADS, NOPE)).astype(jnp.bfloat16)
    value_heads = value_weight.reshape(LATENT, HEADS, VHEAD)
    results = []
    for step_index in range(STEPS):
        fresh_valid = jnp.broadcast_to(jnp.arange(STEPS)[None, :] <= step_index, (ROWS, STEPS))
        results.append(decode_core(absorbed[:, step_index], decode_heads[:, step_index, :, NOPE:], resident_cache, resident_valid, prompts, prompt_valid, placement, decode_latent, fresh_valid, value_heads, score_scale))
    head_mixed = jnp.stack(results, axis=1)
    decode_out = product('rsk,kd->rsd', head_mixed, out_weight).astype(jnp.bfloat16)
    return (prefill_out, decode_out)
```

```python
import functools
import math

import jax
import jax.numpy as jnp
from jax import lax
from jax.experimental import pallas as pl
from jax.experimental.pallas import tpu as pltpu
from jax.sharding import PartitionSpec as P

MESH = pl.DeviceIdType.MESH
NOPE = 128
ROPE = 64
LATENT = 512
WIDTH = LATENT + ROPE
BLOCK = 256
N_CTX = 16
N_TP = 8
HEADS = 8
ROWS = 16
STEPS = 2
NREQ = 8
BIG = 1e30
FACTOR = math.log2(math.e) / math.sqrt(NOPE + ROPE)
F32 = jnp.float32
BF16 = jnp.bfloat16
MIB = 1 << 20


def mm(left, right):
    return lax.dot_general(left, right, (((1,), (0,)), ((), ())), preferred_element_type=F32)


def mm_nt(left, right):
    return lax.dot_general(left, right, (((1,), (1,)), ((), ())), preferred_element_type=F32)


def iota(shape, dim):
    return lax.broadcasted_iota(jnp.int32, shape, dim)


def request_table(lens_ref):
    starts, ends, total = [], [], jnp.int32(0)
    for j in range(NREQ):
        starts.append(total)
        total = total + lens_ref[j]
        ends.append(total)
    return starts, ends


def spread(index, values, other):
    out = jnp.full(index.shape, other, jnp.int32)
    for j, value in enumerate(values):
        out = jnp.where(index == j, value, out)
    return out


def chip_parts():
    ctx = lax.axis_index("ctx")
    tp = lax.axis_index("tp")
    return ctx, tp


def gather_kernel(own_ref, all_ref, send_sem, recv_sem, copy_sem):
    ctx, tp = chip_parts()
    barrier = pltpu.get_barrier_semaphore()
    for d in range(1, N_CTX):
        peer = lax.rem(ctx + d, N_CTX)
        pl.semaphore_signal(barrier, inc=1, device_id=(peer, tp), device_id_type=MESH)
    pl.semaphore_wait(barrier, N_CTX - 1)
    mine = all_ref.at[pl.ds(pl.multiple_of(ctx * WIDTH, 64), WIDTH)]
    local = pltpu.make_async_copy(own_ref, mine, copy_sem)
    local.start()

    def copy_to(d):
        return pltpu.make_async_remote_copy(
            src_ref=own_ref,
            dst_ref=mine,
            send_sem=send_sem.at[d],
            recv_sem=recv_sem.at[d],
            device_id=(lax.rem(ctx + d, N_CTX), tp),
            device_id_type=MESH,
        )

    copies = [copy_to(d) for d in range(1, N_CTX)]
    for c in copies:
        c.start()
    local.wait()
    for d in range(1, N_CTX):
        source = lax.rem(ctx - d + N_CTX, N_CTX)
        theirs = all_ref.at[pl.ds(pl.multiple_of(source * WIDTH, 64), WIDTH)]
        pltpu.make_async_copy(own_ref, theirs, recv_sem.at[d]).wait()
    for c in copies:
        c.wait_send()


def gather(latent_t):
    return pl.pallas_call(
        gather_kernel,
        out_shape=jax.ShapeDtypeStruct((N_CTX * WIDTH, BLOCK), BF16),
        in_specs=[pl.BlockSpec(memory_space=pltpu.VMEM)],
        out_specs=pl.BlockSpec(memory_space=pltpu.VMEM),
        scratch_shapes=[
            pltpu.SemaphoreType.DMA((N_CTX,)),
            pltpu.SemaphoreType.DMA((N_CTX,)),
            pltpu.SemaphoreType.DMA,
        ],
        compiler_params=pltpu.CompilerParams(collective_id=0, has_side_effects=True, vmem_limit_bytes=60 * MIB),
        name="gather",
    )(latent_t)


def prepare_weights(wk_ref, wv_ref, wkt, wvt):
    wkt[...] = wk_ref[...].T
    wvt[...] = wv_ref[...].T


def prepare_queries(me, q_ref, starts, ends, qs):
    lane = iota((BLOCK, 256), 1)
    pos = me * BLOCK + iota((BLOCK, 256), 0)
    for odd in range(2):
        slot = lane if odd else lane - 192
        first = spread(slot, starts, 1 << 30)
        last = spread(slot, ends, -1)
        hot = ((pos >= first) & (pos < last)).astype(F32)
        spare = lane < 64 if odd else lane >= 192
        for pair in range(HEADS // 2):
            base = pair * 384 + odd * 128
            window = q_ref[:, base : base + 256].astype(F32)
            qs[2 * pair + odd] = jnp.where(spare, hot, window).astype(BF16)


def latent_rows(g_ref, block, first, count):
    return g_ref[pl.ds(pl.multiple_of(block * WIDTH + first, 64), count), :]


def attend_pair(pair, causal, me, g_ref, starts, ends, wkt, wvt, qs, kt, vt, best, acc):
    ropes = []
    for half in range(2):
        lat = latent_rows(g_ref, 2 * pair + half, 0, LATENT)
        cols = slice(half * BLOCK, (half + 1) * BLOCK)
        kt[:, cols] = mm(wkt[...], lat).astype(BF16)
        vt[:, cols] = mm(wvt[...], lat).astype(BF16)
        ropes.append(latent_rows(g_ref, 2 * pair + half, LATENT, ROPE))
    rope = jnp.concatenate(ropes, axis=1)
    keys = 2 * BLOCK
    slot = iota((ROPE, keys), 0)
    key_pos = pair * keys + iota((ROPE, keys), 1)
    outside = (slot < NREQ) & ((key_pos < spread(slot, starts, 0)) | (key_pos >= spread(slot, ends, 0)))
    aug = jnp.where(outside, -BIG, 0.0).astype(BF16)
    ones = jnp.ones((NOPE, keys), BF16)
    for h in range(HEADS):
        head = slice(h * NOPE, (h + 1) * NOPE)
        parts = [aug, kt[head, :], rope] if h % 2 else [kt[head, :], rope, aug]
        s = mm(qs[h], jnp.concatenate(parts, axis=0))
        if causal:
            ahead = pair * keys + iota((BLOCK, keys), 1) > me * BLOCK + iota((BLOCK, keys), 0)
            s = jnp.where(ahead, -BIG, s)
        block_best = jnp.max(s, axis=1, keepdims=True) * FACTOR
        values = jnp.concatenate([vt[head, :], ones], axis=0)
        if causal:
            new_best = jnp.broadcast_to(block_best, (BLOCK, 128))
        else:
            new_best = jnp.maximum(best[h], block_best)
        p = jnp.exp2(s * FACTOR - jnp.concatenate([new_best] * 4, axis=1)).astype(BF16)
        gained = mm_nt(p, values)
        if causal:
            acc[h] = gained
        else:
            keep = jnp.exp2(best[h] - new_best)
            acc[h] = acc[h] * jnp.concatenate([keep] * 2, axis=1) + gained
        best[h] = new_best


def finish_prefill(acc, out_ref):
    for h in range(HEADS):
        out_ref[:, h * NOPE : (h + 1) * NOPE] = (acc[h][:, :NOPE] / acc[h][:, NOPE:]).astype(BF16)


def to_row_major(index):
    return (index % HEADS) * (ROWS * STEPS) + index // HEADS


def hot_matrix(condition):
    return condition.astype(F32).astype(BF16)


def decode_queries(dq_ref, wkt, qh, qr):
    rows = ROWS * STEPS
    eye = hot_matrix(iota((ROPE, 128), 0) == iota((ROPE, 128), 1))
    side = jnp.zeros((ROPE, 128), BF16)
    below = jnp.zeros((ROPE, LATENT), BF16)
    for h in range(HEADS):
        base = (h // 2) * 384 + (h % 2) * 128
        window = dq_ref[:, base : base + 256]
        weight = wkt[h * NOPE : (h + 1) * NOPE, :]
        lat = [below, weight, below] if h % 2 else [weight, below, below]
        rot = [side, side, side, eye] if h % 2 else [side, side, eye, side]
        qh[h * rows : (h + 1) * rows, :LATENT] = mm(window, jnp.concatenate(lat, axis=0)).astype(BF16)
        qh[h * rows : (h + 1) * rows, LATENT:] = mm(window, jnp.concatenate(rot, axis=0)).astype(BF16)
    count = rows * HEADS
    order = hot_matrix(to_row_major(iota((count, count), 0)) == iota((count, count), 1))
    qr[...] = mm(order, qh[...]).astype(BF16)


def scores_of(queries, lat, rope):
    return mm(queries[:, :LATENT], lat) + mm(queries[:, LATENT:WIDTH], rope)


def decode_resident(qr, ct_ref, fresh_ref, rlen_ref, sr, ar, lo):
    per = STEPS * HEADS
    for r in range(ROWS):
        rows = slice(r * per, (r + 1) * per)
        sr[rows, :] = scores_of(
            qr[rows, :], ct_ref[r * WIDTH : r * WIDTH + LATENT, :], ct_ref[r * WIDTH + LATENT : (r + 1) * WIDTH, :]
        )
    count = ROWS * per
    row_of = iota((count, BLOCK), 0) // per
    filled = spread(row_of, [rlen_ref[r] for r in range(ROWS)], 0)
    s = jnp.where(iota((count, BLOCK), 1) < filled, sr[...], -BIG) * FACTOR
    fs = mm_nt(qr[:, :LATENT], fresh_ref[:, :LATENT]) + mm_nt(qr[:, LATENT:WIDTH], fresh_ref[:, LATENT:])
    place, col = iota(fs.shape, 0), iota(fs.shape, 1)
    open_ = (place // per == col // STEPS) & (col % STEPS <= (place // HEADS) % STEPS)
    fs = jnp.where(open_, fs, -BIG) * FACTOR
    best = jnp.maximum(jnp.max(s, axis=1, keepdims=True), jnp.max(fs, axis=1, keepdims=True))
    w = jnp.exp2(s - best)
    fw = jnp.exp2(fs - best)
    total = jnp.sum(w, axis=1, keepdims=True) + jnp.sum(fw, axis=1, keepdims=True)
    sr[...] = w
    for r in range(ROWS):
        rows = slice(r * per, (r + 1) * per)
        ar[rows, :] = mm_nt(sr[rows, :].astype(BF16), ct_ref[r * WIDTH : r * WIDTH + LATENT, :])
    lo[...] = ((ar[...] + mm(fw.astype(BF16), fresh_ref[:, :LATENT])) / total).astype(BF16)


def slot_table(me, lens_ref, place_ref, starts):
    rank = jnp.int32(0)
    row = [jnp.int32(-1)] * 2
    first = [jnp.int32(0)] * 2
    length = [jnp.int32(0)] * 2
    for j in range(NREQ):
        there = place_ref[j] // ROWS == me
        for k in range(2):
            hit = there & (rank == k)
            row[k] = jnp.where(hit, place_ref[j] % ROWS, row[k])
            first[k] = jnp.where(hit, starts[j], first[k])
            length[k] = jnp.where(hit, lens_ref[j], length[k])
        rank = rank + there.astype(jnp.int32)
    return row, first, length


def slot_queries(table, qr, qs2):
    per = STEPS * HEADS
    shape = (2 * per, ROWS * per)
    place = iota(shape, 0)
    row = spread(place // per, table[0], -1)
    pick = hot_matrix((row >= 0) & (iota(shape, 1) == row * per + place % per))
    qs2[...] = mm(pick, qr[...]).astype(BF16)


def slot_scores(block, g_ref, qs2, ss):
    ss[block] = scores_of(qs2[...], latent_rows(g_ref, block, 0, LATENT), latent_rows(g_ref, block, LATENT, ROPE))


def decode_slots(table, g_ref, qs2, ss, fresh_ref, lo_ref, out_rows):
    per = STEPS * HEADS
    row, first, length = table
    lines = 2 * per
    slot = iota((lines, BLOCK), 0) // per
    low = spread(slot, first, 0)
    high = low + spread(slot, length, 0)
    fs = mm_nt(qs2[:, :LATENT], fresh_ref[:, :LATENT]) + mm_nt(qs2[:, LATENT:WIDTH], fresh_ref[:, LATENT:])
    place, col = iota(fs.shape, 0), iota(fs.shape, 1)
    open_ = (spread(place // per, row, -1) == col // STEPS) & (col % STEPS <= (place // HEADS) % STEPS)
    fs = jnp.where(open_, fs, -BIG) * FACTOR
    best = jnp.max(fs, axis=1, keepdims=True)
    peak = jnp.full((lines, BLOCK), -BIG, F32)
    for b in range(N_CTX):
        pos = b * BLOCK + iota((lines, BLOCK), 1)
        s = jnp.where((pos >= low) & (pos < high), ss[b] * FACTOR, -BIG)
        ss[b] = s
        peak = jnp.maximum(peak, s)
    best = jnp.maximum(best, jnp.max(peak, axis=1, keepdims=True))
    fw = jnp.exp2(fs - best)
    mass = jnp.zeros((lines, BLOCK), F32)
    total = mm(fw.astype(BF16), fresh_ref[:, :LATENT])
    for b in range(N_CTX):
        w = jnp.exp2(ss[b] - best)
        mass = mass + w
        total = total + mm_nt(w.astype(BF16), latent_rows(g_ref, b, 0, LATENT))
    weight = jnp.sum(mass, axis=1, keepdims=True) + jnp.sum(fw, axis=1, keepdims=True)
    slot_out = (total / weight).astype(BF16)
    shape = (ROWS * per, lines)
    back = iota(shape, 1)
    back_row = spread(back // per, row, -1)
    route = hot_matrix((back_row >= 0) & (iota(shape, 0) == back_row * per + back % per))
    spot = iota((ROWS * per, LATENT), 0) // per
    replaced = (spot == row[0]) | (spot == row[1])
    out_rows[...] = jnp.where(replaced, mm(route, slot_out), lo_ref[...].astype(F32)).astype(BF16)


def head_values(rows_ref, wv_ref, x_ref):
    rows = ROWS * STEPS
    count = rows * HEADS
    order = hot_matrix(iota((count, count), 0) == to_row_major(iota((count, count), 1)))
    lat = mm(order, rows_ref[...]).astype(BF16)
    for h in range(HEADS):
        head = slice(h * NOPE, (h + 1) * NOPE)
        x_ref[:, head] = mm(lat[h * rows : (h + 1) * rows, :], wv_ref[:, head]).astype(BF16)


def attention_kernel(
    me_of,
    lens_ref,
    place_ref,
    rlen_ref,
    q_ref,
    g_ref,
    wk_ref,
    wv_ref,
    ct_ref,
    dq_ref,
    fresh_ref,
    out_ref,
    x_ref,
    wkt,
    wvt,
    qs,
    kt,
    vt,
    best,
    acc,
    qh,
    qr,
    sr,
    ar,
    lo,
    qs2,
    ss,
    lo2,
):
    me = me_of()
    starts, ends = request_table(lens_ref)
    table = slot_table(me, lens_ref, place_ref, starts)
    prepare_weights(wk_ref, wv_ref, wkt, wvt)
    decode_queries(dq_ref, wkt, qh, qr)
    slot_queries(table, qr, qs2)
    decode_resident(qr, ct_ref, fresh_ref, rlen_ref, sr, ar, lo)
    prepare_queries(me, q_ref, starts, ends, qs)
    step = functools.partial(
        attend_pair,
        me=me,
        g_ref=g_ref,
        starts=starts,
        ends=ends,
        wkt=wkt,
        wvt=wvt,
        qs=qs,
        kt=kt,
        vt=vt,
        best=best,
        acc=acc,
    )
    own = me // 2
    step(own, True)

    @pl.loop(jnp.maximum(own - 5, 0), own)
    def _(pair):
        step(pair, False)

    finish_prefill(acc, out_ref)

    @pl.loop(0, N_CTX)
    def _(b):
        slot_scores(b, g_ref, qs2, ss)

    decode_slots(table, g_ref, qs2, ss, fresh_ref, lo, lo2)
    head_values(lo2, wv_ref, x_ref)


def attention(me_of, lens, place, rlen, q, g, wk, wv, ct, dq, fresh):
    smem = pl.BlockSpec(memory_space=pltpu.SMEM)
    vmem = pl.BlockSpec(memory_space=pltpu.VMEM)
    lines = ROWS * STEPS * HEADS
    two = 2 * STEPS * HEADS
    return pl.pallas_call(
        functools.partial(attention_kernel, me_of),
        out_shape=(
            jax.ShapeDtypeStruct((BLOCK, HEADS * NOPE), BF16),
            jax.ShapeDtypeStruct((ROWS * STEPS, HEADS * NOPE), BF16),
        ),
        in_specs=[smem] * 3 + [vmem] * 7,
        out_specs=(vmem, vmem),
        scratch_shapes=[
            pltpu.VMEM((HEADS * NOPE, LATENT), BF16),
            pltpu.VMEM((HEADS * NOPE, LATENT), BF16),
            pltpu.VMEM((HEADS, BLOCK, 256), BF16),
            pltpu.VMEM((HEADS * NOPE, 2 * BLOCK), BF16),
            pltpu.VMEM((HEADS * NOPE, 2 * BLOCK), BF16),
            pltpu.VMEM((HEADS, BLOCK, 128), F32),
            pltpu.VMEM((HEADS, BLOCK, 256), F32),
            pltpu.VMEM((lines, 640), BF16),
            pltpu.VMEM((lines, 640), BF16),
            pltpu.VMEM((lines, BLOCK), F32),
            pltpu.VMEM((lines, LATENT), F32),
            pltpu.VMEM((lines, LATENT), BF16),
            pltpu.VMEM((two, 640), BF16),
            pltpu.VMEM((N_CTX, two, BLOCK), F32),
            pltpu.VMEM((lines, LATENT), BF16),
        ],
        compiler_params=pltpu.CompilerParams(vmem_limit_bytes=60 * MIB),
        name="attention",
    )(lens, place, rlen, q, g, wk, wv, ct, dq, fresh)


CHUNKS = (2048, 2048, 2048, 1024)


def project_kernel(x_ref, w_ref, out_ref, w_buf, send, recv, w_sem, send_sem, recv_sem):
    ctx, tp = chip_parts()
    loads = []
    first = 0
    for c, width in enumerate(CHUNKS):
        cols = slice(first, first + width)
        loads.append(pltpu.make_async_copy(w_ref.at[:, cols], w_buf.at[:, cols], w_sem.at[c]))
        first += width
    for load in loads:
        load.start()
    barrier = pltpu.get_barrier_semaphore()
    for d in range(1, N_TP):
        pl.semaphore_signal(barrier, inc=1, device_id=(ctx, lax.rem(tp + d, N_TP)), device_id_type=MESH)
    pl.semaphore_wait(barrier, N_TP - 1)
    copies = []
    first = 0
    for c, width in enumerate(CHUNKS):
        quarter = width // 4
        q0 = first // 4
        loads[c].wait()
        part = mm(x_ref[...], w_buf[:, first : first + width])
        for p in range(N_TP):
            rows = part[4 * p : 4 * p + 4, :]
            piece = jnp.concatenate([rows[:, k * quarter : (k + 1) * quarter] for k in range(4)], axis=0)
            send[p, :, q0 : q0 + quarter] = piece.astype(BF16)
        for d in range(1, N_TP):
            peer = lax.rem(tp + d, N_TP)
            copy = pltpu.make_async_remote_copy(
                src_ref=send.at[peer, :, q0 : q0 + quarter],
                dst_ref=recv.at[d, :, q0 : q0 + quarter],
                send_sem=send_sem.at[c, d],
                recv_sem=recv_sem.at[c, d],
                device_id=(ctx, peer),
                device_id_type=MESH,
            )
            copy.start()
            copies.append((c, d, copy))
        first += width
    first = 0
    for c, width in enumerate(CHUNKS):
        quarter = width // 4
        q0 = first // 4
        total = send[tp, :, q0 : q0 + quarter].astype(F32)
        for c2, d, copy in copies:
            if c2 == c:
                copy.wait_recv()
                total = total + recv[d, :, q0 : q0 + quarter].astype(F32)
        for k in range(4):
            out_ref[:, first + k * quarter : first + (k + 1) * quarter] = total[4 * k : 4 * k + 4, :].astype(BF16)
        first += width
    for _, _, copy in copies:
        copy.wait_send()


def project(x, w):
    width = w.shape[1]
    return pl.pallas_call(
        project_kernel,
        out_shape=jax.ShapeDtypeStruct((4, width), BF16),
        in_specs=[pl.BlockSpec(memory_space=pltpu.VMEM), pl.BlockSpec(memory_space=pl.ANY)],
        out_specs=pl.BlockSpec(memory_space=pltpu.VMEM),
        scratch_shapes=[
            pltpu.VMEM(w.shape, BF16),
            pltpu.VMEM((N_TP, 16, width // 4), BF16),
            pltpu.VMEM((N_TP, 16, width // 4), BF16),
            pltpu.SemaphoreType.DMA((len(CHUNKS),)),
            pltpu.SemaphoreType.DMA((len(CHUNKS), N_TP)),
            pltpu.SemaphoreType.DMA((len(CHUNKS), N_TP)),
        ],
        compiler_params=pltpu.CompilerParams(collective_id=1, has_side_effects=True, vmem_limit_bytes=60 * MIB),
        name="project",
    )(x, w)


def on_device(
    prefill_query,
    span_latent,
    prompt_lengths,
    key_weight,
    value_weight,
    placement,
    resident_cache,
    resident_lengths,
    decode_query,
    decode_latent,
    out_weight,
):
    latents = gather(span_latent.T)
    cache_t = jnp.swapaxes(resident_cache, 1, 2).reshape(ROWS * WIDTH, BLOCK)
    prefill_out, mixed = attention(
        lambda: lax.axis_index("ctx"),
        prompt_lengths,
        placement,
        resident_lengths,
        prefill_query,
        latents,
        key_weight,
        value_weight,
        cache_t,
        decode_query.reshape(ROWS * STEPS, -1),
        decode_latent.reshape(ROWS * STEPS, -1),
    )
    decode_out = project(mixed, out_weight).reshape(2, STEPS, -1)
    return (prefill_out, decode_out)


def solution(mesh):
    placed = (
        P("ctx", "tp"),
        P("ctx", None),
        P(),
        P(None, "tp"),
        P(None, "tp"),
        P(),
        P("ctx", None, None),
        P("ctx"),
        P("ctx", None, "tp"),
        P("ctx", None, None),
        P("tp", None),
    )
    return jax.shard_map(
        on_device,
        mesh=mesh,
        in_specs=placed,
        out_specs=(P("ctx", "tp"), P(("ctx", "tp"), None, None)),
        check_vma=False,
    )
```

```python
import functools
import math

import jax
import jax.numpy as jnp
from jax import lax
from jax.experimental import pallas as pl
from jax.experimental.pallas import tpu as pltpu
from jax.sharding import PartitionSpec as P

MESH = pl.DeviceIdType.MESH
NOPE = 128
ROPE = 64
LATENT = 512
WIDTH = LATENT + ROPE
BLOCK = 256
N_CTX = 16
N_TP = 8
HEADS = 8
ROWS = 16
STEPS = 2
NREQ = 8
BIG = 1e30
FACTOR = math.log2(math.e) / math.sqrt(NOPE + ROPE)
F32 = jnp.float32
BF16 = jnp.bfloat16
MIB = 1 << 20
HALF = WIDTH // 2
N_Z = 4
N_STATION = 7
CHUNKS = (2048, 2048, 2048, 1024)


def mm(left, right):
    return lax.dot_general(left, right, (((1,), (0,)), ((), ())), preferred_element_type=F32)


def mm_nt(left, right):
    return lax.dot_general(left, right, (((1,), (1,)), ((), ())), preferred_element_type=F32)


def iota(shape, dim):
    return lax.broadcasted_iota(jnp.int32, shape, dim)


def request_table(lens_ref):
    starts, ends, total = [], [], jnp.int32(0)
    for j in range(NREQ):
        starts.append(total)
        total = total + lens_ref[j]
        ends.append(total)
    return starts, ends


def spread(index, values, other):
    out = jnp.full(index.shape, other, jnp.int32)
    for j, value in enumerate(values):
        out = jnp.where(index == j, value, out)
    return out


def prepare_weights(wk_ref, wv_ref, wkt, wvt):
    wkt[...] = wk_ref[...].T
    wvt[...] = wv_ref[...].T


def prepare_queries(me, q_ref, starts, ends, qs):
    lane = iota((BLOCK, 256), 1)
    pos = me * BLOCK + iota((BLOCK, 256), 0)
    for odd in range(2):
        slot = lane if odd else lane - 192
        first = spread(slot, starts, 1 << 30)
        last = spread(slot, ends, -1)
        hot = ((pos >= first) & (pos < last)).astype(F32)
        spare = lane < 64 if odd else lane >= 192
        for pair in range(HEADS // 2):
            base = pair * 384 + odd * 128
            window = q_ref[:, base : base + 256].astype(F32)
            qs[2 * pair + odd] = jnp.where(spare, hot, window).astype(BF16)


def latent_rows(g_ref, block, first, count):
    return g_ref[pl.ds(pl.multiple_of(block * WIDTH + first, 64), count), :]


def attend_pair(pair, causal, me, g_ref, starts, ends, wkt, wvt, qs, kt, vt, best, acc):
    ropes = []
    for half in range(2):
        lat = latent_rows(g_ref, 2 * pair + half, 0, LATENT)
        cols = slice(half * BLOCK, (half + 1) * BLOCK)
        kt[:, cols] = mm(wkt[...], lat).astype(BF16)
        vt[:, cols] = mm(wvt[...], lat).astype(BF16)
        ropes.append(latent_rows(g_ref, 2 * pair + half, LATENT, ROPE))
    rope = jnp.concatenate(ropes, axis=1)
    keys = 2 * BLOCK
    slot = iota((ROPE, keys), 0)
    key_pos = pair * keys + iota((ROPE, keys), 1)
    outside = (slot < NREQ) & ((key_pos < spread(slot, starts, 0)) | (key_pos >= spread(slot, ends, 0)))
    aug = jnp.where(outside, -BIG, 0.0).astype(BF16)
    ones = jnp.ones((NOPE, keys), BF16)
    for h in range(HEADS):
        head = slice(h * NOPE, (h + 1) * NOPE)
        parts = [aug, kt[head, :], rope] if h % 2 else [kt[head, :], rope, aug]
        s = mm(qs[h], jnp.concatenate(parts, axis=0))
        if causal:
            ahead = pair * keys + iota((BLOCK, keys), 1) > me * BLOCK + iota((BLOCK, keys), 0)
            s = jnp.where(ahead, -BIG, s)
        block_best = jnp.max(s, axis=1, keepdims=True) * FACTOR
        values = jnp.concatenate([vt[head, :], ones], axis=0)
        if causal:
            new_best = jnp.broadcast_to(block_best, (BLOCK, 128))
        else:
            new_best = jnp.maximum(best[h], block_best)
        p = jnp.exp2(s * FACTOR - jnp.concatenate([new_best] * 4, axis=1)).astype(BF16)
        gained = mm_nt(p, values)
        if causal:
            acc[h] = gained
        else:
            keep = jnp.exp2(best[h] - new_best)
            acc[h] = acc[h] * jnp.concatenate([keep] * 2, axis=1) + gained
        best[h] = new_best


def finish_prefill(acc, out_ref):
    for h in range(HEADS):
        out_ref[:, h * NOPE : (h + 1) * NOPE] = (acc[h][:, :NOPE] / acc[h][:, NOPE:]).astype(BF16)


def to_row_major(index):
    return (index % HEADS) * (ROWS * STEPS) + index // HEADS


def hot_matrix(condition):
    return condition.astype(F32).astype(BF16)


def decode_queries(dq_ref, wkt, qh, qr):
    rows = ROWS * STEPS
    eye = hot_matrix(iota((ROPE, 128), 0) == iota((ROPE, 128), 1))
    side = jnp.zeros((ROPE, 128), BF16)
    below = jnp.zeros((ROPE, LATENT), BF16)
    for h in range(HEADS):
        base = (h // 2) * 384 + (h % 2) * 128
        window = dq_ref[:, base : base + 256]
        weight = wkt[h * NOPE : (h + 1) * NOPE, :]
        lat = [below, weight, below] if h % 2 else [weight, below, below]
        rot = [side, side, side, eye] if h % 2 else [side, side, eye, side]
        qh[h * rows : (h + 1) * rows, :LATENT] = mm(window, jnp.concatenate(lat, axis=0)).astype(BF16)
        qh[h * rows : (h + 1) * rows, LATENT:] = mm(window, jnp.concatenate(rot, axis=0)).astype(BF16)
    count = rows * HEADS
    order = hot_matrix(to_row_major(iota((count, count), 0)) == iota((count, count), 1))
    qr[...] = mm(order, qh[...]).astype(BF16)


def scores_of(queries, lat, rope):
    return mm(queries[:, :LATENT], lat) + mm(queries[:, LATENT:WIDTH], rope)


def decode_resident(qr, ct_ref, fresh_ref, rlen_ref, sr, ar, lo):
    per = STEPS * HEADS
    for r in range(ROWS):
        rows = slice(r * per, (r + 1) * per)
        sr[rows, :] = scores_of(
            qr[rows, :], ct_ref[r * WIDTH : r * WIDTH + LATENT, :], ct_ref[r * WIDTH + LATENT : (r + 1) * WIDTH, :]
        )
    count = ROWS * per
    row_of = iota((count, BLOCK), 0) // per
    filled = spread(row_of, [rlen_ref[r] for r in range(ROWS)], 0)
    s = jnp.where(iota((count, BLOCK), 1) < filled, sr[...], -BIG) * FACTOR
    fs = mm_nt(qr[:, :LATENT], fresh_ref[:, :LATENT]) + mm_nt(qr[:, LATENT:WIDTH], fresh_ref[:, LATENT:])
    place, col = iota(fs.shape, 0), iota(fs.shape, 1)
    open_ = (place // per == col // STEPS) & (col % STEPS <= (place // HEADS) % STEPS)
    fs = jnp.where(open_, fs, -BIG) * FACTOR
    best = jnp.maximum(jnp.max(s, axis=1, keepdims=True), jnp.max(fs, axis=1, keepdims=True))
    w = jnp.exp2(s - best)
    fw = jnp.exp2(fs - best)
    total = jnp.sum(w, axis=1, keepdims=True) + jnp.sum(fw, axis=1, keepdims=True)
    sr[...] = w
    for r in range(ROWS):
        rows = slice(r * per, (r + 1) * per)
        ar[rows, :] = mm_nt(sr[rows, :].astype(BF16), ct_ref[r * WIDTH : r * WIDTH + LATENT, :])
    lo[...] = ((ar[...] + mm(fw.astype(BF16), fresh_ref[:, :LATENT])) / total).astype(BF16)


def slot_table(me, lens_ref, place_ref, starts):
    rank = jnp.int32(0)
    row = [jnp.int32(-1)] * 2
    first = [jnp.int32(0)] * 2
    length = [jnp.int32(0)] * 2
    for j in range(NREQ):
        there = place_ref[j] // ROWS == me
        for k in range(2):
            hit = there & (rank == k)
            row[k] = jnp.where(hit, place_ref[j] % ROWS, row[k])
            first[k] = jnp.where(hit, starts[j], first[k])
            length[k] = jnp.where(hit, lens_ref[j], length[k])
        rank = rank + there.astype(jnp.int32)
    return row, first, length


def slot_queries(table, qr, qs2):
    per = STEPS * HEADS
    shape = (2 * per, ROWS * per)
    place = iota(shape, 0)
    row = spread(place // per, table[0], -1)
    pick = hot_matrix((row >= 0) & (iota(shape, 1) == row * per + place % per))
    qs2[...] = mm(pick, qr[...]).astype(BF16)


def slot_scores(block, g_ref, qs2, ss):
    ss[block] = scores_of(qs2[...], latent_rows(g_ref, block, 0, LATENT), latent_rows(g_ref, block, LATENT, ROPE))


def decode_slots(table, g_ref, qs2, ss, fresh_ref, lo_ref, out_rows):
    per = STEPS * HEADS
    row, first, length = table
    lines = 2 * per
    slot = iota((lines, BLOCK), 0) // per
    low = spread(slot, first, 0)
    high = low + spread(slot, length, 0)
    fs = mm_nt(qs2[:, :LATENT], fresh_ref[:, :LATENT]) + mm_nt(qs2[:, LATENT:WIDTH], fresh_ref[:, LATENT:])
    place, col = iota(fs.shape, 0), iota(fs.shape, 1)
    open_ = (spread(place // per, row, -1) == col // STEPS) & (col % STEPS <= (place // HEADS) % STEPS)
    fs = jnp.where(open_, fs, -BIG) * FACTOR
    best = jnp.max(fs, axis=1, keepdims=True)
    peak = jnp.full((lines, BLOCK), -BIG, F32)
    for b in range(N_CTX):
        pos = b * BLOCK + iota((lines, BLOCK), 1)
        s = jnp.where((pos >= low) & (pos < high), ss[b] * FACTOR, -BIG)
        ss[b] = s
        peak = jnp.maximum(peak, s)
    best = jnp.maximum(best, jnp.max(peak, axis=1, keepdims=True))
    fw = jnp.exp2(fs - best)
    mass = jnp.zeros((lines, BLOCK), F32)
    total = mm(fw.astype(BF16), fresh_ref[:, :LATENT])
    for b in range(N_CTX):
        w = jnp.exp2(ss[b] - best)
        mass = mass + w
        total = total + mm_nt(w.astype(BF16), latent_rows(g_ref, b, 0, LATENT))
    weight = jnp.sum(mass, axis=1, keepdims=True) + jnp.sum(fw, axis=1, keepdims=True)
    slot_out = (total / weight).astype(BF16)
    shape = (ROWS * per, lines)
    back = iota(shape, 1)
    back_row = spread(back // per, row, -1)
    route = hot_matrix((back_row >= 0) & (iota(shape, 0) == back_row * per + back % per))
    spot = iota((ROWS * per, LATENT), 0) // per
    replaced = (spot == row[0]) | (spot == row[1])
    out_rows[...] = jnp.where(replaced, mm(route, slot_out), lo_ref[...].astype(F32)).astype(BF16)


def head_values(rows_ref, wv_ref, x_ref):
    rows = ROWS * STEPS
    count = rows * HEADS
    order = hot_matrix(iota((count, count), 0) == to_row_major(iota((count, count), 1)))
    lat = mm(order, rows_ref[...]).astype(BF16)
    for h in range(HEADS):
        head = slice(h * NOPE, (h + 1) * NOPE)
        x_ref[:, head] = mm(lat[h * rows : (h + 1) * rows, :], wv_ref[:, head]).astype(BF16)


def z_step(v):
    zz = v // 2
    return (zz * 3) % 5 - (zz // 3) * 2


class Place:
    def __init__(self):
        self.ctx = lax.axis_index("ctx")
        self.tp = lax.axis_index("tp")
        self.core = self.ctx % 2
        self.z = self.ctx // 4
        self.x_lo = (self.ctx // 2) % 2
        self.x = (self.tp // 4) * 2 + self.x_lo
        self.y = self.tp % 4

    def at(self, dz, dx):
        z = (self.z + dz + N_Z) % N_Z
        x = (self.x + dx + 4) % 4
        return ((z * 2 + x % 2) * 2 + self.core, (x // 2) * 4 + self.y)

    def sibling(self):
        return (self.ctx + 1 - 2 * self.core, self.tp)

    def station_pair(self, station):
        v = station + 1
        return ((self.z + z_step(v) + N_Z) % N_Z) * 2 + (self.x_lo + v) % 2


def half_rows(g_ref, block, half):
    return g_ref.at[pl.ds(pl.multiple_of(block * WIDTH + half * HALF, 32), HALF)]


def block_rows(g_ref, block):
    return g_ref.at[pl.ds(pl.multiple_of(block * WIDTH, 64), WIDTH)]


def mega_kernel(
    lens_ref,
    place_ref,
    rlen_ref,
    q_hbm,
    own_hbm,
    wk_hbm,
    wv_hbm,
    ct_hbm,
    dq_hbm,
    fresh_hbm,
    w_hbm,
    out_hbm,
    dec_ref,
    q_ref,
    g_ref,
    wk_ref,
    wv_ref,
    ct_ref,
    dq_ref,
    fresh_ref,
    w_ref,
    out_ref,
    x_ref,
    wkt,
    wvt,
    qs,
    kt,
    vt,
    best,
    acc,
    qh,
    qr,
    sr,
    ar,
    lo,
    qs2,
    ss,
    lo2,
    send,
    recv,
    load_sem,
    w_sem,
    link_send,
    link_recv,
    core_send,
    core_recv,
    sum_send,
    sum_recv,
):
    at = Place()
    me, tp = at.ctx, at.tp
    barrier = pltpu.get_barrier_semaphore()
    peers = [at.sibling()]
    peers += [at.at(dz, dx) for dz in (-1, 1) for dx in (-1, 0, 1)] + [at.at(0, -1), at.at(0, 1)]
    peers += [(me, (tp + d) % N_TP) for d in range(1, N_TP)]
    for peer in peers:
        pl.semaphore_signal(barrier, inc=1, device_id=peer, device_id_type=MESH)

    pairs = [
        (wk_hbm, wk_ref),
        (wv_hbm, wv_ref),
        (dq_hbm, dq_ref),
        (fresh_hbm, fresh_ref),
        (ct_hbm, ct_ref),
        (q_hbm, q_ref),
        (own_hbm, block_rows(g_ref, me)),
    ]
    loads = [pltpu.make_async_copy(src, dst, load_sem.at[i]) for i, (src, dst) in enumerate(pairs)]
    for load in loads:
        load.start()
    pl.semaphore_wait(barrier, len(peers))

    sent = []

    def push(src, block, half, station, device):
        copy = pltpu.make_async_remote_copy(
            src_ref=src,
            dst_ref=half_rows(g_ref, block, half),
            send_sem=link_send.at[station, half],
            recv_sem=link_recv.at[station, half],
            device_id=device,
            device_id_type=MESH,
        )
        copy.start()
        sent.append(copy)

    def own_half(half):
        return own_hbm.at[half * HALF : (half + 1) * HALF]

    own_to_core = pltpu.make_async_remote_copy(
        src_ref=own_hbm,
        dst_ref=block_rows(g_ref, me),
        send_sem=core_send.at[N_STATION],
        recv_sem=core_recv.at[N_STATION],
        device_id=at.sibling(),
        device_id_type=MESH,
    )
    own_to_core.start()
    sent.append(own_to_core)
    for dz, station in ((1, 1), (0, 0), (-1, 3)):
        for half in range(2):
            if dz:
                push(own_half(half), me, half, station, at.at(dz, 0))
            push(own_half(half), me, half, station + (1 if dz else 0), at.at(dz, 2 * half - 1))

    def landed(station, half):
        block = 2 * at.station_pair(station) + at.core
        pltpu.make_async_copy(own_half(half), half_rows(g_ref, block, half), link_recv.at[station, half]).wait()

    def relay(station):
        half = 0 if station < 3 else 1
        block = 2 * at.station_pair(station) + at.core
        push(half_rows(g_ref, block, half), block, half, 5 + (station + 1) % 2, at.at(1 if station < 3 else -1, 0))

    def to_core(station):
        block = 2 * at.station_pair(station) + at.core
        copy = pltpu.make_async_remote_copy(
            src_ref=block_rows(g_ref, block),
            dst_ref=block_rows(g_ref, block),
            send_sem=core_send.at[station],
            recv_sem=core_recv.at[station],
            device_id=at.sibling(),
            device_id_type=MESH,
        )
        copy.start()
        sent.append(copy)

    def from_core(station, pair):
        block = 2 * pair + 1 - at.core
        pltpu.make_async_copy(own_hbm, block_rows(g_ref, block), core_recv.at[station]).wait()

    starts, ends = request_table(lens_ref)
    table = slot_table(me, lens_ref, place_ref, starts)
    loads[0].wait()
    loads[1].wait()
    prepare_weights(wk_ref, wv_ref, wkt, wvt)
    loads[2].wait()
    loads[3].wait()
    decode_queries(dq_ref, wkt, qh, qr)
    slot_queries(table, qr, qs2)
    loads[4].wait()
    w_loads = []
    first = 0
    for c, width in enumerate(CHUNKS):
        cols = slice(first, first + width)
        w_loads.append(pltpu.make_async_copy(w_hbm.at[:, cols], w_ref.at[:, cols], w_sem.at[c]))
        w_loads[-1].start()
        first += width
    decode_resident(qr, ct_ref, fresh_ref, rlen_ref, sr, ar, lo)
    loads[5].wait()
    prepare_queries(me, q_ref, starts, ends, qs)

    for station in (1, 3):
        for half in range(2):
            landed(station, half)
        relay(station)
    for half in range(2):
        landed(0, half)
    for station in (0, 1, 3):
        to_core(station)

    step = functools.partial(
        attend_pair,
        me=me,
        g_ref=g_ref,
        starts=starts,
        ends=ends,
        wkt=wkt,
        wvt=wvt,
        qs=qs,
        kt=kt,
        vt=vt,
        best=best,
        acc=acc,
    )
    own = me // 2
    loads[6].wait()
    from_core(N_STATION, own)
    step(own, True)

    for station in (2, 4):
        for half in range(2):
            landed(station, half)
        relay(station)
        to_core(station)

    def project():
        copies = []
        first = 0
        for c, width in enumerate(CHUNKS):
            quarter = width // 4
            q0 = first // 4
            w_loads[c].wait()
            part = mm(x_ref[...], w_ref[:, first : first + width])
            for p in range(N_TP):
                rows = part[4 * p : 4 * p + 4, :]
                piece = jnp.concatenate([rows[:, k * quarter : (k + 1) * quarter] for k in range(4)], axis=0)
                send[p, :, q0 : q0 + quarter] = piece.astype(BF16)
            for d in range(1, N_TP):
                peer = (tp + d) % N_TP
                copy = pltpu.make_async_remote_copy(
                    src_ref=send.at[peer, :, q0 : q0 + quarter],
                    dst_ref=recv.at[d, :, q0 : q0 + quarter],
                    send_sem=sum_send.at[c, d],
                    recv_sem=sum_recv.at[c, d],
                    device_id=(me, peer),
                    device_id_type=MESH,
                )
                copy.start()
                copies.append((c, d, copy))
            first += width
        return copies

    def near(station):
        pair = at.station_pair(station)
        from_core(station, pair)

        @pl.when((pair < own) & (pair >= own - 5))
        def _():
            step(pair, False)

    @pl.loop(0, 5)
    def _(station):
        near(station)

    for station in (5, 6):
        for half in range(2):
            landed(station, half)
        to_core(station)
    for station in (5, 6):
        from_core(station, at.station_pair(station))

    for b in range(N_CTX):
        slot_scores(b, g_ref, qs2, ss)
    decode_slots(table, g_ref, qs2, ss, fresh_ref, lo, lo2)
    head_values(lo2, wv_ref, x_ref)
    sums = project()

    @pl.loop(5, N_STATION)
    def _(station):
        pair = at.station_pair(station)

        @pl.when((pair < own) & (pair >= own - 5))
        def _():
            step(pair, False)

    finish_prefill(acc, out_ref)
    store = pltpu.make_async_copy(out_ref, out_hbm, load_sem.at[len(pairs)])
    store.start()

    first = 0
    for c, width in enumerate(CHUNKS):
        quarter = width // 4
        q0 = first // 4
        total = send[tp, :, q0 : q0 + quarter].astype(F32)
        for c2, d, copy in sums:
            if c2 == c:
                copy.wait_recv()
                total = total + recv[d, :, q0 : q0 + quarter].astype(F32)
        for k in range(4):
            for row in range(2):
                piece = total[4 * k + 2 * row : 4 * k + 2 * row + 2, :]
                dec_ref[row, :, first + k * quarter : first + (k + 1) * quarter] = piece.astype(BF16)
        first += width
    for _, _, copy in sums:
        copy.wait_send()
    for copy in sent:
        copy.wait_send()
    store.wait()


def mega(lens, place, rlen, q, own, wk, wv, ct, dq, fresh, w):
    smem = pl.BlockSpec(memory_space=pltpu.SMEM)
    vmem = pl.BlockSpec(memory_space=pltpu.VMEM)
    far = pl.BlockSpec(memory_space=pl.ANY)
    lines = ROWS * STEPS * HEADS
    two = 2 * STEPS * HEADS
    width = w.shape[1]
    dma = pltpu.SemaphoreType.DMA
    return pl.pallas_call(
        mega_kernel,
        out_shape=(
            jax.ShapeDtypeStruct((BLOCK, HEADS * NOPE), BF16),
            jax.ShapeDtypeStruct((2, STEPS, width), BF16),
        ),
        in_specs=[smem] * 3 + [far] * 8,
        out_specs=(far, vmem),
        scratch_shapes=[
            pltpu.VMEM(q.shape, BF16),
            pltpu.VMEM((N_CTX * WIDTH, BLOCK), BF16),
            pltpu.VMEM(wk.shape, BF16),
            pltpu.VMEM(wv.shape, BF16),
            pltpu.VMEM(ct.shape, BF16),
            pltpu.VMEM(dq.shape, BF16),
            pltpu.VMEM(fresh.shape, BF16),
            pltpu.VMEM(w.shape, BF16),
            pltpu.VMEM((BLOCK, HEADS * NOPE), BF16),
            pltpu.VMEM((ROWS * STEPS, HEADS * NOPE), BF16),
            pltpu.VMEM((HEADS * NOPE, LATENT), BF16),
            pltpu.VMEM((HEADS * NOPE, LATENT), BF16),
            pltpu.VMEM((HEADS, BLOCK, 256), BF16),
            pltpu.VMEM((HEADS * NOPE, 2 * BLOCK), BF16),
            pltpu.VMEM((HEADS * NOPE, 2 * BLOCK), BF16),
            pltpu.VMEM((HEADS, BLOCK, 128), F32),
            pltpu.VMEM((HEADS, BLOCK, 256), F32),
            pltpu.VMEM((lines, 640), BF16),
            pltpu.VMEM((lines, 640), BF16),
            pltpu.VMEM((lines, BLOCK), F32),
            pltpu.VMEM((lines, LATENT), F32),
            pltpu.VMEM((lines, LATENT), BF16),
            pltpu.VMEM((two, 640), BF16),
            pltpu.VMEM((N_CTX, two, BLOCK), F32),
            pltpu.VMEM((lines, LATENT), BF16),
            pltpu.VMEM((N_TP, 16, width // 4), BF16),
            pltpu.VMEM((N_TP, 16, width // 4), BF16),
            dma((8,)),
            dma((len(CHUNKS),)),
            dma((N_STATION, 2)),
            dma((N_STATION, 2)),
            dma((N_STATION + 1,)),
            dma((N_STATION + 1,)),
            dma((len(CHUNKS), N_TP)),
            dma((len(CHUNKS), N_TP)),
        ],
        compiler_params=pltpu.CompilerParams(collective_id=0, has_side_effects=True, vmem_limit_bytes=60 * MIB),
        name="latent_attention",
    )(lens, place, rlen, q, own, wk, wv, ct, dq, fresh, w)


def on_device(
    prefill_query,
    span_latent,
    prompt_lengths,
    key_weight,
    value_weight,
    placement,
    resident_cache,
    resident_lengths,
    decode_query,
    decode_latent,
    out_weight,
):
    cache_t = jnp.swapaxes(resident_cache, 1, 2).reshape(ROWS * WIDTH, BLOCK)
    return mega(
        prompt_lengths,
        placement,
        resident_lengths,
        prefill_query,
        span_latent.T,
        key_weight,
        value_weight,
        cache_t,
        decode_query.reshape(ROWS * STEPS, -1),
        decode_latent.reshape(ROWS * STEPS, -1),
        out_weight,
    )


def solution(mesh):
    placed = (
        P("ctx", "tp"),
        P("ctx", None),
        P(),
        P(None, "tp"),
        P(None, "tp"),
        P(),
        P("ctx", None, None),
        P("ctx"),
        P("ctx", None, "tp"),
        P("ctx", None, None),
        P("tp", None),
    )
    return jax.shard_map(
        on_device,
        mesh=mesh,
        in_specs=placed,
        out_specs=(P("ctx", "tp"), P(("ctx", "tp"), None, None)),
        check_vma=False,
    )
```

```python
import functools
import math

import jax
import jax.numpy as jnp
from jax import lax
from jax.experimental import pallas as pl
from jax.experimental.pallas import tpu as pltpu
from jax.sharding import PartitionSpec as P

MESH = pl.DeviceIdType.MESH
NOPE = 128
ROPE = 64
LATENT = 512
WIDTH = LATENT + ROPE
BLOCK = 256
N_CTX = 16
N_TP = 8
HEADS = 8
ROWS = 16
STEPS = 2
NREQ = 8
BIG = 1e30
FACTOR = math.log2(math.e) / math.sqrt(NOPE + ROPE)
F32 = jnp.float32
BF16 = jnp.bfloat16
MIB = 1 << 20
HALF = WIDTH // 2
QUARTER = WIDTH // 4
N_Z = 4
N_STATION = 7
FAR = (5, 6, 4)
CHUNKS = (2048, 2048, 2048, 1024)


def mm(left, right):
    return lax.dot_general(left, right, (((1,), (0,)), ((), ())), preferred_element_type=F32)


def mm_nt(left, right):
    return lax.dot_general(left, right, (((1,), (1,)), ((), ())), preferred_element_type=F32)


def iota(shape, dim):
    return lax.broadcasted_iota(jnp.int32, shape, dim)


def request_table(lens_ref):
    starts, ends, total = [], [], jnp.int32(0)
    for j in range(NREQ):
        starts.append(total)
        total = total + lens_ref[j]
        ends.append(total)
    return starts, ends


def spread(index, values, other):
    out = jnp.full(index.shape, other, jnp.int32)
    for j, value in enumerate(values):
        out = jnp.where(index == j, value, out)
    return out


def prepare_weights(wk_ref, wv_ref, wkt, wvt):
    wkt[...] = wk_ref[...].T
    wvt[...] = wv_ref[...].T


def prepare_queries(me, q_ref, starts, ends, qs):
    lane = iota((BLOCK, 256), 1)
    pos = me * BLOCK + iota((BLOCK, 256), 0)
    for odd in range(2):
        slot = lane if odd else lane - 192
        first = spread(slot, starts, 1 << 30)
        last = spread(slot, ends, -1)
        hot = ((pos >= first) & (pos < last)).astype(F32)
        spare = lane < 64 if odd else lane >= 192
        for pair in range(HEADS // 2):
            base = pair * 384 + odd * 128
            window = q_ref[:, base : base + 256].astype(F32)
            qs[2 * pair + odd] = jnp.where(spare, hot, window).astype(BF16)


def latent_rows(g_ref, block, first, count):
    return g_ref[pl.ds(pl.multiple_of(block * WIDTH + first, 64), count), :]


def attend_pair(pair, causal, me, g_ref, starts, ends, wkt, wvt, qs, kt, vt, best, acc):
    ropes = []
    for half in range(2):
        lat = latent_rows(g_ref, 2 * pair + half, 0, LATENT)
        cols = slice(half * BLOCK, (half + 1) * BLOCK)
        kt[:, cols] = mm(wkt[...], lat).astype(BF16)
        vt[:, cols] = mm(wvt[...], lat).astype(BF16)
        ropes.append(latent_rows(g_ref, 2 * pair + half, LATENT, ROPE))
    rope = jnp.concatenate(ropes, axis=1)
    keys = 2 * BLOCK
    slot = iota((ROPE, keys), 0)
    key_pos = pair * keys + iota((ROPE, keys), 1)
    outside = (slot < NREQ) & ((key_pos < spread(slot, starts, 0)) | (key_pos >= spread(slot, ends, 0)))
    aug = jnp.where(outside, -BIG, 0.0).astype(BF16)
    ones = jnp.ones((NOPE, keys), BF16)
    for h in range(HEADS):
        head = slice(h * NOPE, (h + 1) * NOPE)
        parts = [aug, kt[head, :], rope] if h % 2 else [kt[head, :], rope, aug]
        s = mm(qs[h], jnp.concatenate(parts, axis=0))
        if causal:
            ahead = pair * keys + iota((BLOCK, keys), 1) > me * BLOCK + iota((BLOCK, keys), 0)
            s = jnp.where(ahead, -BIG, s)
        block_best = jnp.max(s, axis=1, keepdims=True) * FACTOR
        values = jnp.concatenate([vt[head, :], ones], axis=0)
        if causal:
            new_best = jnp.broadcast_to(block_best, (BLOCK, 128))
        else:
            new_best = jnp.maximum(best[h], block_best)
        p = jnp.exp2(s * FACTOR - jnp.concatenate([new_best] * 4, axis=1)).astype(BF16)
        gained = mm_nt(p, values)
        if causal:
            acc[h] = gained
        else:
            keep = jnp.exp2(best[h] - new_best)
            acc[h] = acc[h] * jnp.concatenate([keep] * 2, axis=1) + gained
        best[h] = new_best


def finish_prefill(acc, out_ref):
    for h in range(HEADS):
        out_ref[:, h * NOPE : (h + 1) * NOPE] = (acc[h][:, :NOPE] / acc[h][:, NOPE:]).astype(BF16)


def to_row_major(index):
    return (index % HEADS) * (ROWS * STEPS) + index // HEADS


def hot_matrix(condition):
    return condition.astype(F32).astype(BF16)


def pack_rows(rows_ref, wide_ref, flat_ref):
    for r in range(ROWS):
        wide_ref[r * STEPS : (r + 1) * STEPS, :] = rows_ref[r].astype(F32)
    flat_ref[...] = wide_ref[...].astype(BF16)


def decode_queries(dq_ref, wkt, qh, qr):
    rows = ROWS * STEPS
    eye = hot_matrix(iota((ROPE, 128), 0) == iota((ROPE, 128), 1))
    side = jnp.zeros((ROPE, 128), BF16)
    below = jnp.zeros((ROPE, LATENT), BF16)
    for h in range(HEADS):
        base = (h // 2) * 384 + (h % 2) * 128
        window = dq_ref[:, base : base + 256]
        weight = wkt[h * NOPE : (h + 1) * NOPE, :]
        lat = [below, weight, below] if h % 2 else [weight, below, below]
        rot = [side, side, side, eye] if h % 2 else [side, side, eye, side]
        qh[h * rows : (h + 1) * rows, :LATENT] = mm(window, jnp.concatenate(lat, axis=0)).astype(BF16)
        qh[h * rows : (h + 1) * rows, LATENT:] = mm(window, jnp.concatenate(rot, axis=0)).astype(BF16)
    count = rows * HEADS
    order = hot_matrix(to_row_major(iota((count, count), 0)) == iota((count, count), 1))
    qr[...] = mm(order, qh[...]).astype(BF16)


def scores_of(queries, lat, rope):
    return mm(queries[:, :LATENT], lat) + mm(queries[:, LATENT:WIDTH], rope)


def decode_resident(qr, ct_ref, fresh_ref, rlen_ref, sr, ar, lo):
    per = STEPS * HEADS
    for r in range(ROWS):
        rows = slice(r * per, (r + 1) * per)
        sr[rows, :] = scores_of(
            qr[rows, :], ct_ref[r * WIDTH : r * WIDTH + LATENT, :], ct_ref[r * WIDTH + LATENT : (r + 1) * WIDTH, :]
        )
    count = ROWS * per
    row_of = iota((count, BLOCK), 0) // per
    filled = spread(row_of, [rlen_ref[r] for r in range(ROWS)], 0)
    s = jnp.where(iota((count, BLOCK), 1) < filled, sr[...], -BIG) * FACTOR
    fs = mm_nt(qr[:, :LATENT], fresh_ref[:, :LATENT]) + mm_nt(qr[:, LATENT:WIDTH], fresh_ref[:, LATENT:])
    place, col = iota(fs.shape, 0), iota(fs.shape, 1)
    open_ = (place // per == col // STEPS) & (col % STEPS <= (place // HEADS) % STEPS)
    fs = jnp.where(open_, fs, -BIG) * FACTOR
    best = jnp.maximum(jnp.max(s, axis=1, keepdims=True), jnp.max(fs, axis=1, keepdims=True))
    w = jnp.exp2(s - best)
    fw = jnp.exp2(fs - best)
    total = jnp.sum(w, axis=1, keepdims=True) + jnp.sum(fw, axis=1, keepdims=True)
    sr[...] = w
    for r in range(ROWS):
        rows = slice(r * per, (r + 1) * per)
        ar[rows, :] = mm_nt(sr[rows, :].astype(BF16), ct_ref[r * WIDTH : r * WIDTH + LATENT, :])
    lo[...] = ((ar[...] + mm(fw.astype(BF16), fresh_ref[:, :LATENT])) / total).astype(BF16)


def slot_table(me, lens_ref, place_ref, starts):
    rank = jnp.int32(0)
    row = [jnp.int32(-1)] * 2
    first = [jnp.int32(0)] * 2
    length = [jnp.int32(0)] * 2
    for j in range(NREQ):
        there = place_ref[j] // ROWS == me
        for k in range(2):
            hit = there & (rank == k)
            row[k] = jnp.where(hit, place_ref[j] % ROWS, row[k])
            first[k] = jnp.where(hit, starts[j], first[k])
            length[k] = jnp.where(hit, lens_ref[j], length[k])
        rank = rank + there.astype(jnp.int32)
    return row, first, length


def slot_queries(table, qr, qs2):
    per = STEPS * HEADS
    shape = (2 * per, ROWS * per)
    place = iota(shape, 0)
    row = spread(place // per, table[0], -1)
    pick = hot_matrix((row >= 0) & (iota(shape, 1) == row * per + place % per))
    qs2[...] = mm(pick, qr[...]).astype(BF16)


def slot_scores(block, g_ref, qs2, ss):
    ss[block] = scores_of(qs2[...], latent_rows(g_ref, block, 0, LATENT), latent_rows(g_ref, block, LATENT, ROPE))


def decode_slots(table, g_ref, qs2, ss, fresh_ref, lo_ref, out_rows):
    per = STEPS * HEADS
    row, first, length = table
    lines = 2 * per
    slot = iota((lines, BLOCK), 0) // per
    low = spread(slot, first, 0)
    high = low + spread(slot, length, 0)
    fs = mm_nt(qs2[:, :LATENT], fresh_ref[:, :LATENT]) + mm_nt(qs2[:, LATENT:WIDTH], fresh_ref[:, LATENT:])
    place, col = iota(fs.shape, 0), iota(fs.shape, 1)
    open_ = (spread(place // per, row, -1) == col // STEPS) & (col % STEPS <= (place // HEADS) % STEPS)
    fs = jnp.where(open_, fs, -BIG) * FACTOR
    best = jnp.max(fs, axis=1, keepdims=True)
    peak = jnp.full((lines, BLOCK), -BIG, F32)
    for b in range(N_CTX):
        pos = b * BLOCK + iota((lines, BLOCK), 1)
        s = jnp.where((pos >= low) & (pos < high), ss[b] * FACTOR, -BIG)
        ss[b] = s
        peak = jnp.maximum(peak, s)
    best = jnp.maximum(best, jnp.max(peak, axis=1, keepdims=True))
    fw = jnp.exp2(fs - best)
    mass = jnp.zeros((lines, BLOCK), F32)
    total = mm(fw.astype(BF16), fresh_ref[:, :LATENT])
    for b in range(N_CTX):
        w = jnp.exp2(ss[b] - best)
        mass = mass + w
        total = total + mm_nt(w.astype(BF16), latent_rows(g_ref, b, 0, LATENT))
    weight = jnp.sum(mass, axis=1, keepdims=True) + jnp.sum(fw, axis=1, keepdims=True)
    slot_out = (total / weight).astype(BF16)
    shape = (ROWS * per, lines)
    back = iota(shape, 1)
    back_row = spread(back // per, row, -1)
    route = hot_matrix((back_row >= 0) & (iota(shape, 0) == back_row * per + back % per))
    spot = iota((ROWS * per, LATENT), 0) // per
    replaced = (spot == row[0]) | (spot == row[1])
    out_rows[...] = jnp.where(replaced, mm(route, slot_out), lo_ref[...].astype(F32)).astype(BF16)


def head_values(rows_ref, wv_ref, x_ref):
    rows = ROWS * STEPS
    count = rows * HEADS
    order = hot_matrix(iota((count, count), 0) == to_row_major(iota((count, count), 1)))
    lat = mm(order, rows_ref[...]).astype(BF16)
    for h in range(HEADS):
        head = slice(h * NOPE, (h + 1) * NOPE)
        x_ref[:, head] = mm(lat[h * rows : (h + 1) * rows, :], wv_ref[:, head]).astype(BF16)


def z_step(v):
    zz = v // 2
    return (zz * 3) % 5 - (zz // 3) * 2


class Place:
    def __init__(self):
        self.ctx = lax.axis_index("ctx")
        self.tp = lax.axis_index("tp")
        self.core = self.ctx % 2
        self.z = self.ctx // 4
        self.x_lo = (self.ctx // 2) % 2
        self.x = (self.tp // 4) * 2 + self.x_lo
        self.y = self.tp % 4

    def at(self, dz, dx, dy=0):
        z = (self.z + dz + N_Z) % N_Z
        x = (self.x + dx + 4) % 4
        y = (self.y + dy + 4) % 4
        return ((z * 2 + x % 2) * 2 + self.core, (x // 2) * 4 + y)

    def sibling(self):
        return (self.ctx + 1 - 2 * self.core, self.tp)

    def station_pair(self, station):
        v = station + 1
        return ((self.z + z_step(v) + N_Z) % N_Z) * 2 + (self.x_lo + v) % 2


def half_rows(g_ref, block, half):
    return g_ref.at[pl.ds(pl.multiple_of(block * WIDTH + half * HALF, 32), HALF)]


def quarter_rows(g_ref, block, quarter):
    return g_ref.at[pl.ds(pl.multiple_of(block * WIDTH + quarter * QUARTER, 16), QUARTER)]


def block_rows(g_ref, block):
    return g_ref.at[pl.ds(pl.multiple_of(block * WIDTH, 64), WIDTH)]


def mega_kernel(
    lens_ref,
    place_ref,
    rlen_ref,
    q_hbm,
    own_hbm,
    wk_hbm,
    wv_hbm,
    ct_hbm,
    dq_hbm,
    fresh_hbm,
    w_hbm,
    out_hbm,
    dec_ref,
    q_ref,
    g_ref,
    wk_ref,
    wv_ref,
    ct_ref,
    dq_ref,
    fresh_ref,
    dq3,
    fresh3,
    dq32,
    fresh32,
    w_ref,
    out_ref,
    x_ref,
    wkt,
    wvt,
    qs,
    kt,
    vt,
    best,
    acc,
    qh,
    qr,
    sr,
    ar,
    lo,
    qs2,
    ss,
    lo2,
    send,
    recv,
    load_sem,
    w_sem,
    link_send,
    link_recv,
    far_send,
    far_recv,
    core_send,
    core_recv,
    sum_send,
    sum_recv,
):
    at = Place()
    me, tp = at.ctx, at.tp
    barrier = pltpu.get_barrier_semaphore()
    peers = [at.sibling()]
    aside = 1 - 2 * (at.y % 2)
    peers += [at.at(1, 0), at.at(-1, 0), at.at(2, 0), at.at(0, -1), at.at(0, 1)]
    peers += [at.at(2, 1), at.at(2, -1), at.at(1, 1), at.at(1, -1), at.at(-1, 1), at.at(-1, -1)]
    peers += [(me, (tp + d) % N_TP) for d in range(1, N_TP)]
    for peer in peers:
        pl.semaphore_signal(barrier, inc=1, device_id=peer, device_id_type=MESH)

    pairs = [
        (wk_hbm, wk_ref),
        (wv_hbm, wv_ref),
        (dq_hbm, dq3),
        (fresh_hbm, fresh3),
        (ct_hbm, ct_ref),
        (q_hbm, q_ref),
        (own_hbm, block_rows(g_ref, me)),
    ]
    loads = [pltpu.make_async_copy(src, dst, load_sem.at[i]) for i, (src, dst) in enumerate(pairs)]
    for load in loads:
        load.start()
    pl.semaphore_wait(barrier, len(peers))

    sent = []

    def push(src, block, half, station, device):
        copy = pltpu.make_async_remote_copy(
            src_ref=src,
            dst_ref=half_rows(g_ref, block, half),
            send_sem=link_send.at[station, half],
            recv_sem=link_recv.at[station, half],
            device_id=device,
            device_id_type=MESH,
        )
        copy.start()
        sent.append(copy)

    def own_half(half):
        return own_hbm.at[half * HALF : (half + 1) * HALF]

    def push_quarter(src, block, quarter, which, step, device):
        copy = pltpu.make_async_remote_copy(
            src_ref=src,
            dst_ref=quarter_rows(g_ref, block, quarter),
            send_sem=far_send.at[which, step],
            recv_sem=far_recv.at[which, step],
            device_id=device,
            device_id_type=MESH,
        )
        copy.start()
        sent.append(copy)

    own_quarter = own_hbm.at[pl.ds(pl.multiple_of(at.y * QUARTER, 16), QUARTER)]
    for which, device in enumerate((at.at(2, 0), at.at(2, aside), at.at(-1, aside))):
        push_quarter(own_quarter, me, at.y, which, 0, device)
    for half in range(2):
        push(own_half(half), me, half, 0, at.at(0, 2 * half - 1))
    own_to_core = pltpu.make_async_remote_copy(
        src_ref=own_hbm,
        dst_ref=block_rows(g_ref, me),
        send_sem=core_send.at[N_STATION],
        recv_sem=core_recv.at[N_STATION],
        device_id=at.sibling(),
        device_id_type=MESH,
    )
    own_to_core.start()
    sent.append(own_to_core)

    def landed(station, half):
        block = 2 * at.station_pair(station) + at.core
        pltpu.make_async_copy(own_half(half), half_rows(g_ref, block, half), link_recv.at[station, half]).wait()

    def share_x(half):
        landed(1, half)
        block = 2 * at.station_pair(1) + at.core
        push(half_rows(g_ref, block, half), block, half, 2, at.at(0, 2 * half - 1))

    def landed_quarter(which, step):
        block = 2 * at.station_pair(FAR[which]) + at.core
        quarter = (at.y - step + 4) % 4
        source = own_hbm.at[0:QUARTER]
        pltpu.make_async_copy(source, quarter_rows(g_ref, block, quarter), far_recv.at[which, step]).wait()

    def share_far(which):
        landed_quarter(which, 0)
        block = 2 * at.station_pair(FAR[which]) + at.core
        mine = quarter_rows(g_ref, block, at.y)
        for step in (1, 3, 2):
            push_quarter(mine, block, at.y, which, step, at.at(0, 0, step))

    def to_core(station):
        block = 2 * at.station_pair(station) + at.core
        copy = pltpu.make_async_remote_copy(
            src_ref=block_rows(g_ref, block),
            dst_ref=block_rows(g_ref, block),
            send_sem=core_send.at[station],
            recv_sem=core_recv.at[station],
            device_id=at.sibling(),
            device_id_type=MESH,
        )
        copy.start()
        sent.append(copy)

    def from_core(station, pair):
        block = 2 * pair + 1 - at.core
        pltpu.make_async_copy(own_hbm, block_rows(g_ref, block), core_recv.at[station]).wait()

    starts, ends = request_table(lens_ref)
    table = slot_table(me, lens_ref, place_ref, starts)
    loads[0].wait()
    loads[1].wait()
    prepare_weights(wk_ref, wv_ref, wkt, wvt)
    for half in range(2):
        push(own_half(half), me, half, 1, at.at(1, 0))
        push(own_half(half), me, half, 3, at.at(-1, 0))
    loads[2].wait()
    loads[3].wait()
    pack_rows(dq3, dq32, dq_ref)
    pack_rows(fresh3, fresh32, fresh_ref)
    decode_queries(dq_ref, wkt, qh, qr)
    slot_queries(table, qr, qs2)
    for which in range(3):
        share_far(which)
    loads[4].wait()
    w_loads = []
    first = 0
    for c, width in enumerate(CHUNKS):
        cols = slice(first, first + width)
        w_loads.append(pltpu.make_async_copy(w_hbm.at[:, cols], w_ref.at[:, cols], w_sem.at[c]))
        w_loads[-1].start()
        first += width
    decode_resident(qr, ct_ref, fresh_ref, rlen_ref, sr, ar, lo)
    share_x(0)
    share_x(1)
    loads[5].wait()
    prepare_queries(me, q_ref, starts, ends, qs)

    for half in range(2):
        landed(0, half)
    for station in (0, 1):
        to_core(station)

    step = functools.partial(
        attend_pair,
        me=me,
        g_ref=g_ref,
        starts=starts,
        ends=ends,
        wkt=wkt,
        wvt=wvt,
        qs=qs,
        kt=kt,
        vt=vt,
        best=best,
        acc=acc,
    )
    own = me // 2
    loads[6].wait()
    from_core(N_STATION, own)
    step(own, True)

    for station in (2, 3):
        for half in range(2):
            landed(station, half)
        to_core(station)

    def project():
        copies = []
        first = 0
        for c, width in enumerate(CHUNKS):
            quarter = width // 4
            q0 = first // 4
            w_loads[c].wait()
            part = mm(x_ref[...], w_ref[:, first : first + width])
            for p in range(N_TP):
                rows = part[4 * p : 4 * p + 4, :]
                piece = jnp.concatenate([rows[:, k * quarter : (k + 1) * quarter] for k in range(4)], axis=0)
                send[p, :, q0 : q0 + quarter] = piece.astype(BF16)
            for d in range(1, N_TP):
                peer = (tp + d) % N_TP
                copy = pltpu.make_async_remote_copy(
                    src_ref=send.at[peer, :, q0 : q0 + quarter],
                    dst_ref=recv.at[d, :, q0 : q0 + quarter],
                    send_sem=sum_send.at[c, d],
                    recv_sem=sum_recv.at[c, d],
                    device_id=(me, peer),
                    device_id_type=MESH,
                )
                copy.start()
                copies.append((c, d, copy))
            first += width
        return copies

    def near(station):
        pair = at.station_pair(station)
        from_core(station, pair)

        @pl.when((pair < own) & (pair >= own - 5))
        def _():
            step(pair, False)

    @pl.loop(0, 3)
    def _(station):
        near(station)

    for which in range(3):
        for step_y in range(1, 4):
            landed_quarter(which, step_y)
        to_core(FAR[which])
    for station in (3, 4, 5, 6):
        from_core(station, at.station_pair(station))

    for b in range(N_CTX):
        slot_scores(b, g_ref, qs2, ss)
    decode_slots(table, g_ref, qs2, ss, fresh_ref, lo, lo2)
    head_values(lo2, wv_ref, x_ref)
    sums = project()

    @pl.loop(4, N_STATION)
    def _(station):
        pair = at.station_pair(station)

        @pl.when((pair < own) & (pair >= own - 5))
        def _():
            step(pair, False)

    finish_prefill(acc, out_ref)
    store = pltpu.make_async_copy(out_ref, out_hbm, load_sem.at[len(pairs)])
    store.start()

    first = 0
    for c, width in enumerate(CHUNKS):
        quarter = width // 4
        q0 = first // 4
        total = send[tp, :, q0 : q0 + quarter].astype(F32)
        for c2, d, copy in sums:
            if c2 == c:
                copy.wait_recv()
                total = total + recv[d, :, q0 : q0 + quarter].astype(F32)
        for k in range(4):
            for row in range(2):
                piece = total[4 * k + 2 * row : 4 * k + 2 * row + 2, :]
                dec_ref[row, :, first + k * quarter : first + (k + 1) * quarter] = piece.astype(BF16)
        first += width
    for _, _, copy in sums:
        copy.wait_send()
    for copy in sent:
        copy.wait_send()
    store.wait()


def mega(lens, place, rlen, q, own, wk, wv, ct, dq, fresh, w):
    smem = pl.BlockSpec(memory_space=pltpu.SMEM)
    vmem = pl.BlockSpec(memory_space=pltpu.VMEM)
    far = pl.BlockSpec(memory_space=pl.ANY)
    lines = ROWS * STEPS * HEADS
    two = 2 * STEPS * HEADS
    width = w.shape[1]
    dma = pltpu.SemaphoreType.DMA
    return pl.pallas_call(
        mega_kernel,
        out_shape=(
            jax.ShapeDtypeStruct((BLOCK, HEADS * NOPE), BF16),
            jax.ShapeDtypeStruct((2, STEPS, width), BF16),
        ),
        in_specs=[smem] * 3 + [far] * 8,
        out_specs=(far, vmem),
        scratch_shapes=[
            pltpu.VMEM(q.shape, BF16),
            pltpu.VMEM((N_CTX * WIDTH, BLOCK), BF16),
            pltpu.VMEM(wk.shape, BF16),
            pltpu.VMEM(wv.shape, BF16),
            pltpu.VMEM(ct.shape, BF16),
            pltpu.VMEM((ROWS * STEPS, dq.shape[2]), BF16),
            pltpu.VMEM((ROWS * STEPS, WIDTH), BF16),
            pltpu.VMEM(dq.shape, BF16),
            pltpu.VMEM(fresh.shape, BF16),
            pltpu.VMEM((ROWS * STEPS, dq.shape[2]), F32),
            pltpu.VMEM((ROWS * STEPS, WIDTH), F32),
            pltpu.VMEM(w.shape, BF16),
            pltpu.VMEM((BLOCK, HEADS * NOPE), BF16),
            pltpu.VMEM((ROWS * STEPS, HEADS * NOPE), BF16),
            pltpu.VMEM((HEADS * NOPE, LATENT), BF16),
            pltpu.VMEM((HEADS * NOPE, LATENT), BF16),
            pltpu.VMEM((HEADS, BLOCK, 256), BF16),
            pltpu.VMEM((HEADS * NOPE, 2 * BLOCK), BF16),
            pltpu.VMEM((HEADS * NOPE, 2 * BLOCK), BF16),
            pltpu.VMEM((HEADS, BLOCK, 128), F32),
            pltpu.VMEM((HEADS, BLOCK, 256), F32),
            pltpu.VMEM((lines, 640), BF16),
            pltpu.VMEM((lines, 640), BF16),
            pltpu.VMEM((lines, BLOCK), F32),
            pltpu.VMEM((lines, LATENT), F32),
            pltpu.VMEM((lines, LATENT), BF16),
            pltpu.VMEM((two, 640), BF16),
            pltpu.VMEM((N_CTX, two, BLOCK), F32),
            pltpu.VMEM((lines, LATENT), BF16),
            pltpu.VMEM((N_TP, 16, width // 4), BF16),
            pltpu.VMEM((N_TP, 16, width // 4), BF16),
            dma((8,)),
            dma((len(CHUNKS),)),
            dma((4, 2)),
            dma((4, 2)),
            dma((3, 4)),
            dma((3, 4)),
            dma((N_STATION + 1,)),
            dma((N_STATION + 1,)),
            dma((len(CHUNKS), N_TP)),
            dma((len(CHUNKS), N_TP)),
        ],
        compiler_params=pltpu.CompilerParams(collective_id=0, has_side_effects=True, vmem_limit_bytes=60 * MIB),
        name="latent_attention",
    )(lens, place, rlen, q, own, wk, wv, ct, dq, fresh, w)


def on_device(
    prefill_query,
    span_latent,
    prompt_lengths,
    key_weight,
    value_weight,
    placement,
    resident_cache,
    resident_lengths,
    decode_query,
    decode_latent,
    out_weight,
):
    cache_t = jnp.swapaxes(resident_cache, 1, 2).reshape(ROWS * WIDTH, BLOCK)
    return mega(
        prompt_lengths,
        placement,
        resident_lengths,
        prefill_query,
        span_latent.T,
        key_weight,
        value_weight,
        cache_t,
        decode_query,
        decode_latent,
        out_weight,
    )


def solution(mesh):
    placed = (
        P("ctx", "tp"),
        P("ctx", None),
        P(),
        P(None, "tp"),
        P(None, "tp"),
        P(),
        P("ctx", None, None),
        P("ctx"),
        P("ctx", None, "tp"),
        P("ctx", None, None),
        P("tp", None),
    )
    return jax.shard_map(
        on_device,
        mesh=mesh,
        in_specs=placed,
        out_specs=(P("ctx", "tp"), P(("ctx", "tp"), None, None)),
        check_vma=False,
    )
```

```python
import functools
import math

import jax
import jax.numpy as jnp
from jax import lax
from jax.experimental import pallas as pl
from jax.experimental.pallas import tpu as pltpu
from jax.sharding import PartitionSpec as P

MESH = pl.DeviceIdType.MESH
NOPE = 128
ROPE = 64
LATENT = 512
WIDTH = LATENT + ROPE
BLOCK = 256
N_CTX = 16
N_TP = 8
HEADS = 8
ROWS = 16
STEPS = 2
NREQ = 8
BIG = 1e30
FACTOR = math.log2(math.e) / math.sqrt(NOPE + ROPE)
F32 = jnp.float32
BF16 = jnp.bfloat16
MIB = 1 << 20
HALF = WIDTH // 2
QUARTER = WIDTH // 4
N_Z = 4
N_STATION = 7
FAR = (5, 6, 4)
CHUNKS = (2048, 2048, 2048, 1024)


def mm(left, right):
    return lax.dot_general(left, right, (((1,), (0,)), ((), ())), preferred_element_type=F32)


def mm_nt(left, right):
    return lax.dot_general(left, right, (((1,), (1,)), ((), ())), preferred_element_type=F32)


def iota(shape, dim):
    return lax.broadcasted_iota(jnp.int32, shape, dim)


def request_table(lens_ref):
    starts, ends, total = [], [], jnp.int32(0)
    for j in range(NREQ):
        starts.append(total)
        total = total + lens_ref[j]
        ends.append(total)
    return starts, ends


def spread(index, values, other):
    out = jnp.full(index.shape, other, jnp.int32)
    for j, value in enumerate(values):
        out = jnp.where(index == j, value, out)
    return out


def prepare_weights(wk_ref, wv_ref, wkt, wvt):
    wkt[...] = wk_ref[...].T
    wvt[...] = wv_ref[...].T


def prepare_queries(me, q_ref, starts, ends, qs):
    lane = iota((BLOCK, 256), 1)
    pos = me * BLOCK + iota((BLOCK, 256), 0)
    for odd in range(2):
        slot = lane if odd else lane - 192
        first = spread(slot, starts, 1 << 30)
        last = spread(slot, ends, -1)
        hot = ((pos >= first) & (pos < last)).astype(F32)
        spare = lane < 64 if odd else lane >= 192
        for pair in range(HEADS // 2):
            base = pair * 384 + odd * 128
            window = q_ref[:, base : base + 256].astype(F32)
            qs[2 * pair + odd] = jnp.where(spare, hot, window).astype(BF16)


def latent_rows(g_ref, block, first, count):
    return g_ref[pl.ds(pl.multiple_of(block * WIDTH + first, 64), count), :]


def attend_pair(pair, causal, me, g_ref, starts, ends, wkt, wvt, qs, kt, vt, best, acc):
    ropes = []
    for half in range(2):
        lat = latent_rows(g_ref, 2 * pair + half, 0, LATENT)
        cols = slice(half * BLOCK, (half + 1) * BLOCK)
        kt[:, cols] = mm(wkt[...], lat).astype(BF16)
        vt[:, cols] = mm(wvt[...], lat).astype(BF16)
        ropes.append(latent_rows(g_ref, 2 * pair + half, LATENT, ROPE))
    rope = jnp.concatenate(ropes, axis=1)
    keys = 2 * BLOCK
    slot = iota((ROPE, keys), 0)
    key_pos = pair * keys + iota((ROPE, keys), 1)
    outside = (slot < NREQ) & ((key_pos < spread(slot, starts, 0)) | (key_pos >= spread(slot, ends, 0)))
    aug = jnp.where(outside, -BIG, 0.0).astype(BF16)
    ones = jnp.ones((NOPE, keys), BF16)
    for h in range(HEADS):
        head = slice(h * NOPE, (h + 1) * NOPE)
        parts = [aug, kt[head, :], rope] if h % 2 else [kt[head, :], rope, aug]
        s = mm(qs[h], jnp.concatenate(parts, axis=0))
        if causal:
            ahead = pair * keys + iota((BLOCK, keys), 1) > me * BLOCK + iota((BLOCK, keys), 0)
            s = jnp.where(ahead, -BIG, s)
        block_best = jnp.max(s, axis=1, keepdims=True) * FACTOR
        values = jnp.concatenate([vt[head, :], ones], axis=0)
        if causal:
            new_best = jnp.broadcast_to(block_best, (BLOCK, 128))
        else:
            new_best = jnp.maximum(best[h], block_best)
        p = jnp.exp2(s * FACTOR - jnp.concatenate([new_best] * 4, axis=1)).astype(BF16)
        gained = mm_nt(p, values)
        if causal:
            acc[h] = gained
        else:
            keep = jnp.exp2(best[h] - new_best)
            acc[h] = acc[h] * jnp.concatenate([keep] * 2, axis=1) + gained
        best[h] = new_best


def finish_prefill(acc, out_ref):
    for h in range(HEADS):
        out_ref[:, h * NOPE : (h + 1) * NOPE] = (acc[h][:, :NOPE] / acc[h][:, NOPE:]).astype(BF16)


def to_row_major(index):
    return (index % HEADS) * (ROWS * STEPS) + index // HEADS


def hot_matrix(condition):
    return condition.astype(F32).astype(BF16)


def pack_rows(rows_ref, wide_ref, flat_ref):
    for r in range(ROWS):
        wide_ref[r * STEPS : (r + 1) * STEPS, :] = rows_ref[r].astype(F32)
    flat_ref[...] = wide_ref[...].astype(BF16)


def absorb_head(window, h, wkt, qh, rows):
    eye = hot_matrix(iota((ROPE, 128), 0) == iota((ROPE, 128), 1))
    side = jnp.zeros((ROPE, 128), BF16)
    below = jnp.zeros((ROPE, LATENT), BF16)
    weight = wkt[h * NOPE : (h + 1) * NOPE, :]
    lat = [below, weight, below] if h % 2 else [weight, below, below]
    rot = [side, side, side, eye] if h % 2 else [side, side, eye, side]
    qh[h * rows : (h + 1) * rows, :LATENT] = mm(window, jnp.concatenate(lat, axis=0)).astype(BF16)
    qh[h * rows : (h + 1) * rows, LATENT:] = mm(window, jnp.concatenate(rot, axis=0)).astype(BF16)


def decode_queries(dq_ref, wkt, qh, qr):
    rows = ROWS * STEPS
    for h in range(HEADS):
        base = (h // 2) * 384 + (h % 2) * 128
        absorb_head(dq_ref[:, base : base + 256], h, wkt, qh, rows)
    count = rows * HEADS
    order = hot_matrix(to_row_major(iota((count, count), 0)) == iota((count, count), 1))
    qr[...] = mm(order, qh[...]).astype(BF16)


def scores_of(queries, lat, rope):
    return mm(queries[:, :LATENT], lat) + mm(queries[:, LATENT:WIDTH], rope)


def decode_resident(qr, ct_ref, fresh_ref, rlen_ref, sr, ar, lo):
    per = STEPS * HEADS
    for r in range(ROWS):
        rows = slice(r * per, (r + 1) * per)
        sr[rows, :] = scores_of(
            qr[rows, :], ct_ref[r * WIDTH : r * WIDTH + LATENT, :], ct_ref[r * WIDTH + LATENT : (r + 1) * WIDTH, :]
        )
    count = ROWS * per
    row_of = iota((count, BLOCK), 0) // per
    filled = spread(row_of, [rlen_ref[r] for r in range(ROWS)], 0)
    s = jnp.where(iota((count, BLOCK), 1) < filled, sr[...], -BIG) * FACTOR
    fs = mm_nt(qr[:, :LATENT], fresh_ref[:, :LATENT]) + mm_nt(qr[:, LATENT:WIDTH], fresh_ref[:, LATENT:])
    place, col = iota(fs.shape, 0), iota(fs.shape, 1)
    open_ = (place // per == col // STEPS) & (col % STEPS <= (place // HEADS) % STEPS)
    fs = jnp.where(open_, fs, -BIG) * FACTOR
    best = jnp.maximum(jnp.max(s, axis=1, keepdims=True), jnp.max(fs, axis=1, keepdims=True))
    w = jnp.exp2(s - best)
    fw = jnp.exp2(fs - best)
    total = jnp.sum(w, axis=1, keepdims=True) + jnp.sum(fw, axis=1, keepdims=True)
    sr[...] = w
    for r in range(ROWS):
        rows = slice(r * per, (r + 1) * per)
        ar[rows, :] = mm_nt(sr[rows, :].astype(BF16), ct_ref[r * WIDTH : r * WIDTH + LATENT, :])
    lo[...] = ((ar[...] + mm(fw.astype(BF16), fresh_ref[:, :LATENT])) / total).astype(BF16)


def slot_table(me, lens_ref, place_ref, starts):
    rank = jnp.int32(0)
    row = [jnp.int32(-1)] * 2
    first = [jnp.int32(0)] * 2
    length = [jnp.int32(0)] * 2
    for j in range(NREQ):
        there = place_ref[j] // ROWS == me
        for k in range(2):
            hit = there & (rank == k)
            row[k] = jnp.where(hit, place_ref[j] % ROWS, row[k])
            first[k] = jnp.where(hit, starts[j], first[k])
            length[k] = jnp.where(hit, lens_ref[j], length[k])
        rank = rank + there.astype(jnp.int32)
    return row, first, length


def slot_picks(table, dq_ref, picks):
    shape = (8, ROWS * STEPS)
    place = iota(shape, 0)
    row = spread(place // STEPS, table[0], -1)
    pick = hot_matrix((row >= 0) & (iota(shape, 1) == row * STEPS + place % STEPS))
    got = mm(pick, dq_ref[...])
    picks[...] = jnp.concatenate([got[:4, p * 384 : (p + 1) * 384] for p in range(HEADS // 2)], axis=0).astype(BF16)


def all_slot_queries(raw, wkt, qh2, qa):
    lines = N_CTX * 4
    shape = (lines, N_CTX * 16)
    place = iota(shape, 0)
    for pair in range(HEADS // 2):
        pick = hot_matrix(iota(shape, 1) == (place // 4) * 16 + pair * 4 + place % 4)
        got = mm(pick, raw[...]).astype(BF16)
        for odd in range(2):
            absorb_head(got[:, odd * 128 : odd * 128 + 256], 2 * pair + odd, wkt, qh2, lines)
    count = lines * HEADS
    place = iota((count, count), 0)
    order = (place % 32) // 4 * lines + (place // 32) * 4 + place % 4
    qa[...] = mm(hot_matrix(order == iota((count, count), 1)), qh2[...]).astype(BF16)


def slot_partials(me, g_ref, starts, ends, place_ref, qa, part, stat):
    count = N_CTX * 32
    place = iota((count, 1), 0)
    slot = (place // 32) * 2 + (place % 4) // 2
    low = jnp.full((count, 1), 1 << 30, jnp.int32)
    high = jnp.full((count, 1), -1, jnp.int32)
    for j in range(NREQ):
        group = place_ref[j] // ROWS
        rank = jnp.int32(0)
        for i in range(j):
            rank = rank + (place_ref[i] // ROWS == group).astype(jnp.int32)
        hit = slot == group * 2 + rank
        low = jnp.where(hit, starts[j], low)
        high = jnp.where(hit, ends[j], high)
    lat = latent_rows(g_ref, me, 0, LATENT)
    s = mm(qa[:, :LATENT], lat) + mm(qa[:, LATENT:WIDTH], latent_rows(g_ref, me, LATENT, ROPE))
    pos = me * BLOCK + iota((count, BLOCK), 1)
    s = jnp.where((pos >= low) & (pos < high), s * FACTOR, -BIG)
    best = jnp.max(s, axis=1, keepdims=True)
    w = jnp.exp2(s - best)
    weight = jnp.sum(w, axis=1, keepdims=True)
    part[...] = (mm_nt(w.astype(BF16), lat) / weight).astype(BF16)
    stat[...] = jnp.where(iota((count, 128), 1) < 64, best, weight)


def merge_slots(me, table, qa, parts, stats, fresh_ref, lo_ref, out_rows):
    row = table[0]
    q = qa[pl.ds(pl.multiple_of(me * 32, 32), 32), :]
    fs = mm_nt(q[:, :LATENT], fresh_ref[:, :LATENT]) + mm_nt(q[:, LATENT:WIDTH], fresh_ref[:, LATENT:])
    place, col = iota(fs.shape, 0), iota(fs.shape, 1)
    open_ = (spread((place % 4) // 2, row, -1) == col // STEPS) & (col % STEPS <= place % STEPS)
    fs = jnp.where(open_, fs, -BIG) * FACTOR
    best = jnp.max(fs, axis=1, keepdims=True)
    tops = [stats[i, :, 0:1] for i in range(N_CTX)]
    for top in tops:
        best = jnp.maximum(best, top)
    fw = jnp.exp2(fs - best)
    weight = jnp.sum(fw, axis=1, keepdims=True)
    total = mm(fw.astype(BF16), fresh_ref[:, :LATENT])
    for i in range(N_CTX):
        share = jnp.exp2(tops[i] - best) * stats[i, :, 64:65]
        weight = weight + share
        total = total + share * parts[i].astype(F32)
    slot_out = (total / weight).astype(BF16)
    per = STEPS * HEADS
    shape = (ROWS * per, 32)
    spot, back = iota(shape, 0), iota(shape, 1)
    there = spread((back % 4) // 2, row, -1) == spot // per
    route = hot_matrix(there & ((spot // HEADS) % STEPS == back % STEPS) & (spot % HEADS == back // 4))
    line = iota((ROWS * per, LATENT), 0) // per
    replaced = (line == row[0]) | (line == row[1])
    out_rows[...] = jnp.where(replaced, mm(route, slot_out), lo_ref[...].astype(F32)).astype(BF16)


def head_values(rows_ref, wv_ref, x_ref):
    rows = ROWS * STEPS
    count = rows * HEADS
    order = hot_matrix(iota((count, count), 0) == to_row_major(iota((count, count), 1)))
    lat = mm(order, rows_ref[...]).astype(BF16)
    for h in range(HEADS):
        head = slice(h * NOPE, (h + 1) * NOPE)
        x_ref[:, head] = mm(lat[h * rows : (h + 1) * rows, :], wv_ref[:, head]).astype(BF16)


def z_step(v):
    zz = v // 2
    return (zz * 3) % 5 - (zz // 3) * 2


class Place:
    def __init__(self):
        self.ctx = lax.axis_index("ctx")
        self.tp = lax.axis_index("tp")
        self.core = self.ctx % 2
        self.z = self.ctx // 4
        self.x_lo = (self.ctx // 2) % 2
        self.x = (self.tp // 4) * 2 + self.x_lo
        self.y = self.tp % 4

    def at(self, dz, dx, dy=0):
        z = (self.z + dz + N_Z) % N_Z
        x = (self.x + dx + 4) % 4
        y = (self.y + dy + 4) % 4
        return ((z * 2 + x % 2) * 2 + self.core, (x // 2) * 4 + y)

    def sibling(self):
        return (self.ctx + 1 - 2 * self.core, self.tp)

    def station_pair(self, station):
        v = station + 1
        return ((self.z + z_step(v) + N_Z) % N_Z) * 2 + (self.x_lo + v) % 2


def half_rows(g_ref, block, half):
    return g_ref.at[pl.ds(pl.multiple_of(block * WIDTH + half * HALF, 32), HALF)]


def quarter_rows(g_ref, block, quarter):
    return g_ref.at[pl.ds(pl.multiple_of(block * WIDTH + quarter * QUARTER, 16), QUARTER)]


def block_rows(g_ref, block):
    return g_ref.at[pl.ds(pl.multiple_of(block * WIDTH, 64), WIDTH)]


def mega_kernel(
    lens_ref,
    place_ref,
    rlen_ref,
    q_hbm,
    own_hbm,
    wk_hbm,
    wv_hbm,
    ct_hbm,
    dq_hbm,
    fresh_hbm,
    w_hbm,
    out_hbm,
    dec_ref,
    q_ref,
    g_ref,
    wk_ref,
    wv_ref,
    ct_ref,
    dq_ref,
    fresh_ref,
    dq3,
    fresh3,
    dq32,
    fresh32,
    w_ref,
    out_ref,
    x_ref,
    wkt,
    wvt,
    qs,
    kt,
    vt,
    best,
    acc,
    qh,
    qr,
    sr,
    ar,
    lo,
    lo2,
    picks,
    raw,
    qh2,
    qa,
    part,
    stat,
    parts,
    stats,
    send,
    recv,
    load_sem,
    w_sem,
    link_send,
    link_recv,
    far_send,
    far_recv,
    core_send,
    core_recv,
    sum_send,
    sum_recv,
    slot_send,
    slot_recv,
):
    at = Place()
    me, tp = at.ctx, at.tp
    barrier = pltpu.get_barrier_semaphore()
    peers = [at.sibling()]
    aside = 1 - 2 * (at.y % 2)
    peers += [at.at(1, 0), at.at(-1, 0), at.at(2, 0), at.at(0, -1), at.at(0, 1)]
    peers += [at.at(2, 1), at.at(2, -1), at.at(1, 1), at.at(1, -1), at.at(-1, 1), at.at(-1, -1)]
    peers += [(me, (tp + d) % N_TP) for d in range(1, N_TP)]
    peers += [((me + d) % N_CTX, tp) for d in range(1, N_CTX)]
    for peer in peers:
        pl.semaphore_signal(barrier, inc=1, device_id=peer, device_id_type=MESH)

    pairs = [
        (wk_hbm, wk_ref),
        (wv_hbm, wv_ref),
        (dq_hbm, dq3),
        (fresh_hbm, fresh3),
        (ct_hbm, ct_ref),
        (q_hbm, q_ref),
        (own_hbm, block_rows(g_ref, me)),
    ]
    loads = [pltpu.make_async_copy(src, dst, load_sem.at[i]) for i, (src, dst) in enumerate(pairs)]
    for load in loads:
        load.start()
    pl.semaphore_wait(barrier, len(peers))

    sent = []

    def push(src, block, half, station, device):
        copy = pltpu.make_async_remote_copy(
            src_ref=src,
            dst_ref=half_rows(g_ref, block, half),
            send_sem=link_send.at[station, half],
            recv_sem=link_recv.at[station, half],
            device_id=device,
            device_id_type=MESH,
        )
        copy.start()
        sent.append(copy)

    def own_half(half):
        return own_hbm.at[half * HALF : (half + 1) * HALF]

    def push_quarter(src, block, quarter, which, step, device):
        copy = pltpu.make_async_remote_copy(
            src_ref=src,
            dst_ref=quarter_rows(g_ref, block, quarter),
            send_sem=far_send.at[which, step],
            recv_sem=far_recv.at[which, step],
            device_id=device,
            device_id_type=MESH,
        )
        copy.start()
        sent.append(copy)

    own_quarter = own_hbm.at[pl.ds(pl.multiple_of(at.y * QUARTER, 16), QUARTER)]
    for which, device in enumerate((at.at(2, 0), at.at(2, aside), at.at(-1, aside))):
        push_quarter(own_quarter, me, at.y, which, 0, device)
    for half in range(2):
        push(own_half(half), me, half, 0, at.at(0, 2 * half - 1))
        push(own_half(half), me, half, 1, at.at(1, 0))
    own_to_core = pltpu.make_async_remote_copy(
        src_ref=own_hbm,
        dst_ref=block_rows(g_ref, me),
        send_sem=core_send.at[N_STATION],
        recv_sem=core_recv.at[N_STATION],
        device_id=at.sibling(),
        device_id_type=MESH,
    )
    own_to_core.start()
    sent.append(own_to_core)

    def landed(station, half):
        block = 2 * at.station_pair(station) + at.core
        pltpu.make_async_copy(own_half(half), half_rows(g_ref, block, half), link_recv.at[station, half]).wait()

    def share_x(half):
        landed(1, half)
        block = 2 * at.station_pair(1) + at.core
        push(half_rows(g_ref, block, half), block, half, 2, at.at(0, 2 * half - 1))

    def landed_quarter(which, step):
        block = 2 * at.station_pair(FAR[which]) + at.core
        quarter = (at.y - step + 4) % 4
        source = own_hbm.at[0:QUARTER]
        pltpu.make_async_copy(source, quarter_rows(g_ref, block, quarter), far_recv.at[which, step]).wait()

    def share_far(which):
        landed_quarter(which, 0)
        block = 2 * at.station_pair(FAR[which]) + at.core
        mine = quarter_rows(g_ref, block, at.y)
        for step in (1, 3, 2):
            push_quarter(mine, block, at.y, which, step, at.at(0, 0, step))

    def to_core(station):
        block = 2 * at.station_pair(station) + at.core
        copy = pltpu.make_async_remote_copy(
            src_ref=block_rows(g_ref, block),
            dst_ref=block_rows(g_ref, block),
            send_sem=core_send.at[station],
            recv_sem=core_recv.at[station],
            device_id=at.sibling(),
            device_id_type=MESH,
        )
        copy.start()
        sent.append(copy)

    def from_core(station, pair):
        block = 2 * pair + 1 - at.core
        pltpu.make_async_copy(own_hbm, block_rows(g_ref, block), core_recv.at[station]).wait()

    def spread_to(src, dst, kind, d):
        copy = pltpu.make_async_remote_copy(
            src_ref=src,
            dst_ref=dst,
            send_sem=slot_send.at[kind, d],
            recv_sem=slot_recv.at[kind, d],
            device_id=((me + d) % N_CTX, tp),
            device_id_type=MESH,
        )
        copy.start()
        slot_copies[kind].append(copy)

    slot_copies = ([], [], [])

    starts, ends = request_table(lens_ref)
    table = slot_table(me, lens_ref, place_ref, starts)
    loads[2].wait()
    pack_rows(dq3, dq32, dq_ref)
    slot_picks(table, dq_ref, picks)
    raw[pl.ds(pl.multiple_of(me * 16, 16), 16), :] = picks[...]
    for d in range(1, N_CTX):
        spread_to(picks, raw.at[pl.ds(pl.multiple_of(me * 16, 16), 16)], 0, d)
    loads[0].wait()
    loads[1].wait()
    prepare_weights(wk_ref, wv_ref, wkt, wvt)
    loads[3].wait()
    pack_rows(fresh3, fresh32, fresh_ref)
    decode_queries(dq_ref, wkt, qh, qr)
    loads[5].wait()
    prepare_queries(me, q_ref, starts, ends, qs)
    step = functools.partial(
        attend_pair,
        me=me,
        g_ref=g_ref,
        starts=starts,
        ends=ends,
        wkt=wkt,
        wvt=wvt,
        qs=qs,
        kt=kt,
        vt=vt,
        best=best,
        acc=acc,
    )
    own = me // 2
    loads[6].wait()
    from_core(N_STATION, own)
    step(own, True)
    for copy in slot_copies[0]:
        copy.wait_recv()
    all_slot_queries(raw, wkt, qh2, qa)
    slot_partials(me, g_ref, starts, ends, place_ref, qa, part, stat)
    mine = pl.ds(pl.multiple_of(me * 32, 32), 32)
    parts[me] = part[mine, :]
    stats[me] = stat[mine, :]
    for d in range(1, N_CTX):
        theirs = pl.ds(pl.multiple_of(((me + d) % N_CTX) * 32, 32), 32)
        spread_to(part.at[theirs], parts.at[me], 1, d)
        spread_to(stat.at[theirs], stats.at[me], 2, d)
    for which in range(3):
        share_far(which)
    loads[4].wait()
    w_loads = []
    first = 0
    for c, width in enumerate(CHUNKS):
        cols = slice(first, first + width)
        w_loads.append(pltpu.make_async_copy(w_hbm.at[:, cols], w_ref.at[:, cols], w_sem.at[c]))
        w_loads[-1].start()
        first += width
    decode_resident(qr, ct_ref, fresh_ref, rlen_ref, sr, ar, lo)
    for half in range(2):
        landed(0, half)
    to_core(0)
    share_x(0)
    share_x(1)
    to_core(1)

    def project():
        copies = []
        first = 0
        for c, width in enumerate(CHUNKS):
            quarter = width // 4
            q0 = first // 4
            w_loads[c].wait()
            part = mm(x_ref[...], w_ref[:, first : first + width])
            for p in range(N_TP):
                rows = part[4 * p : 4 * p + 4, :]
                piece = jnp.concatenate([rows[:, k * quarter : (k + 1) * quarter] for k in range(4)], axis=0)
                send[p, :, q0 : q0 + quarter] = piece.astype(BF16)
            for d in range(1, N_TP):
                peer = (tp + d) % N_TP
                copy = pltpu.make_async_remote_copy(
                    src_ref=send.at[peer, :, q0 : q0 + quarter],
                    dst_ref=recv.at[d, :, q0 : q0 + quarter],
                    send_sem=sum_send.at[c, d],
                    recv_sem=sum_recv.at[c, d],
                    device_id=(me, peer),
                    device_id_type=MESH,
                )
                copy.start()
                copies.append((c, d, copy))
            first += width
        return copies

    def near(station):
        pair = at.station_pair(station)
        from_core(station, pair)

        @pl.when((pair < own) & (pair >= own - 5))
        def _():
            step(pair, False)

    @pl.loop(0, 2)
    def _(station):
        near(station)

    for half in range(2):
        landed(2, half)
    to_core(2)
    for which in range(3):
        for step_y in range(1, 4):
            landed_quarter(which, step_y)
        to_core(FAR[which])
    near(2)

    for kind in (1, 2):
        for copy in slot_copies[kind]:
            copy.wait_recv()
    merge_slots(me, table, qa, parts, stats, fresh_ref, lo, lo2)
    head_values(lo2, wv_ref, x_ref)
    sums = project()

    for station in (4, 5, 6):
        from_core(station, at.station_pair(station))

    @pl.loop(4, N_STATION)
    def _(station):
        pair = at.station_pair(station)

        @pl.when((pair < own) & (pair >= own - 5))
        def _():
            step(pair, False)

    finish_prefill(acc, out_ref)
    store = pltpu.make_async_copy(out_ref, out_hbm, load_sem.at[len(pairs)])
    store.start()

    first = 0
    for c, width in enumerate(CHUNKS):
        quarter = width // 4
        q0 = first // 4
        total = send[tp, :, q0 : q0 + quarter].astype(F32)
        for c2, d, copy in sums:
            if c2 == c:
                copy.wait_recv()
                total = total + recv[d, :, q0 : q0 + quarter].astype(F32)
        for k in range(4):
            for row in range(2):
                piece = total[4 * k + 2 * row : 4 * k + 2 * row + 2, :]
                dec_ref[row, :, first + k * quarter : first + (k + 1) * quarter] = piece.astype(BF16)
        first += width
    for _, _, copy in sums:
        copy.wait_send()
    for copy in sent + slot_copies[0] + slot_copies[1] + slot_copies[2]:
        copy.wait_send()
    store.wait()


def mega(lens, place, rlen, q, own, wk, wv, ct, dq, fresh, w):
    smem = pl.BlockSpec(memory_space=pltpu.SMEM)
    vmem = pl.BlockSpec(memory_space=pltpu.VMEM)
    far = pl.BlockSpec(memory_space=pl.ANY)
    lines = ROWS * STEPS * HEADS
    width = w.shape[1]
    dma = pltpu.SemaphoreType.DMA
    return pl.pallas_call(
        mega_kernel,
        out_shape=(
            jax.ShapeDtypeStruct((BLOCK, HEADS * NOPE), BF16),
            jax.ShapeDtypeStruct((2, STEPS, width), BF16),
        ),
        in_specs=[smem] * 3 + [far] * 8,
        out_specs=(far, vmem),
        scratch_shapes=[
            pltpu.VMEM(q.shape, BF16),
            pltpu.VMEM((N_CTX * WIDTH, BLOCK), BF16),
            pltpu.VMEM(wk.shape, BF16),
            pltpu.VMEM(wv.shape, BF16),
            pltpu.VMEM(ct.shape, BF16),
            pltpu.VMEM((ROWS * STEPS, dq.shape[2]), BF16),
            pltpu.VMEM((ROWS * STEPS, WIDTH), BF16),
            pltpu.VMEM(dq.shape, BF16),
            pltpu.VMEM(fresh.shape, BF16),
            pltpu.VMEM((ROWS * STEPS, dq.shape[2]), F32),
            pltpu.VMEM((ROWS * STEPS, WIDTH), F32),
            pltpu.VMEM(w.shape, BF16),
            pltpu.VMEM((BLOCK, HEADS * NOPE), BF16),
            pltpu.VMEM((ROWS * STEPS, HEADS * NOPE), BF16),
            pltpu.VMEM((HEADS * NOPE, LATENT), BF16),
            pltpu.VMEM((HEADS * NOPE, LATENT), BF16),
            pltpu.VMEM((HEADS, BLOCK, 256), BF16),
            pltpu.VMEM((HEADS * NOPE, 2 * BLOCK), BF16),
            pltpu.VMEM((HEADS * NOPE, 2 * BLOCK), BF16),
            pltpu.VMEM((HEADS, BLOCK, 128), F32),
            pltpu.VMEM((HEADS, BLOCK, 256), F32),
            pltpu.VMEM((lines, 640), BF16),
            pltpu.VMEM((lines, 640), BF16),
            pltpu.VMEM((lines, BLOCK), F32),
            pltpu.VMEM((lines, LATENT), F32),
            pltpu.VMEM((lines, LATENT), BF16),
            pltpu.VMEM((lines, LATENT), BF16),
            pltpu.VMEM((16, 384), BF16),
            pltpu.VMEM((N_CTX * 16, 384), BF16),
            pltpu.VMEM((N_CTX * 32, 640), BF16),
            pltpu.VMEM((N_CTX * 32, 640), BF16),
            pltpu.VMEM((N_CTX * 32, LATENT), BF16),
            pltpu.VMEM((N_CTX * 32, 128), F32),
            pltpu.VMEM((N_CTX, 32, LATENT), BF16),
            pltpu.VMEM((N_CTX, 32, 128), F32),
            pltpu.VMEM((N_TP, 16, width // 4), BF16),
            pltpu.VMEM((N_TP, 16, width // 4), BF16),
            dma((8,)),
            dma((len(CHUNKS),)),
            dma((3, 2)),
            dma((3, 2)),
            dma((3, 4)),
            dma((3, 4)),
            dma((N_STATION + 1,)),
            dma((N_STATION + 1,)),
            dma((len(CHUNKS), N_TP)),
            dma((len(CHUNKS), N_TP)),
            dma((3, N_CTX)),
            dma((3, N_CTX)),
        ],
        compiler_params=pltpu.CompilerParams(collective_id=0, has_side_effects=True, vmem_limit_bytes=60 * MIB),
        name="latent_attention",
    )(lens, place, rlen, q, own, wk, wv, ct, dq, fresh, w)


def on_device(
    prefill_query,
    span_latent,
    prompt_lengths,
    key_weight,
    value_weight,
    placement,
    resident_cache,
    resident_lengths,
    decode_query,
    decode_latent,
    out_weight,
):
    cache_t = jnp.swapaxes(resident_cache, 1, 2).reshape(ROWS * WIDTH, BLOCK)
    return mega(
        prompt_lengths,
        placement,
        resident_lengths,
        prefill_query,
        span_latent.T,
        key_weight,
        value_weight,
        cache_t,
        decode_query,
        decode_latent,
        out_weight,
    )


def solution(mesh):
    placed = (
        P("ctx", "tp"),
        P("ctx", None),
        P(),
        P(None, "tp"),
        P(None, "tp"),
        P(),
        P("ctx", None, None),
        P("ctx"),
        P("ctx", None, "tp"),
        P("ctx", None, None),
        P("tp", None),
    )
    return jax.shard_map(
        on_device,
        mesh=mesh,
        in_specs=placed,
        out_specs=(P("ctx", "tp"), P(("ctx", "tp"), None, None)),
        check_vma=False,
    )
```

```python
import functools
import math

import jax
import jax.numpy as jnp
from jax import lax
from jax.experimental import pallas as pl
from jax.experimental.pallas import tpu as pltpu
from jax.sharding import PartitionSpec as P

MESH = pl.DeviceIdType.MESH
NOPE = 128
ROPE = 64
LATENT = 512
WIDTH = LATENT + ROPE
BLOCK = 256
N_CTX = 16
N_TP = 8
HEADS = 8
ROWS = 16
STEPS = 2
NREQ = 8
BIG = 1e30
FACTOR = math.log2(math.e) / math.sqrt(NOPE + ROPE)
F32 = jnp.float32
BF16 = jnp.bfloat16
MIB = 1 << 20
HALF = WIDTH // 2
QUARTER = WIDTH // 4
N_Z = 4
N_STATION = 7
FAR = (5, 6)
CHUNKS = (2048, 2048, 2048, 1024)


def mm(left, right):
    return lax.dot_general(left, right, (((1,), (0,)), ((), ())), preferred_element_type=F32)


def mm_nt(left, right):
    return lax.dot_general(left, right, (((1,), (1,)), ((), ())), preferred_element_type=F32)


def iota(shape, dim):
    return lax.broadcasted_iota(jnp.int32, shape, dim)


def request_table(lens_ref):
    starts, ends, total = [], [], jnp.int32(0)
    for j in range(NREQ):
        starts.append(total)
        total = total + lens_ref[j]
        ends.append(total)
    return starts, ends


def spread(index, values, other):
    out = jnp.full(index.shape, other, jnp.int32)
    for j, value in enumerate(values):
        out = jnp.where(index == j, value, out)
    return out


def prepare_weights(wk_ref, wv_ref, wkt, wvt):
    wkt[...] = wk_ref[...].T
    wvt[...] = wv_ref[...].T


def prepare_queries(me, q_ref, starts, ends, qs):
    lane = iota((BLOCK, 256), 1)
    pos = me * BLOCK + iota((BLOCK, 256), 0)
    for odd in range(2):
        slot = lane if odd else lane - 192
        first = spread(slot, starts, 1 << 30)
        last = spread(slot, ends, -1)
        hot = ((pos >= first) & (pos < last)).astype(F32)
        spare = lane < 64 if odd else lane >= 192
        for pair in range(HEADS // 2):
            base = pair * 384 + odd * 128
            window = q_ref[:, base : base + 256].astype(F32)
            qs[2 * pair + odd] = jnp.where(spare, hot, window).astype(BF16)


def latent_rows(g_ref, block, first, count):
    return g_ref[pl.ds(pl.multiple_of(block * WIDTH + first, 64), count), :]


def attend_pair(pair, causal, me, g_ref, starts, ends, wkt, wvt, qs, kt, vt, best, acc):
    ropes = []
    for half in range(2):
        lat = latent_rows(g_ref, 2 * pair + half, 0, LATENT)
        cols = slice(half * BLOCK, (half + 1) * BLOCK)
        kt[:, cols] = mm(wkt[...], lat).astype(BF16)
        vt[:, cols] = mm(wvt[...], lat).astype(BF16)
        ropes.append(latent_rows(g_ref, 2 * pair + half, LATENT, ROPE))
    rope = jnp.concatenate(ropes, axis=1)
    keys = 2 * BLOCK
    slot = iota((ROPE, keys), 0)
    key_pos = pair * keys + iota((ROPE, keys), 1)
    outside = (slot < NREQ) & ((key_pos < spread(slot, starts, 0)) | (key_pos >= spread(slot, ends, 0)))
    aug = jnp.where(outside, -BIG, 0.0).astype(BF16)
    ones = jnp.ones((NOPE, keys), BF16)
    for h in range(HEADS):
        head = slice(h * NOPE, (h + 1) * NOPE)
        parts = [aug, kt[head, :], rope] if h % 2 else [kt[head, :], rope, aug]
        s = mm(qs[h], jnp.concatenate(parts, axis=0))
        if causal:
            ahead = pair * keys + iota((BLOCK, keys), 1) > me * BLOCK + iota((BLOCK, keys), 0)
            s = jnp.where(ahead, -BIG, s)
        block_best = jnp.max(s, axis=1, keepdims=True) * FACTOR
        values = jnp.concatenate([vt[head, :], ones], axis=0)
        if causal:
            new_best = jnp.broadcast_to(block_best, (BLOCK, 128))
        else:
            new_best = jnp.maximum(best[h], block_best)
        p = jnp.exp2(s * FACTOR - jnp.concatenate([new_best] * 4, axis=1)).astype(BF16)
        gained = mm_nt(p, values)
        if causal:
            acc[h] = gained
        else:
            keep = jnp.exp2(best[h] - new_best)
            acc[h] = acc[h] * jnp.concatenate([keep] * 2, axis=1) + gained
        best[h] = new_best


def finish_prefill(acc, out_ref):
    for h in range(HEADS):
        out_ref[:, h * NOPE : (h + 1) * NOPE] = (acc[h][:, :NOPE] / acc[h][:, NOPE:]).astype(BF16)


def to_row_major(index):
    return (index % HEADS) * (ROWS * STEPS) + index // HEADS


def hot_matrix(condition):
    return condition.astype(F32).astype(BF16)


def pack_rows(rows_ref, wide_ref, flat_ref):
    for r in range(ROWS):
        wide_ref[r * STEPS : (r + 1) * STEPS, :] = rows_ref[r].astype(F32)
    flat_ref[...] = wide_ref[...].astype(BF16)


def decode_queries(dq_ref, wkt, qh, qr):
    rows = ROWS * STEPS
    eye = hot_matrix(iota((ROPE, 128), 0) == iota((ROPE, 128), 1))
    side = jnp.zeros((ROPE, 128), BF16)
    below = jnp.zeros((ROPE, LATENT), BF16)
    for h in range(HEADS):
        base = (h // 2) * 384 + (h % 2) * 128
        window = dq_ref[:, base : base + 256]
        weight = wkt[h * NOPE : (h + 1) * NOPE, :]
        lat = [below, weight, below] if h % 2 else [weight, below, below]
        rot = [side, side, side, eye] if h % 2 else [side, side, eye, side]
        qh[h * rows : (h + 1) * rows, :LATENT] = mm(window, jnp.concatenate(lat, axis=0)).astype(BF16)
        qh[h * rows : (h + 1) * rows, LATENT:] = mm(window, jnp.concatenate(rot, axis=0)).astype(BF16)
    count = rows * HEADS
    order = hot_matrix(to_row_major(iota((count, count), 0)) == iota((count, count), 1))
    qr[...] = mm(order, qh[...]).astype(BF16)


def scores_of(queries, lat, rope):
    return mm(queries[:, :LATENT], lat) + mm(queries[:, LATENT:WIDTH], rope)


def decode_resident(qr, ct_ref, fresh_ref, rlen_ref, sr, ar, lo):
    per = STEPS * HEADS
    for r in range(ROWS):
        rows = slice(r * per, (r + 1) * per)
        sr[rows, :] = scores_of(
            qr[rows, :], ct_ref[r * WIDTH : r * WIDTH + LATENT, :], ct_ref[r * WIDTH + LATENT : (r + 1) * WIDTH, :]
        )
    count = ROWS * per
    row_of = iota((count, BLOCK), 0) // per
    filled = spread(row_of, [rlen_ref[r] for r in range(ROWS)], 0)
    s = jnp.where(iota((count, BLOCK), 1) < filled, sr[...], -BIG) * FACTOR
    fs = mm_nt(qr[:, :LATENT], fresh_ref[:, :LATENT]) + mm_nt(qr[:, LATENT:WIDTH], fresh_ref[:, LATENT:])
    place, col = iota(fs.shape, 0), iota(fs.shape, 1)
    open_ = (place // per == col // STEPS) & (col % STEPS <= (place // HEADS) % STEPS)
    fs = jnp.where(open_, fs, -BIG) * FACTOR
    best = jnp.maximum(jnp.max(s, axis=1, keepdims=True), jnp.max(fs, axis=1, keepdims=True))
    w = jnp.exp2(s - best)
    fw = jnp.exp2(fs - best)
    total = jnp.sum(w, axis=1, keepdims=True) + jnp.sum(fw, axis=1, keepdims=True)
    sr[...] = w
    for r in range(ROWS):
        rows = slice(r * per, (r + 1) * per)
        ar[rows, :] = mm_nt(sr[rows, :].astype(BF16), ct_ref[r * WIDTH : r * WIDTH + LATENT, :])
    lo[...] = ((ar[...] + mm(fw.astype(BF16), fresh_ref[:, :LATENT])) / total).astype(BF16)


def slot_table(me, lens_ref, place_ref, starts):
    rank = jnp.int32(0)
    row = [jnp.int32(-1)] * 2
    first = [jnp.int32(0)] * 2
    length = [jnp.int32(0)] * 2
    for j in range(NREQ):
        there = place_ref[j] // ROWS == me
        for k in range(2):
            hit = there & (rank == k)
            row[k] = jnp.where(hit, place_ref[j] % ROWS, row[k])
            first[k] = jnp.where(hit, starts[j], first[k])
            length[k] = jnp.where(hit, lens_ref[j], length[k])
        rank = rank + there.astype(jnp.int32)
    return row, first, length


def slot_queries(table, qr, qs2):
    per = STEPS * HEADS
    shape = (2 * per, ROWS * per)
    place = iota(shape, 0)
    row = spread(place // per, table[0], -1)
    pick = hot_matrix((row >= 0) & (iota(shape, 1) == row * per + place % per))
    qs2[...] = mm(pick, qr[...]).astype(BF16)


def slot_scores(block, g_ref, qs2, ss):
    ss[block] = scores_of(qs2[...], latent_rows(g_ref, block, 0, LATENT), latent_rows(g_ref, block, LATENT, ROPE))


def decode_slots(table, g_ref, qs2, ss, fresh_ref, lo_ref, out_rows):
    per = STEPS * HEADS
    row, first, length = table
    lines = 2 * per
    slot = iota((lines, BLOCK), 0) // per
    low = spread(slot, first, 0)
    high = low + spread(slot, length, 0)
    fs = mm_nt(qs2[:, :LATENT], fresh_ref[:, :LATENT]) + mm_nt(qs2[:, LATENT:WIDTH], fresh_ref[:, LATENT:])
    place, col = iota(fs.shape, 0), iota(fs.shape, 1)
    open_ = (spread(place // per, row, -1) == col // STEPS) & (col % STEPS <= (place // HEADS) % STEPS)
    fs = jnp.where(open_, fs, -BIG) * FACTOR
    best = jnp.max(fs, axis=1, keepdims=True)
    peak = jnp.full((lines, BLOCK), -BIG, F32)
    for b in range(N_CTX):
        pos = b * BLOCK + iota((lines, BLOCK), 1)
        s = jnp.where((pos >= low) & (pos < high), ss[b] * FACTOR, -BIG)
        ss[b] = s
        peak = jnp.maximum(peak, s)
    best = jnp.maximum(best, jnp.max(peak, axis=1, keepdims=True))
    fw = jnp.exp2(fs - best)
    mass = jnp.zeros((lines, BLOCK), F32)
    total = mm(fw.astype(BF16), fresh_ref[:, :LATENT])
    for b in range(N_CTX):
        w = jnp.exp2(ss[b] - best)
        mass = mass + w
        total = total + mm_nt(w.astype(BF16), latent_rows(g_ref, b, 0, LATENT))
    weight = jnp.sum(mass, axis=1, keepdims=True) + jnp.sum(fw, axis=1, keepdims=True)
    slot_out = (total / weight).astype(BF16)
    shape = (ROWS * per, lines)
    back = iota(shape, 1)
    back_row = spread(back // per, row, -1)
    route = hot_matrix((back_row >= 0) & (iota(shape, 0) == back_row * per + back % per))
    spot = iota((ROWS * per, LATENT), 0) // per
    replaced = (spot == row[0]) | (spot == row[1])
    out_rows[...] = jnp.where(replaced, mm(route, slot_out), lo_ref[...].astype(F32)).astype(BF16)


def head_values(rows_ref, wv_ref, x_ref):
    rows = ROWS * STEPS
    count = rows * HEADS
    order = hot_matrix(iota((count, count), 0) == to_row_major(iota((count, count), 1)))
    lat = mm(order, rows_ref[...]).astype(BF16)
    for h in range(HEADS):
        head = slice(h * NOPE, (h + 1) * NOPE)
        x_ref[:, head] = mm(lat[h * rows : (h + 1) * rows, :], wv_ref[:, head]).astype(BF16)


def z_step(v):
    zz = v // 2
    return (zz * 3) % 5 - (zz // 3) * 2


class Place:
    def __init__(self):
        self.ctx = lax.axis_index("ctx")
        self.tp = lax.axis_index("tp")
        self.core = self.ctx % 2
        self.z = self.ctx // 4
        self.x_lo = (self.ctx // 2) % 2
        self.x = (self.tp // 4) * 2 + self.x_lo
        self.y = self.tp % 4

    def at(self, dz, dx, dy=0):
        z = (self.z + dz + N_Z) % N_Z
        x = (self.x + dx + 4) % 4
        y = (self.y + dy + 4) % 4
        return ((z * 2 + x % 2) * 2 + self.core, (x // 2) * 4 + y)

    def sibling(self):
        return (self.ctx + 1 - 2 * self.core, self.tp)

    def station_pair(self, station):
        v = station + 1
        return ((self.z + z_step(v) + N_Z) % N_Z) * 2 + (self.x_lo + v) % 2


def half_rows(g_ref, block, half):
    return g_ref.at[pl.ds(pl.multiple_of(block * WIDTH + half * HALF, 32), HALF)]


def quarter_rows(g_ref, block, quarter):
    return g_ref.at[pl.ds(pl.multiple_of(block * WIDTH + quarter * QUARTER, 16), QUARTER)]


def block_rows(g_ref, block):
    return g_ref.at[pl.ds(pl.multiple_of(block * WIDTH, 64), WIDTH)]


def mega_kernel(
    lens_ref,
    place_ref,
    rlen_ref,
    q_hbm,
    own_hbm,
    wk_hbm,
    wv_hbm,
    ct_hbm,
    dq_hbm,
    fresh_hbm,
    w_hbm,
    out_hbm,
    dec_ref,
    q_ref,
    g_ref,
    wk_ref,
    wv_ref,
    ct_ref,
    dq_ref,
    fresh_ref,
    dq3,
    fresh3,
    dq32,
    fresh32,
    w_ref,
    out_ref,
    x_ref,
    wkt,
    wvt,
    qs,
    kt,
    vt,
    best,
    acc,
    qh,
    qr,
    sr,
    ar,
    lo,
    qs2,
    ss,
    lo2,
    send,
    recv,
    load_sem,
    w_sem,
    link_send,
    link_recv,
    far_send,
    far_recv,
    core_send,
    core_recv,
    sum_send,
    sum_recv,
):
    at = Place()
    me, tp = at.ctx, at.tp
    barrier = pltpu.get_barrier_semaphore()
    peers = [at.sibling()]
    aside = 1 - 2 * (at.y % 2)
    peers += [at.at(1, 0), at.at(-1, 0), at.at(2, 0), at.at(0, -1), at.at(0, 1)]
    peers += [at.at(2, 1), at.at(2, -1)]
    peers += [(me, (tp + d) % N_TP) for d in range(1, N_TP)]
    for peer in peers:
        pl.semaphore_signal(barrier, inc=1, device_id=peer, device_id_type=MESH)

    pairs = [
        (wk_hbm, wk_ref),
        (wv_hbm, wv_ref),
        (dq_hbm, dq3),
        (fresh_hbm, fresh3),
        (ct_hbm, ct_ref),
        (q_hbm, q_ref),
        (own_hbm, block_rows(g_ref, me)),
    ]
    loads = [pltpu.make_async_copy(src, dst, load_sem.at[i]) for i, (src, dst) in enumerate(pairs)]
    for load in loads:
        load.start()
    pl.semaphore_wait(barrier, len(peers))

    sent = []

    def push(src, block, half, station, device):
        copy = pltpu.make_async_remote_copy(
            src_ref=src,
            dst_ref=half_rows(g_ref, block, half),
            send_sem=link_send.at[station, half],
            recv_sem=link_recv.at[station, half],
            device_id=device,
            device_id_type=MESH,
        )
        copy.start()
        sent.append(copy)

    def own_half(half):
        return own_hbm.at[half * HALF : (half + 1) * HALF]

    def push_quarter(src, block, quarter, which, step, device):
        copy = pltpu.make_async_remote_copy(
            src_ref=src,
            dst_ref=quarter_rows(g_ref, block, quarter),
            send_sem=far_send.at[which, step],
            recv_sem=far_recv.at[which, step],
            device_id=device,
            device_id_type=MESH,
        )
        copy.start()
        sent.append(copy)

    own_quarter = own_hbm.at[pl.ds(pl.multiple_of(at.y * QUARTER, 16), QUARTER)]
    for which, device in enumerate((at.at(2, 0), at.at(2, aside))):
        push_quarter(own_quarter, me, at.y, which, 0, device)
    for half in range(2):
        push(own_half(half), me, half, 0, at.at(0, 2 * half - 1))
    own_to_core = pltpu.make_async_remote_copy(
        src_ref=own_hbm,
        dst_ref=block_rows(g_ref, me),
        send_sem=core_send.at[N_STATION],
        recv_sem=core_recv.at[N_STATION],
        device_id=at.sibling(),
        device_id_type=MESH,
    )
    own_to_core.start()
    sent.append(own_to_core)

    def landed(station, half):
        block = 2 * at.station_pair(station) + at.core
        pltpu.make_async_copy(own_half(half), half_rows(g_ref, block, half), link_recv.at[station, half]).wait()

    def share_x(half):
        for station in (1, 3):
            landed(station, half)
            block = 2 * at.station_pair(station) + at.core
            push(half_rows(g_ref, block, half), block, half, station + 1, at.at(0, 2 * half - 1))

    def landed_quarter(which, step):
        block = 2 * at.station_pair(FAR[which]) + at.core
        quarter = (at.y - step + 4) % 4
        source = own_hbm.at[0:QUARTER]
        pltpu.make_async_copy(source, quarter_rows(g_ref, block, quarter), far_recv.at[which, step]).wait()

    def share_far(which):
        landed_quarter(which, 0)
        block = 2 * at.station_pair(FAR[which]) + at.core
        mine = quarter_rows(g_ref, block, at.y)
        for step in (1, 3, 2):
            push_quarter(mine, block, at.y, which, step, at.at(0, 0, step))

    def to_core(station):
        block = 2 * at.station_pair(station) + at.core
        copy = pltpu.make_async_remote_copy(
            src_ref=block_rows(g_ref, block),
            dst_ref=block_rows(g_ref, block),
            send_sem=core_send.at[station],
            recv_sem=core_recv.at[station],
            device_id=at.sibling(),
            device_id_type=MESH,
        )
        copy.start()
        sent.append(copy)

    def from_core(station, pair):
        block = 2 * pair + 1 - at.core
        pltpu.make_async_copy(own_hbm, block_rows(g_ref, block), core_recv.at[station]).wait()

    starts, ends = request_table(lens_ref)
    table = slot_table(me, lens_ref, place_ref, starts)
    loads[0].wait()
    loads[1].wait()
    prepare_weights(wk_ref, wv_ref, wkt, wvt)
    for half in range(2):
        push(own_half(half), me, half, 1, at.at(1, 0))
        push(own_half(half), me, half, 3, at.at(-1, 0))
    loads[2].wait()
    loads[3].wait()
    pack_rows(dq3, dq32, dq_ref)
    pack_rows(fresh3, fresh32, fresh_ref)
    decode_queries(dq_ref, wkt, qh, qr)
    slot_queries(table, qr, qs2)
    loads[5].wait()
    prepare_queries(me, q_ref, starts, ends, qs)
    step = functools.partial(
        attend_pair,
        me=me,
        g_ref=g_ref,
        starts=starts,
        ends=ends,
        wkt=wkt,
        wvt=wvt,
        qs=qs,
        kt=kt,
        vt=vt,
        best=best,
        acc=acc,
    )
    own = me // 2
    loads[6].wait()
    from_core(N_STATION, own)
    step(own, True)
    for half in range(2):
        slot_scores(2 * own + half, g_ref, qs2, ss)
    for which in range(2):
        share_far(which)
    loads[4].wait()
    w_loads = []
    first = 0
    for c, width in enumerate(CHUNKS):
        cols = slice(first, first + width)
        w_loads.append(pltpu.make_async_copy(w_hbm.at[:, cols], w_ref.at[:, cols], w_sem.at[c]))
        w_loads[-1].start()
        first += width
    decode_resident(qr, ct_ref, fresh_ref, rlen_ref, sr, ar, lo)
    for half in range(2):
        landed(0, half)
    to_core(0)
    share_x(0)
    share_x(1)
    to_core(1)
    to_core(3)

    def project():
        copies = []
        first = 0
        for c, width in enumerate(CHUNKS):
            quarter = width // 4
            q0 = first // 4
            w_loads[c].wait()
            part = mm(x_ref[...], w_ref[:, first : first + width])
            for p in range(N_TP):
                rows = part[4 * p : 4 * p + 4, :]
                piece = jnp.concatenate([rows[:, k * quarter : (k + 1) * quarter] for k in range(4)], axis=0)
                send[p, :, q0 : q0 + quarter] = piece.astype(BF16)
            for d in range(1, N_TP):
                peer = (tp + d) % N_TP
                copy = pltpu.make_async_remote_copy(
                    src_ref=send.at[peer, :, q0 : q0 + quarter],
                    dst_ref=recv.at[d, :, q0 : q0 + quarter],
                    send_sem=sum_send.at[c, d],
                    recv_sem=sum_recv.at[c, d],
                    device_id=(me, peer),
                    device_id_type=MESH,
                )
                copy.start()
                copies.append((c, d, copy))
            first += width
        return copies

    def near(station):
        pair = at.station_pair(station)
        from_core(station, pair)

        @pl.when((pair < own) & (pair >= own - 5))
        def _():
            step(pair, False)

    @pl.loop(0, 2)
    def _(station):
        near(station)

    for station in (2, 4):
        for half in range(2):
            landed(station, half)
        to_core(station)
    near(2)
    for which in range(2):
        for step_y in range(1, 4):
            landed_quarter(which, step_y)
        to_core(FAR[which])
    for station in range(3):
        for half in range(2):
            slot_scores(2 * at.station_pair(station) + half, g_ref, qs2, ss)
    for station in (3, 4, 5, 6):
        from_core(station, at.station_pair(station))

    for station in (3, 4, 5, 6):
        for half in range(2):
            slot_scores(2 * at.station_pair(station) + half, g_ref, qs2, ss)
    decode_slots(table, g_ref, qs2, ss, fresh_ref, lo, lo2)
    head_values(lo2, wv_ref, x_ref)
    sums = project()

    @pl.loop(4, N_STATION)
    def _(station):
        pair = at.station_pair(station)

        @pl.when((pair < own) & (pair >= own - 5))
        def _():
            step(pair, False)

    finish_prefill(acc, out_ref)
    store = pltpu.make_async_copy(out_ref, out_hbm, load_sem.at[len(pairs)])
    store.start()

    first = 0
    for c, width in enumerate(CHUNKS):
        quarter = width // 4
        q0 = first // 4
        total = send[tp, :, q0 : q0 + quarter].astype(F32)
        for c2, d, copy in sums:
            if c2 == c:
                copy.wait_recv()
                total = total + recv[d, :, q0 : q0 + quarter].astype(F32)
        for k in range(4):
            for row in range(2):
                piece = total[4 * k + 2 * row : 4 * k + 2 * row + 2, :]
                dec_ref[row, :, first + k * quarter : first + (k + 1) * quarter] = piece.astype(BF16)
        first += width
    for _, _, copy in sums:
        copy.wait_send()
    for copy in sent:
        copy.wait_send()
    store.wait()


def mega(lens, place, rlen, q, own, wk, wv, ct, dq, fresh, w):
    smem = pl.BlockSpec(memory_space=pltpu.SMEM)
    vmem = pl.BlockSpec(memory_space=pltpu.VMEM)
    far = pl.BlockSpec(memory_space=pl.ANY)
    lines = ROWS * STEPS * HEADS
    two = 2 * STEPS * HEADS
    width = w.shape[1]
    dma = pltpu.SemaphoreType.DMA
    return pl.pallas_call(
        mega_kernel,
        out_shape=(
            jax.ShapeDtypeStruct((BLOCK, HEADS * NOPE), BF16),
            jax.ShapeDtypeStruct((2, STEPS, width), BF16),
        ),
        in_specs=[smem] * 3 + [far] * 8,
        out_specs=(far, vmem),
        scratch_shapes=[
            pltpu.VMEM(q.shape, BF16),
            pltpu.VMEM((N_CTX * WIDTH, BLOCK), BF16),
            pltpu.VMEM(wk.shape, BF16),
            pltpu.VMEM(wv.shape, BF16),
            pltpu.VMEM(ct.shape, BF16),
            pltpu.VMEM((ROWS * STEPS, dq.shape[2]), BF16),
            pltpu.VMEM((ROWS * STEPS, WIDTH), BF16),
            pltpu.VMEM(dq.shape, BF16),
            pltpu.VMEM(fresh.shape, BF16),
            pltpu.VMEM((ROWS * STEPS, dq.shape[2]), F32),
            pltpu.VMEM((ROWS * STEPS, WIDTH), F32),
            pltpu.VMEM(w.shape, BF16),
            pltpu.VMEM((BLOCK, HEADS * NOPE), BF16),
            pltpu.VMEM((ROWS * STEPS, HEADS * NOPE), BF16),
            pltpu.VMEM((HEADS * NOPE, LATENT), BF16),
            pltpu.VMEM((HEADS * NOPE, LATENT), BF16),
            pltpu.VMEM((HEADS, BLOCK, 256), BF16),
            pltpu.VMEM((HEADS * NOPE, 2 * BLOCK), BF16),
            pltpu.VMEM((HEADS * NOPE, 2 * BLOCK), BF16),
            pltpu.VMEM((HEADS, BLOCK, 128), F32),
            pltpu.VMEM((HEADS, BLOCK, 256), F32),
            pltpu.VMEM((lines, 640), BF16),
            pltpu.VMEM((lines, 640), BF16),
            pltpu.VMEM((lines, BLOCK), F32),
            pltpu.VMEM((lines, LATENT), F32),
            pltpu.VMEM((lines, LATENT), BF16),
            pltpu.VMEM((two, 640), BF16),
            pltpu.VMEM((N_CTX, two, BLOCK), F32),
            pltpu.VMEM((lines, LATENT), BF16),
            pltpu.VMEM((N_TP, 16, width // 4), BF16),
            pltpu.VMEM((N_TP, 16, width // 4), BF16),
            dma((8,)),
            dma((len(CHUNKS),)),
            dma((5, 2)),
            dma((5, 2)),
            dma((2, 4)),
            dma((2, 4)),
            dma((N_STATION + 1,)),
            dma((N_STATION + 1,)),
            dma((len(CHUNKS), N_TP)),
            dma((len(CHUNKS), N_TP)),
        ],
        compiler_params=pltpu.CompilerParams(collective_id=0, has_side_effects=True, vmem_limit_bytes=60 * MIB),
        name="latent_attention",
    )(lens, place, rlen, q, own, wk, wv, ct, dq, fresh, w)


def on_device(
    prefill_query,
    span_latent,
    prompt_lengths,
    key_weight,
    value_weight,
    placement,
    resident_cache,
    resident_lengths,
    decode_query,
    decode_latent,
    out_weight,
):
    cache_t = jnp.swapaxes(resident_cache, 1, 2).reshape(ROWS * WIDTH, BLOCK)
    return mega(
        prompt_lengths,
        placement,
        resident_lengths,
        prefill_query,
        span_latent.T,
        key_weight,
        value_weight,
        cache_t,
        decode_query,
        decode_latent,
        out_weight,
    )


def solution(mesh):
    placed = (
        P("ctx", "tp"),
        P("ctx", None),
        P(),
        P(None, "tp"),
        P(None, "tp"),
        P(),
        P("ctx", None, None),
        P("ctx"),
        P("ctx", None, "tp"),
        P("ctx", None, None),
        P("tp", None),
    )
    return jax.shard_map(
        on_device,
        mesh=mesh,
        in_specs=placed,
        out_specs=(P("ctx", "tp"), P(("ctx", "tp"), None, None)),
        check_vma=False,
    )
```

```python
import functools
import math

import jax
import jax.numpy as jnp
from jax import lax
from jax.experimental import pallas as pl
from jax.experimental.pallas import tpu as pltpu
from jax.sharding import PartitionSpec as P

MESH = pl.DeviceIdType.MESH
NOPE = 128
ROPE = 64
LATENT = 512
WIDTH = LATENT + ROPE
BLOCK = 256
N_CTX = 16
N_TP = 8
HEADS = 8
ROWS = 16
STEPS = 2
NREQ = 8
BIG = 1e30
FACTOR = math.log2(math.e) / math.sqrt(NOPE + ROPE)
F32 = jnp.float32
BF16 = jnp.bfloat16
MIB = 1 << 20
HALF = WIDTH // 2
QUARTER = WIDTH // 4
N_Z = 4
N_STATION = 7
FAR = (5, 6)
CHUNKS = (2048, 2048, 2048, 1024)


def mm(left, right):
    return lax.dot_general(left, right, (((1,), (0,)), ((), ())), preferred_element_type=F32)


def mm_nt(left, right):
    return lax.dot_general(left, right, (((1,), (1,)), ((), ())), preferred_element_type=F32)


def iota(shape, dim):
    return lax.broadcasted_iota(jnp.int32, shape, dim)


def request_table(lens_ref):
    starts, ends, total = [], [], jnp.int32(0)
    for j in range(NREQ):
        starts.append(total)
        total = total + lens_ref[j]
        ends.append(total)
    return starts, ends


def spread(index, values, other):
    out = jnp.full(index.shape, other, jnp.int32)
    for j, value in enumerate(values):
        out = jnp.where(index == j, value, out)
    return out


def prepare_weights(wk_ref, wv_ref, wkt, wvt):
    wkt[...] = wk_ref[...].T
    wvt[...] = wv_ref[...].T


def prepare_queries(me, q_ref, starts, ends, qs):
    lane = iota((BLOCK, 256), 1)
    pos = me * BLOCK + iota((BLOCK, 256), 0)
    for odd in range(2):
        slot = lane if odd else lane - 192
        first = spread(slot, starts, 1 << 30)
        last = spread(slot, ends, -1)
        hot = ((pos >= first) & (pos < last)).astype(F32)
        spare = lane < 64 if odd else lane >= 192
        for pair in range(HEADS // 2):
            base = pair * 384 + odd * 128
            window = q_ref[:, base : base + 256].astype(F32)
            qs[2 * pair + odd] = jnp.where(spare, hot, window).astype(BF16)


def latent_rows(g_ref, block, first, count):
    return g_ref[pl.ds(pl.multiple_of(block * WIDTH + first, 64), count), :]


def attend_pair(pair, causal, me, g_ref, starts, ends, wkt, wvt, qs, kt, vt, best, acc):
    ropes = []
    for half in range(2):
        lat = latent_rows(g_ref, 2 * pair + half, 0, LATENT)
        cols = slice(half * BLOCK, (half + 1) * BLOCK)
        kt[:, cols] = mm(wkt[...], lat).astype(BF16)
        vt[:, cols] = mm(wvt[...], lat).astype(BF16)
        ropes.append(latent_rows(g_ref, 2 * pair + half, LATENT, ROPE))
    rope = jnp.concatenate(ropes, axis=1)
    keys = 2 * BLOCK
    slot = iota((ROPE, keys), 0)
    key_pos = pair * keys + iota((ROPE, keys), 1)
    outside = (slot < NREQ) & ((key_pos < spread(slot, starts, 0)) | (key_pos >= spread(slot, ends, 0)))
    aug = jnp.where(outside, -BIG, 0.0).astype(BF16)
    ones = jnp.ones((NOPE, keys), BF16)
    for h in range(HEADS):
        head = slice(h * NOPE, (h + 1) * NOPE)
        parts = [aug, kt[head, :], rope] if h % 2 else [kt[head, :], rope, aug]
        s = mm(qs[h], jnp.concatenate(parts, axis=0))
        if causal:
            ahead = pair * keys + iota((BLOCK, keys), 1) > me * BLOCK + iota((BLOCK, keys), 0)
            s = jnp.where(ahead, -BIG, s)
        block_best = jnp.max(s, axis=1, keepdims=True) * FACTOR
        values = jnp.concatenate([vt[head, :], ones], axis=0)
        if causal:
            new_best = jnp.broadcast_to(block_best, (BLOCK, 128))
        else:
            new_best = jnp.maximum(best[h], block_best)
        p = jnp.exp2(s * FACTOR - jnp.concatenate([new_best] * 4, axis=1)).astype(BF16)
        gained = mm_nt(p, values)
        if causal:
            acc[h] = gained
        else:
            keep = jnp.exp2(best[h] - new_best)
            acc[h] = acc[h] * jnp.concatenate([keep] * 2, axis=1) + gained
        best[h] = new_best


def finish_prefill(acc, out_ref):
    for h in range(HEADS):
        out_ref[:, h * NOPE : (h + 1) * NOPE] = (acc[h][:, :NOPE] / acc[h][:, NOPE:]).astype(BF16)


def to_row_major(index):
    return (index % HEADS) * (ROWS * STEPS) + index // HEADS


def hot_matrix(condition):
    return condition.astype(F32).astype(BF16)


def pack_rows(rows_ref, wide_ref, flat_ref):
    for r in range(ROWS):
        wide_ref[r * STEPS : (r + 1) * STEPS, :] = rows_ref[r].astype(F32)
    flat_ref[...] = wide_ref[...].astype(BF16)


def decode_queries(dq_ref, wkt, qh, qr):
    rows = ROWS * STEPS
    eye = hot_matrix(iota((ROPE, 128), 0) == iota((ROPE, 128), 1))
    side = jnp.zeros((ROPE, 128), BF16)
    below = jnp.zeros((ROPE, LATENT), BF16)
    for h in range(HEADS):
        base = (h // 2) * 384 + (h % 2) * 128
        window = dq_ref[:, base : base + 256]
        weight = wkt[h * NOPE : (h + 1) * NOPE, :]
        lat = [below, weight, below] if h % 2 else [weight, below, below]
        rot = [side, side, side, eye] if h % 2 else [side, side, eye, side]
        qh[h * rows : (h + 1) * rows, :LATENT] = mm(window, jnp.concatenate(lat, axis=0)).astype(BF16)
        qh[h * rows : (h + 1) * rows, LATENT:] = mm(window, jnp.concatenate(rot, axis=0)).astype(BF16)
    count = rows * HEADS
    order = hot_matrix(to_row_major(iota((count, count), 0)) == iota((count, count), 1))
    qr[...] = mm(order, qh[...]).astype(BF16)


def scores_of(queries, lat, rope):
    return mm(queries[:, :LATENT], lat) + mm(queries[:, LATENT:WIDTH], rope)


def decode_resident(qr, ct_ref, fresh_ref, rlen_ref, sr, ar, lo):
    per = STEPS * HEADS
    for r in range(ROWS):
        rows = slice(r * per, (r + 1) * per)
        sr[rows, :] = scores_of(
            qr[rows, :], ct_ref[r * WIDTH : r * WIDTH + LATENT, :], ct_ref[r * WIDTH + LATENT : (r + 1) * WIDTH, :]
        )
    count = ROWS * per
    row_of = iota((count, BLOCK), 0) // per
    filled = spread(row_of, [rlen_ref[r] for r in range(ROWS)], 0)
    s = jnp.where(iota((count, BLOCK), 1) < filled, sr[...], -BIG) * FACTOR
    fs = mm_nt(qr[:, :LATENT], fresh_ref[:, :LATENT]) + mm_nt(qr[:, LATENT:WIDTH], fresh_ref[:, LATENT:])
    place, col = iota(fs.shape, 0), iota(fs.shape, 1)
    open_ = (place // per == col // STEPS) & (col % STEPS <= (place // HEADS) % STEPS)
    fs = jnp.where(open_, fs, -BIG) * FACTOR
    best = jnp.maximum(jnp.max(s, axis=1, keepdims=True), jnp.max(fs, axis=1, keepdims=True))
    w = jnp.exp2(s - best)
    fw = jnp.exp2(fs - best)
    total = jnp.sum(w, axis=1, keepdims=True) + jnp.sum(fw, axis=1, keepdims=True)
    sr[...] = w
    for r in range(ROWS):
        rows = slice(r * per, (r + 1) * per)
        ar[rows, :] = mm_nt(sr[rows, :].astype(BF16), ct_ref[r * WIDTH : r * WIDTH + LATENT, :])
    lo[...] = ((ar[...] + mm(fw.astype(BF16), fresh_ref[:, :LATENT])) / total).astype(BF16)


def slot_table(me, lens_ref, place_ref, starts):
    rank = jnp.int32(0)
    row = [jnp.int32(-1)] * 2
    first = [jnp.int32(0)] * 2
    length = [jnp.int32(0)] * 2
    for j in range(NREQ):
        there = place_ref[j] // ROWS == me
        for k in range(2):
            hit = there & (rank == k)
            row[k] = jnp.where(hit, place_ref[j] % ROWS, row[k])
            first[k] = jnp.where(hit, starts[j], first[k])
            length[k] = jnp.where(hit, lens_ref[j], length[k])
        rank = rank + there.astype(jnp.int32)
    return row, first, length


def slot_queries(table, qr, qs2):
    per = STEPS * HEADS
    shape = (2 * per, ROWS * per)
    place = iota(shape, 0)
    row = spread(place // per, table[0], -1)
    pick = hot_matrix((row >= 0) & (iota(shape, 1) == row * per + place % per))
    qs2[...] = mm(pick, qr[...]).astype(BF16)


def slot_scores(block, g_ref, qs2, ss):
    ss[block] = scores_of(qs2[...], latent_rows(g_ref, block, 0, LATENT), latent_rows(g_ref, block, LATENT, ROPE))


def decode_slots(table, g_ref, qs2, ss, fresh_ref, lo_ref, out_rows):
    per = STEPS * HEADS
    row, first, length = table
    lines = 2 * per
    slot = iota((lines, BLOCK), 0) // per
    low = spread(slot, first, 0)
    high = low + spread(slot, length, 0)
    fs = mm_nt(qs2[:, :LATENT], fresh_ref[:, :LATENT]) + mm_nt(qs2[:, LATENT:WIDTH], fresh_ref[:, LATENT:])
    place, col = iota(fs.shape, 0), iota(fs.shape, 1)
    open_ = (spread(place // per, row, -1) == col // STEPS) & (col % STEPS <= (place // HEADS) % STEPS)
    fs = jnp.where(open_, fs, -BIG) * FACTOR
    best = jnp.max(fs, axis=1, keepdims=True)
    peak = jnp.full((lines, BLOCK), -BIG, F32)
    for b in range(N_CTX):
        pos = b * BLOCK + iota((lines, BLOCK), 1)
        s = jnp.where((pos >= low) & (pos < high), ss[b] * FACTOR, -BIG)
        ss[b] = s
        peak = jnp.maximum(peak, s)
    best = jnp.maximum(best, jnp.max(peak, axis=1, keepdims=True))
    fw = jnp.exp2(fs - best)
    mass = jnp.zeros((lines, BLOCK), F32)
    total = mm(fw.astype(BF16), fresh_ref[:, :LATENT])
    for b in range(N_CTX):
        w = jnp.exp2(ss[b] - best)
        mass = mass + w
        total = total + mm_nt(w.astype(BF16), latent_rows(g_ref, b, 0, LATENT))
    weight = jnp.sum(mass, axis=1, keepdims=True) + jnp.sum(fw, axis=1, keepdims=True)
    slot_out = (total / weight).astype(BF16)
    shape = (ROWS * per, lines)
    back = iota(shape, 1)
    back_row = spread(back // per, row, -1)
    route = hot_matrix((back_row >= 0) & (iota(shape, 0) == back_row * per + back % per))
    spot = iota((ROWS * per, LATENT), 0) // per
    replaced = (spot == row[0]) | (spot == row[1])
    out_rows[...] = jnp.where(replaced, mm(route, slot_out), lo_ref[...].astype(F32)).astype(BF16)


def head_values(rows_ref, wv_ref, x_ref):
    rows = ROWS * STEPS
    count = rows * HEADS
    order = hot_matrix(iota((count, count), 0) == to_row_major(iota((count, count), 1)))
    lat = mm(order, rows_ref[...]).astype(BF16)
    for h in range(HEADS):
        head = slice(h * NOPE, (h + 1) * NOPE)
        x_ref[:, head] = mm(lat[h * rows : (h + 1) * rows, :], wv_ref[:, head]).astype(BF16)


def z_step(v):
    zz = v // 2
    return (zz * 3) % 5 - (zz // 3) * 2


class Place:
    def __init__(self):
        self.ctx = lax.axis_index("ctx")
        self.tp = lax.axis_index("tp")
        self.core = self.ctx % 2
        self.z = self.ctx // 4
        self.x_lo = (self.ctx // 2) % 2
        self.x = (self.tp // 4) * 2 + self.x_lo
        self.y = self.tp % 4

    def at(self, dz, dx, dy=0):
        z = (self.z + dz + N_Z) % N_Z
        x = (self.x + dx + 4) % 4
        y = (self.y + dy + 4) % 4
        return ((z * 2 + x % 2) * 2 + self.core, (x // 2) * 4 + y)

    def sibling(self):
        return (self.ctx + 1 - 2 * self.core, self.tp)

    def station_pair(self, station):
        v = station + 1
        return ((self.z + z_step(v) + N_Z) % N_Z) * 2 + (self.x_lo + v) % 2


def half_rows(g_ref, block, half):
    return g_ref.at[pl.ds(pl.multiple_of(block * WIDTH + half * HALF, 32), HALF)]


def quarter_rows(g_ref, block, quarter):
    return g_ref.at[pl.ds(pl.multiple_of(block * WIDTH + quarter * QUARTER, 16), QUARTER)]


def block_rows(g_ref, block):
    return g_ref.at[pl.ds(pl.multiple_of(block * WIDTH, 64), WIDTH)]


def mega_kernel(
    lens_ref,
    place_ref,
    rlen_ref,
    q_hbm,
    own_hbm,
    wk_hbm,
    wv_hbm,
    ct_hbm,
    dq_hbm,
    fresh_hbm,
    w_hbm,
    out_hbm,
    dec_ref,
    q_ref,
    g_ref,
    wk_ref,
    wv_ref,
    ct_ref,
    dq_ref,
    fresh_ref,
    dq3,
    fresh3,
    dq32,
    fresh32,
    w_ref,
    out_ref,
    x_ref,
    wkt,
    wvt,
    qs,
    kt,
    vt,
    best,
    acc,
    qh,
    qr,
    sr,
    ar,
    lo,
    qs2,
    ss,
    lo2,
    send,
    recv,
    load_sem,
    w_sem,
    link_send,
    link_recv,
    far_send,
    far_recv,
    core_send,
    core_recv,
    sum_send,
    sum_recv,
):
    at = Place()
    me, tp = at.ctx, at.tp
    barrier = pltpu.get_barrier_semaphore()
    peers = [at.sibling()]
    aside = 1 - 2 * (at.y % 2)
    peers += [at.at(1, 0), at.at(-1, 0), at.at(2, 0), at.at(0, -1), at.at(0, 1)]
    peers += [at.at(2, 1), at.at(2, -1)]
    peers += [(me, (tp + d) % N_TP) for d in range(1, N_TP)]
    for peer in peers:
        pl.semaphore_signal(barrier, inc=1, device_id=peer, device_id_type=MESH)

    pairs = [
        (wk_hbm, wk_ref),
        (wv_hbm, wv_ref),
        (dq_hbm, dq3),
        (fresh_hbm, fresh3),
        (ct_hbm, ct_ref),
        (q_hbm, q_ref),
        (own_hbm, block_rows(g_ref, me)),
    ]
    loads = [pltpu.make_async_copy(src, dst, load_sem.at[i]) for i, (src, dst) in enumerate(pairs)]
    for load in loads:
        load.start()
    pl.semaphore_wait(barrier, len(peers))

    sent = []

    def push(src, block, half, station, device):
        copy = pltpu.make_async_remote_copy(
            src_ref=src,
            dst_ref=half_rows(g_ref, block, half),
            send_sem=link_send.at[station, half],
            recv_sem=link_recv.at[station, half],
            device_id=device,
            device_id_type=MESH,
        )
        copy.start()
        sent.append(copy)

    def own_half(half):
        return own_hbm.at[half * HALF : (half + 1) * HALF]

    def push_quarter(src, block, quarter, which, step, device):
        copy = pltpu.make_async_remote_copy(
            src_ref=src,
            dst_ref=quarter_rows(g_ref, block, quarter),
            send_sem=far_send.at[which, step],
            recv_sem=far_recv.at[which, step],
            device_id=device,
            device_id_type=MESH,
        )
        copy.start()
        sent.append(copy)

    own_quarter = own_hbm.at[pl.ds(pl.multiple_of(at.y * QUARTER, 16), QUARTER)]
    for which, device in enumerate((at.at(2, 0), at.at(2, aside))):
        push_quarter(own_quarter, me, at.y, which, 0, device)
    for half in range(2):
        push(own_half(half), me, half, 0, at.at(0, 2 * half - 1))
    own_to_core = pltpu.make_async_remote_copy(
        src_ref=own_hbm,
        dst_ref=block_rows(g_ref, me),
        send_sem=core_send.at[N_STATION],
        recv_sem=core_recv.at[N_STATION],
        device_id=at.sibling(),
        device_id_type=MESH,
    )
    own_to_core.start()
    sent.append(own_to_core)

    def landed(station, half):
        block = 2 * at.station_pair(station) + at.core
        pltpu.make_async_copy(own_half(half), half_rows(g_ref, block, half), link_recv.at[station, half]).wait()

    def share_x(half):
        for station in (1, 3):
            landed(station, half)
            block = 2 * at.station_pair(station) + at.core
            push(half_rows(g_ref, block, half), block, half, station + 1, at.at(0, 2 * half - 1))

    def landed_quarter(which, step):
        block = 2 * at.station_pair(FAR[which]) + at.core
        quarter = (at.y - step + 4) % 4
        source = own_hbm.at[0:QUARTER]
        pltpu.make_async_copy(source, quarter_rows(g_ref, block, quarter), far_recv.at[which, step]).wait()

    def share_far(which):
        landed_quarter(which, 0)
        block = 2 * at.station_pair(FAR[which]) + at.core
        mine = quarter_rows(g_ref, block, at.y)
        for step in (1, 3, 2):
            push_quarter(mine, block, at.y, which, step, at.at(0, 0, step))

    def to_core(station):
        block = 2 * at.station_pair(station) + at.core
        copy = pltpu.make_async_remote_copy(
            src_ref=block_rows(g_ref, block),
            dst_ref=block_rows(g_ref, block),
            send_sem=core_send.at[station],
            recv_sem=core_recv.at[station],
            device_id=at.sibling(),
            device_id_type=MESH,
        )
        copy.start()
        sent.append(copy)

    def from_core(station, pair):
        block = 2 * pair + 1 - at.core
        pltpu.make_async_copy(own_hbm, block_rows(g_ref, block), core_recv.at[station]).wait()

    starts, ends = request_table(lens_ref)
    table = slot_table(me, lens_ref, place_ref, starts)
    loads[0].wait()
    loads[1].wait()
    prepare_weights(wk_ref, wv_ref, wkt, wvt)
    for half in range(2):
        push(own_half(half), me, half, 1, at.at(1, 0))
        push(own_half(half), me, half, 3, at.at(-1, 0))
    loads[2].wait()
    loads[3].wait()
    pack_rows(dq3, dq32, dq_ref)
    pack_rows(fresh3, fresh32, fresh_ref)
    decode_queries(dq_ref, wkt, qh, qr)
    slot_queries(table, qr, qs2)
    loads[5].wait()
    prepare_queries(me, q_ref, starts, ends, qs)
    step = functools.partial(
        attend_pair,
        me=me,
        g_ref=g_ref,
        starts=starts,
        ends=ends,
        wkt=wkt,
        wvt=wvt,
        qs=qs,
        kt=kt,
        vt=vt,
        best=best,
        acc=acc,
    )
    own = me // 2
    loads[6].wait()
    from_core(N_STATION, own)
    step(own, True)
    for half in range(2):
        slot_scores(2 * own + half, g_ref, qs2, ss)
    for which in range(2):
        share_far(which)
    loads[4].wait()
    w_loads = []
    first = 0
    for c, width in enumerate(CHUNKS):
        cols = slice(first, first + width)
        w_loads.append(pltpu.make_async_copy(w_hbm.at[:, cols], w_ref.at[:, cols], w_sem.at[c]))
        w_loads[-1].start()
        first += width
    decode_resident(qr, ct_ref, fresh_ref, rlen_ref, sr, ar, lo)
    for half in range(2):
        landed(0, half)
    to_core(0)
    share_x(0)
    share_x(1)
    to_core(1)
    to_core(3)

    def project():
        copies = []
        first = 0
        for c, width in enumerate(CHUNKS):
            quarter = width // 4
            q0 = first // 4
            w_loads[c].wait()
            part = mm(x_ref[...], w_ref[:, first : first + width])
            for p in range(N_TP):
                rows = part[4 * p : 4 * p + 4, :]
                piece = jnp.concatenate([rows[:, k * quarter : (k + 1) * quarter] for k in range(4)], axis=0)
                send[p, :, q0 : q0 + quarter] = piece.astype(BF16)
            for d in range(1, N_TP):
                peer = (tp + d) % N_TP
                copy = pltpu.make_async_remote_copy(
                    src_ref=send.at[peer, :, q0 : q0 + quarter],
                    dst_ref=recv.at[d, :, q0 : q0 + quarter],
                    send_sem=sum_send.at[c, d],
                    recv_sem=sum_recv.at[c, d],
                    device_id=(me, peer),
                    device_id_type=MESH,
                )
                copy.start()
                copies.append((c, d, copy))
            first += width
        return copies

    def near(station):
        pair = at.station_pair(station)
        from_core(station, pair)

        @pl.when((pair < own) & (pair >= own - 5))
        def _():
            step(pair, False)

    @pl.loop(0, 2)
    def _(station):
        near(station)

    for station in (2, 4):
        for half in range(2):
            landed(station, half)
        to_core(station)
    for which in range(2):
        for step_y in range(1, 4):
            landed_quarter(which, step_y)
        to_core(FAR[which])
    near(2)
    for station in range(3):
        for half in range(2):
            slot_scores(2 * at.station_pair(station) + half, g_ref, qs2, ss)
    for station in (3, 4, 5, 6):
        from_core(station, at.station_pair(station))

    for station in (3, 4, 5, 6):
        for half in range(2):
            slot_scores(2 * at.station_pair(station) + half, g_ref, qs2, ss)
    decode_slots(table, g_ref, qs2, ss, fresh_ref, lo, lo2)
    head_values(lo2, wv_ref, x_ref)
    sums = project()

    @pl.loop(4, N_STATION)
    def _(station):
        pair = at.station_pair(station)

        @pl.when((pair < own) & (pair >= own - 5))
        def _():
            step(pair, False)

    finish_prefill(acc, out_ref)
    store = pltpu.make_async_copy(out_ref, out_hbm, load_sem.at[len(pairs)])
    store.start()

    first = 0
    for c, width in enumerate(CHUNKS):
        quarter = width // 4
        q0 = first // 4
        total = send[tp, :, q0 : q0 + quarter].astype(F32)
        for c2, d, copy in sums:
            if c2 == c:
                copy.wait_recv()
                total = total + recv[d, :, q0 : q0 + quarter].astype(F32)
        for k in range(4):
            for row in range(2):
                piece = total[4 * k + 2 * row : 4 * k + 2 * row + 2, :]
                dec_ref[row, :, first + k * quarter : first + (k + 1) * quarter] = piece.astype(BF16)
        first += width
    for _, _, copy in sums:
        copy.wait_send()
    for copy in sent:
        copy.wait_send()
    store.wait()


def mega(lens, place, rlen, q, own, wk, wv, ct, dq, fresh, w):
    smem = pl.BlockSpec(memory_space=pltpu.SMEM)
    vmem = pl.BlockSpec(memory_space=pltpu.VMEM)
    far = pl.BlockSpec(memory_space=pl.ANY)
    lines = ROWS * STEPS * HEADS
    two = 2 * STEPS * HEADS
    width = w.shape[1]
    dma = pltpu.SemaphoreType.DMA
    return pl.pallas_call(
        mega_kernel,
        out_shape=(
            jax.ShapeDtypeStruct((BLOCK, HEADS * NOPE), BF16),
            jax.ShapeDtypeStruct((2, STEPS, width), BF16),
        ),
        in_specs=[smem] * 3 + [far] * 8,
        out_specs=(far, vmem),
        scratch_shapes=[
            pltpu.VMEM(q.shape, BF16),
            pltpu.VMEM((N_CTX * WIDTH, BLOCK), BF16),
            pltpu.VMEM(wk.shape, BF16),
            pltpu.VMEM(wv.shape, BF16),
            pltpu.VMEM(ct.shape, BF16),
            pltpu.VMEM((ROWS * STEPS, dq.shape[2]), BF16),
            pltpu.VMEM((ROWS * STEPS, WIDTH), BF16),
            pltpu.VMEM(dq.shape, BF16),
            pltpu.VMEM(fresh.shape, BF16),
            pltpu.VMEM((ROWS * STEPS, dq.shape[2]), F32),
            pltpu.VMEM((ROWS * STEPS, WIDTH), F32),
            pltpu.VMEM(w.shape, BF16),
            pltpu.VMEM((BLOCK, HEADS * NOPE), BF16),
            pltpu.VMEM((ROWS * STEPS, HEADS * NOPE), BF16),
            pltpu.VMEM((HEADS * NOPE, LATENT), BF16),
            pltpu.VMEM((HEADS * NOPE, LATENT), BF16),
            pltpu.VMEM((HEADS, BLOCK, 256), BF16),
            pltpu.VMEM((HEADS * NOPE, 2 * BLOCK), BF16),
            pltpu.VMEM((HEADS * NOPE, 2 * BLOCK), BF16),
            pltpu.VMEM((HEADS, BLOCK, 128), F32),
            pltpu.VMEM((HEADS, BLOCK, 256), F32),
            pltpu.VMEM((lines, 640), BF16),
            pltpu.VMEM((lines, 640), BF16),
            pltpu.VMEM((lines, BLOCK), F32),
            pltpu.VMEM((lines, LATENT), F32),
            pltpu.VMEM((lines, LATENT), BF16),
            pltpu.VMEM((two, 640), BF16),
            pltpu.VMEM((N_CTX, two, BLOCK), F32),
            pltpu.VMEM((lines, LATENT), BF16),
            pltpu.VMEM((N_TP, 16, width // 4), BF16),
            pltpu.VMEM((N_TP, 16, width // 4), BF16),
            dma((8,)),
            dma((len(CHUNKS),)),
            dma((5, 2)),
            dma((5, 2)),
            dma((2, 4)),
            dma((2, 4)),
            dma((N_STATION + 1,)),
            dma((N_STATION + 1,)),
            dma((len(CHUNKS), N_TP)),
            dma((len(CHUNKS), N_TP)),
        ],
        compiler_params=pltpu.CompilerParams(collective_id=0, has_side_effects=True, vmem_limit_bytes=60 * MIB),
        name="latent_attention",
    )(lens, place, rlen, q, own, wk, wv, ct, dq, fresh, w)


def on_device(
    prefill_query,
    span_latent,
    prompt_lengths,
    key_weight,
    value_weight,
    placement,
    resident_cache,
    resident_lengths,
    decode_query,
    decode_latent,
    out_weight,
):
    cache_t = jnp.swapaxes(resident_cache, 1, 2).reshape(ROWS * WIDTH, BLOCK)
    return mega(
        prompt_lengths,
        placement,
        resident_lengths,
        prefill_query,
        span_latent.T,
        key_weight,
        value_weight,
        cache_t,
        decode_query,
        decode_latent,
        out_weight,
    )


def solution(mesh):
    placed = (
        P("ctx", "tp"),
        P("ctx", None),
        P(),
        P(None, "tp"),
        P(None, "tp"),
        P(),
        P("ctx", None, None),
        P("ctx"),
        P("ctx", None, "tp"),
        P("ctx", None, None),
        P("tp", None),
    )
    return jax.shard_map(
        on_device,
        mesh=mesh,
        in_specs=placed,
        out_specs=(P("ctx", "tp"), P(("ctx", "tp"), None, None)),
        check_vma=False,
    )
```

```python
import functools
import math

import jax
import jax.numpy as jnp
from jax import lax
from jax.experimental import pallas as pl
from jax.experimental.pallas import tpu as pltpu
from jax.sharding import PartitionSpec as P

MESH = pl.DeviceIdType.MESH
NOPE = 128
ROPE = 64
LATENT = 512
WIDTH = LATENT + ROPE
BLOCK = 256
N_CTX = 16
N_TP = 8
HEADS = 8
ROWS = 16
STEPS = 2
NREQ = 8
BIG = 1e30
FACTOR = math.log2(math.e) / math.sqrt(NOPE + ROPE)
F32 = jnp.float32
BF16 = jnp.bfloat16
MIB = 1 << 20
HALF = WIDTH // 2
QUARTER = WIDTH // 4
N_Z = 4
N_STATION = 7
FAR = (5, 6)
CHUNKS = (2048, 2048, 2048, 1024)


def mm(left, right):
    return lax.dot_general(left, right, (((1,), (0,)), ((), ())), preferred_element_type=F32)


def mm_nt(left, right):
    return lax.dot_general(left, right, (((1,), (1,)), ((), ())), preferred_element_type=F32)


def iota(shape, dim):
    return lax.broadcasted_iota(jnp.int32, shape, dim)


def request_table(lens_ref):
    starts, ends, total = [], [], jnp.int32(0)
    for j in range(NREQ):
        starts.append(total)
        total = total + lens_ref[j]
        ends.append(total)
    return starts, ends


def spread(index, values, other):
    out = jnp.full(index.shape, other, jnp.int32)
    for j, value in enumerate(values):
        out = jnp.where(index == j, value, out)
    return out


def prepare_weights(wk_ref, wv_ref, wkt, wvt):
    wkt[...] = wk_ref[...].T
    wvt[...] = wv_ref[...].T


def prepare_queries(me, q_ref, starts, ends, qs):
    lane = iota((BLOCK, 256), 1)
    pos = me * BLOCK + iota((BLOCK, 256), 0)
    for odd in range(2):
        slot = lane if odd else lane - 192
        first = spread(slot, starts, 1 << 30)
        last = spread(slot, ends, -1)
        hot = ((pos >= first) & (pos < last)).astype(F32)
        spare = lane < 64 if odd else lane >= 192
        for pair in range(HEADS // 2):
            base = pair * 384 + odd * 128
            window = q_ref[:, base : base + 256].astype(F32)
            qs[2 * pair + odd] = jnp.where(spare, hot, window).astype(BF16)


def latent_rows(g_ref, block, first, count):
    return g_ref[pl.ds(pl.multiple_of(block * WIDTH + first, 64), count), :]


def attend_pair(pair, causal, me, g_ref, starts, ends, wkt, wvt, qs, kt, vt, best, acc):
    ropes = []
    for half in range(2):
        lat = latent_rows(g_ref, 2 * pair + half, 0, LATENT)
        cols = slice(half * BLOCK, (half + 1) * BLOCK)
        kt[:, cols] = mm(wkt[...], lat).astype(BF16)
        vt[:, cols] = mm(wvt[...], lat).astype(BF16)
        ropes.append(latent_rows(g_ref, 2 * pair + half, LATENT, ROPE))
    rope = jnp.concatenate(ropes, axis=1)
    keys = 2 * BLOCK
    slot = iota((ROPE, keys), 0)
    key_pos = pair * keys + iota((ROPE, keys), 1)
    outside = (slot < NREQ) & ((key_pos < spread(slot, starts, 0)) | (key_pos >= spread(slot, ends, 0)))
    aug = jnp.where(outside, -BIG, 0.0).astype(BF16)
    ones = jnp.ones((NOPE, keys), BF16)
    for h in range(HEADS):
        head = slice(h * NOPE, (h + 1) * NOPE)
        parts = [aug, kt[head, :], rope] if h % 2 else [kt[head, :], rope, aug]
        s = mm(qs[h], jnp.concatenate(parts, axis=0))
        if causal:
            ahead = pair * keys + iota((BLOCK, keys), 1) > me * BLOCK + iota((BLOCK, keys), 0)
            s = jnp.where(ahead, -BIG, s)
        block_best = jnp.max(s, axis=1, keepdims=True) * FACTOR
        values = jnp.concatenate([vt[head, :], ones], axis=0)
        if causal:
            new_best = jnp.broadcast_to(block_best, (BLOCK, 128))
        else:
            new_best = jnp.maximum(best[h], block_best)
        p = jnp.exp2(s * FACTOR - jnp.concatenate([new_best] * 4, axis=1)).astype(BF16)
        gained = mm_nt(p, values)
        if causal:
            acc[h] = gained
        else:
            keep = jnp.exp2(best[h] - new_best)
            acc[h] = acc[h] * jnp.concatenate([keep] * 2, axis=1) + gained
        best[h] = new_best


def finish_prefill(acc, out_ref):
    for h in range(HEADS):
        out_ref[:, h * NOPE : (h + 1) * NOPE] = (acc[h][:, :NOPE] / acc[h][:, NOPE:]).astype(BF16)


def to_row_major(index):
    return (index % HEADS) * (ROWS * STEPS) + index // HEADS


def hot_matrix(condition):
    return condition.astype(F32).astype(BF16)


def pack_rows(rows_ref, wide_ref, flat_ref):
    for r in range(ROWS):
        wide_ref[r * STEPS : (r + 1) * STEPS, :] = rows_ref[r].astype(F32)
    flat_ref[...] = wide_ref[...].astype(BF16)


def decode_queries(dq_ref, wkt, qh, qr):
    rows = ROWS * STEPS
    eye = hot_matrix(iota((ROPE, 128), 0) == iota((ROPE, 128), 1))
    side = jnp.zeros((ROPE, 128), BF16)
    below = jnp.zeros((ROPE, LATENT), BF16)
    for h in range(HEADS):
        base = (h // 2) * 384 + (h % 2) * 128
        window = dq_ref[:, base : base + 256]
        weight = wkt[h * NOPE : (h + 1) * NOPE, :]
        lat = [below, weight, below] if h % 2 else [weight, below, below]
        rot = [side, side, side, eye] if h % 2 else [side, side, eye, side]
        qh[h * rows : (h + 1) * rows, :LATENT] = mm(window, jnp.concatenate(lat, axis=0)).astype(BF16)
        qh[h * rows : (h + 1) * rows, LATENT:] = mm(window, jnp.concatenate(rot, axis=0)).astype(BF16)
    count = rows * HEADS
    order = hot_matrix(to_row_major(iota((count, count), 0)) == iota((count, count), 1))
    qr[...] = mm(order, qh[...]).astype(BF16)


def scores_of(queries, lat, rope):
    return mm(queries[:, :LATENT], lat) + mm(queries[:, LATENT:WIDTH], rope)


def decode_resident(qr, ct_ref, fresh_ref, rlen_ref, sr, ar, lo):
    per = STEPS * HEADS
    for r in range(ROWS):
        rows = slice(r * per, (r + 1) * per)
        sr[rows, :] = scores_of(
            qr[rows, :], ct_ref[r * WIDTH : r * WIDTH + LATENT, :], ct_ref[r * WIDTH + LATENT : (r + 1) * WIDTH, :]
        )
    count = ROWS * per
    row_of = iota((count, BLOCK), 0) // per
    filled = spread(row_of, [rlen_ref[r] for r in range(ROWS)], 0)
    s = jnp.where(iota((count, BLOCK), 1) < filled, sr[...], -BIG) * FACTOR
    fs = mm_nt(qr[:, :LATENT], fresh_ref[:, :LATENT]) + mm_nt(qr[:, LATENT:WIDTH], fresh_ref[:, LATENT:])
    place, col = iota(fs.shape, 0), iota(fs.shape, 1)
    open_ = (place // per == col // STEPS) & (col % STEPS <= (place // HEADS) % STEPS)
    fs = jnp.where(open_, fs, -BIG) * FACTOR
    best = jnp.maximum(jnp.max(s, axis=1, keepdims=True), jnp.max(fs, axis=1, keepdims=True))
    w = jnp.exp2(s - best)
    fw = jnp.exp2(fs - best)
    total = jnp.sum(w, axis=1, keepdims=True) + jnp.sum(fw, axis=1, keepdims=True)
    sr[...] = w
    for r in range(ROWS):
        rows = slice(r * per, (r + 1) * per)
        ar[rows, :] = mm_nt(sr[rows, :].astype(BF16), ct_ref[r * WIDTH : r * WIDTH + LATENT, :])
    lo[...] = ((ar[...] + mm(fw.astype(BF16), fresh_ref[:, :LATENT])) / total).astype(BF16)


def slot_table(me, lens_ref, place_ref, starts):
    rank = jnp.int32(0)
    row = [jnp.int32(-1)] * 2
    first = [jnp.int32(0)] * 2
    length = [jnp.int32(0)] * 2
    for j in range(NREQ):
        there = place_ref[j] // ROWS == me
        for k in range(2):
            hit = there & (rank == k)
            row[k] = jnp.where(hit, place_ref[j] % ROWS, row[k])
            first[k] = jnp.where(hit, starts[j], first[k])
            length[k] = jnp.where(hit, lens_ref[j], length[k])
        rank = rank + there.astype(jnp.int32)
    return row, first, length


def slot_queries(table, qr, qs2):
    per = STEPS * HEADS
    shape = (2 * per, ROWS * per)
    place = iota(shape, 0)
    row = spread(place // per, table[0], -1)
    pick = hot_matrix((row >= 0) & (iota(shape, 1) == row * per + place % per))
    qs2[...] = mm(pick, qr[...]).astype(BF16)


def slot_scores(block, g_ref, qs2, ss):
    ss[block] = scores_of(qs2[...], latent_rows(g_ref, block, 0, LATENT), latent_rows(g_ref, block, LATENT, ROPE))


def decode_slots(table, g_ref, qs2, ss, fresh_ref, lo_ref, out_rows):
    per = STEPS * HEADS
    row, first, length = table
    lines = 2 * per
    slot = iota((lines, BLOCK), 0) // per
    low = spread(slot, first, 0)
    high = low + spread(slot, length, 0)
    fs = mm_nt(qs2[:, :LATENT], fresh_ref[:, :LATENT]) + mm_nt(qs2[:, LATENT:WIDTH], fresh_ref[:, LATENT:])
    place, col = iota(fs.shape, 0), iota(fs.shape, 1)
    open_ = (spread(place // per, row, -1) == col // STEPS) & (col % STEPS <= (place // HEADS) % STEPS)
    fs = jnp.where(open_, fs, -BIG) * FACTOR
    best = jnp.max(fs, axis=1, keepdims=True)
    peak = jnp.full((lines, BLOCK), -BIG, F32)
    for b in range(N_CTX):
        pos = b * BLOCK + iota((lines, BLOCK), 1)
        s = jnp.where((pos >= low) & (pos < high), ss[b] * FACTOR, -BIG)
        ss[b] = s
        peak = jnp.maximum(peak, s)
    best = jnp.maximum(best, jnp.max(peak, axis=1, keepdims=True))
    fw = jnp.exp2(fs - best)
    mass = jnp.zeros((lines, BLOCK), F32)
    total = mm(fw.astype(BF16), fresh_ref[:, :LATENT])
    for b in range(N_CTX):
        w = jnp.exp2(ss[b] - best)
        mass = mass + w
        total = total + mm_nt(w.astype(BF16), latent_rows(g_ref, b, 0, LATENT))
    weight = jnp.sum(mass, axis=1, keepdims=True) + jnp.sum(fw, axis=1, keepdims=True)
    slot_out = (total / weight).astype(BF16)
    shape = (ROWS * per, lines)
    back = iota(shape, 1)
    back_row = spread(back // per, row, -1)
    route = hot_matrix((back_row >= 0) & (iota(shape, 0) == back_row * per + back % per))
    spot = iota((ROWS * per, LATENT), 0) // per
    replaced = (spot == row[0]) | (spot == row[1])
    out_rows[...] = jnp.where(replaced, mm(route, slot_out), lo_ref[...].astype(F32)).astype(BF16)


def head_values(rows_ref, wv_ref, x_ref):
    rows = ROWS * STEPS
    count = rows * HEADS
    order = hot_matrix(iota((count, count), 0) == to_row_major(iota((count, count), 1)))
    lat = mm(order, rows_ref[...]).astype(BF16)
    for h in range(HEADS):
        head = slice(h * NOPE, (h + 1) * NOPE)
        x_ref[:, head] = mm(lat[h * rows : (h + 1) * rows, :], wv_ref[:, head]).astype(BF16)


def z_step(v):
    zz = v // 2
    return (zz * 3) % 5 - (zz // 3) * 2


class Place:
    def __init__(self):
        self.ctx = lax.axis_index("ctx")
        self.tp = lax.axis_index("tp")
        self.core = self.ctx % 2
        self.z = self.ctx // 4
        self.x_lo = (self.ctx // 2) % 2
        self.x = (self.tp // 4) * 2 + self.x_lo
        self.y = self.tp % 4

    def at(self, dz, dx, dy=0):
        z = (self.z + dz + N_Z) % N_Z
        x = (self.x + dx + 4) % 4
        y = (self.y + dy + 4) % 4
        return ((z * 2 + x % 2) * 2 + self.core, (x // 2) * 4 + y)

    def sibling(self):
        return (self.ctx + 1 - 2 * self.core, self.tp)

    def station_pair(self, station):
        v = station + 1
        return ((self.z + z_step(v) + N_Z) % N_Z) * 2 + (self.x_lo + v) % 2


def half_rows(g_ref, block, half):
    return g_ref.at[pl.ds(pl.multiple_of(block * WIDTH + half * HALF, 32), HALF)]


def quarter_rows(g_ref, block, quarter):
    return g_ref.at[pl.ds(pl.multiple_of(block * WIDTH + quarter * QUARTER, 16), QUARTER)]


def block_rows(g_ref, block):
    return g_ref.at[pl.ds(pl.multiple_of(block * WIDTH, 64), WIDTH)]


def mega_kernel(
    lens_ref,
    place_ref,
    rlen_ref,
    q_hbm,
    own_hbm,
    wk_hbm,
    wv_hbm,
    ct_hbm,
    dq_hbm,
    fresh_hbm,
    w_hbm,
    out_hbm,
    dec_ref,
    q_ref,
    g_ref,
    wk_ref,
    wv_ref,
    ct_ref,
    dq_ref,
    fresh_ref,
    dq3,
    fresh3,
    dq32,
    fresh32,
    w_ref,
    out_ref,
    x_ref,
    wkt,
    wvt,
    qs,
    kt,
    vt,
    best,
    acc,
    qh,
    qr,
    sr,
    ar,
    lo,
    qs2,
    ss,
    lo2,
    send,
    recv,
    load_sem,
    w_sem,
    link_send,
    link_recv,
    far_send,
    far_recv,
    core_send,
    core_recv,
    sum_send,
    sum_recv,
):
    at = Place()
    me, tp = at.ctx, at.tp
    barrier = pltpu.get_barrier_semaphore()
    peers = [at.sibling()]
    aside = 1 - 2 * (at.y % 2)
    peers += [at.at(1, 0), at.at(-1, 0), at.at(2, 0), at.at(0, -1), at.at(0, 1)]
    peers += [at.at(2, 1), at.at(2, -1)]
    peers += [(me, (tp + d) % N_TP) for d in range(1, N_TP)]
    for peer in peers:
        pl.semaphore_signal(barrier, inc=1, device_id=peer, device_id_type=MESH)

    pairs = [
        (wk_hbm, wk_ref),
        (wv_hbm, wv_ref),
        (dq_hbm, dq3),
        (fresh_hbm, fresh3),
        (ct_hbm, ct_ref),
        (q_hbm, q_ref),
        (own_hbm, block_rows(g_ref, me)),
    ]
    loads = [pltpu.make_async_copy(src, dst, load_sem.at[i]) for i, (src, dst) in enumerate(pairs)]
    for load in loads:
        load.start()
    pl.semaphore_wait(barrier, len(peers))

    sent = []

    def push(src, block, half, station, device):
        copy = pltpu.make_async_remote_copy(
            src_ref=src,
            dst_ref=half_rows(g_ref, block, half),
            send_sem=link_send.at[station, half],
            recv_sem=link_recv.at[station, half],
            device_id=device,
            device_id_type=MESH,
        )
        copy.start()
        sent.append(copy)

    def own_half(half):
        return own_hbm.at[half * HALF : (half + 1) * HALF]

    def push_quarter(src, block, quarter, which, step, device):
        copy = pltpu.make_async_remote_copy(
            src_ref=src,
            dst_ref=quarter_rows(g_ref, block, quarter),
            send_sem=far_send.at[which, step],
            recv_sem=far_recv.at[which, step],
            device_id=device,
            device_id_type=MESH,
        )
        copy.start()
        sent.append(copy)

    own_quarter = own_hbm.at[pl.ds(pl.multiple_of(at.y * QUARTER, 16), QUARTER)]
    for which, device in enumerate((at.at(2, 0), at.at(2, aside))):
        push_quarter(own_quarter, me, at.y, which, 0, device)
    for half in range(2):
        push(own_half(half), me, half, 1, at.at(1, 0))
        push(own_half(half), me, half, 3, at.at(-1, 0))
        push(own_half(half), me, half, 0, at.at(0, 2 * half - 1))
    own_to_core = pltpu.make_async_remote_copy(
        src_ref=own_hbm,
        dst_ref=block_rows(g_ref, me),
        send_sem=core_send.at[N_STATION],
        recv_sem=core_recv.at[N_STATION],
        device_id=at.sibling(),
        device_id_type=MESH,
    )
    own_to_core.start()
    sent.append(own_to_core)

    def landed(station, half):
        block = 2 * at.station_pair(station) + at.core
        pltpu.make_async_copy(own_half(half), half_rows(g_ref, block, half), link_recv.at[station, half]).wait()

    def share_x(half):
        for station in (1, 3):
            landed(station, half)
            block = 2 * at.station_pair(station) + at.core
            push(half_rows(g_ref, block, half), block, half, station + 1, at.at(0, 2 * half - 1))

    def landed_quarter(which, step):
        block = 2 * at.station_pair(FAR[which]) + at.core
        quarter = (at.y - step + 4) % 4
        source = own_hbm.at[0:QUARTER]
        pltpu.make_async_copy(source, quarter_rows(g_ref, block, quarter), far_recv.at[which, step]).wait()

    def share_far(which):
        landed_quarter(which, 0)
        block = 2 * at.station_pair(FAR[which]) + at.core
        mine = quarter_rows(g_ref, block, at.y)
        for step in (1, 3, 2):
            push_quarter(mine, block, at.y, which, step, at.at(0, 0, step))

    def to_core(station):
        block = 2 * at.station_pair(station) + at.core
        copy = pltpu.make_async_remote_copy(
            src_ref=block_rows(g_ref, block),
            dst_ref=block_rows(g_ref, block),
            send_sem=core_send.at[station],
            recv_sem=core_recv.at[station],
            device_id=at.sibling(),
            device_id_type=MESH,
        )
        copy.start()
        sent.append(copy)

    def from_core(station, pair):
        block = 2 * pair + 1 - at.core
        pltpu.make_async_copy(own_hbm, block_rows(g_ref, block), core_recv.at[station]).wait()

    starts, ends = request_table(lens_ref)
    table = slot_table(me, lens_ref, place_ref, starts)
    loads[0].wait()
    loads[1].wait()
    prepare_weights(wk_ref, wv_ref, wkt, wvt)
    loads[2].wait()
    loads[3].wait()
    pack_rows(dq3, dq32, dq_ref)
    pack_rows(fresh3, fresh32, fresh_ref)
    decode_queries(dq_ref, wkt, qh, qr)
    slot_queries(table, qr, qs2)
    loads[5].wait()
    prepare_queries(me, q_ref, starts, ends, qs)
    step = functools.partial(
        attend_pair,
        me=me,
        g_ref=g_ref,
        starts=starts,
        ends=ends,
        wkt=wkt,
        wvt=wvt,
        qs=qs,
        kt=kt,
        vt=vt,
        best=best,
        acc=acc,
    )
    own = me // 2
    loads[6].wait()
    from_core(N_STATION, own)
    step(own, True)
    for half in range(2):
        slot_scores(2 * own + half, g_ref, qs2, ss)
    for which in range(2):
        share_far(which)
    loads[4].wait()
    w_loads = []
    first = 0
    for c, width in enumerate(CHUNKS):
        cols = slice(first, first + width)
        w_loads.append(pltpu.make_async_copy(w_hbm.at[:, cols], w_ref.at[:, cols], w_sem.at[c]))
        w_loads[-1].start()
        first += width
    decode_resident(qr, ct_ref, fresh_ref, rlen_ref, sr, ar, lo)
    for half in range(2):
        landed(0, half)
    to_core(0)
    share_x(0)
    share_x(1)
    to_core(1)
    to_core(3)

    def project():
        copies = []
        first = 0
        for c, width in enumerate(CHUNKS):
            quarter = width // 4
            q0 = first // 4
            w_loads[c].wait()
            part = mm(x_ref[...], w_ref[:, first : first + width])
            for p in range(N_TP):
                rows = part[4 * p : 4 * p + 4, :]
                piece = jnp.concatenate([rows[:, k * quarter : (k + 1) * quarter] for k in range(4)], axis=0)
                send[p, :, q0 : q0 + quarter] = piece.astype(BF16)
            for d in range(1, N_TP):
                peer = (tp + d) % N_TP
                copy = pltpu.make_async_remote_copy(
                    src_ref=send.at[peer, :, q0 : q0 + quarter],
                    dst_ref=recv.at[d, :, q0 : q0 + quarter],
                    send_sem=sum_send.at[c, d],
                    recv_sem=sum_recv.at[c, d],
                    device_id=(me, peer),
                    device_id_type=MESH,
                )
                copy.start()
                copies.append((c, d, copy))
            first += width
        return copies

    def near(station):
        pair = at.station_pair(station)
        from_core(station, pair)

        @pl.when((pair < own) & (pair >= own - 5))
        def _():
            step(pair, False)

    @pl.loop(0, 2)
    def _(station):
        near(station)

    for station in (2, 4):
        for half in range(2):
            landed(station, half)
        to_core(station)
    for which in range(2):
        for step_y in range(1, 4):
            landed_quarter(which, step_y)
        to_core(FAR[which])
    near(2)
    for station in range(3):
        for half in range(2):
            slot_scores(2 * at.station_pair(station) + half, g_ref, qs2, ss)
    for station in (3, 4, 5, 6):
        from_core(station, at.station_pair(station))

    for station in (3, 4, 5, 6):
        for half in range(2):
            slot_scores(2 * at.station_pair(station) + half, g_ref, qs2, ss)
    decode_slots(table, g_ref, qs2, ss, fresh_ref, lo, lo2)
    head_values(lo2, wv_ref, x_ref)
    sums = project()

    @pl.loop(4, N_STATION)
    def _(station):
        pair = at.station_pair(station)

        @pl.when((pair < own) & (pair >= own - 5))
        def _():
            step(pair, False)

    finish_prefill(acc, out_ref)
    store = pltpu.make_async_copy(out_ref, out_hbm, load_sem.at[len(pairs)])
    store.start()

    first = 0
    for c, width in enumerate(CHUNKS):
        quarter = width // 4
        q0 = first // 4
        total = send[tp, :, q0 : q0 + quarter].astype(F32)
        for c2, d, copy in sums:
            if c2 == c:
                copy.wait_recv()
                total = total + recv[d, :, q0 : q0 + quarter].astype(F32)
        for k in range(4):
            for row in range(2):
                piece = total[4 * k + 2 * row : 4 * k + 2 * row + 2, :]
                dec_ref[row, :, first + k * quarter : first + (k + 1) * quarter] = piece.astype(BF16)
        first += width
    for _, _, copy in sums:
        copy.wait_send()
    for copy in sent:
        copy.wait_send()
    store.wait()


def mega(lens, place, rlen, q, own, wk, wv, ct, dq, fresh, w):
    smem = pl.BlockSpec(memory_space=pltpu.SMEM)
    vmem = pl.BlockSpec(memory_space=pltpu.VMEM)
    far = pl.BlockSpec(memory_space=pl.ANY)
    lines = ROWS * STEPS * HEADS
    two = 2 * STEPS * HEADS
    width = w.shape[1]
    dma = pltpu.SemaphoreType.DMA
    return pl.pallas_call(
        mega_kernel,
        out_shape=(
            jax.ShapeDtypeStruct((BLOCK, HEADS * NOPE), BF16),
            jax.ShapeDtypeStruct((2, STEPS, width), BF16),
        ),
        in_specs=[smem] * 3 + [far] * 8,
        out_specs=(far, vmem),
        scratch_shapes=[
            pltpu.VMEM(q.shape, BF16),
            pltpu.VMEM((N_CTX * WIDTH, BLOCK), BF16),
            pltpu.VMEM(wk.shape, BF16),
            pltpu.VMEM(wv.shape, BF16),
            pltpu.VMEM(ct.shape, BF16),
            pltpu.VMEM((ROWS * STEPS, dq.shape[2]), BF16),
            pltpu.VMEM((ROWS * STEPS, WIDTH), BF16),
            pltpu.VMEM(dq.shape, BF16),
            pltpu.VMEM(fresh.shape, BF16),
            pltpu.VMEM((ROWS * STEPS, dq.shape[2]), F32),
            pltpu.VMEM((ROWS * STEPS, WIDTH), F32),
            pltpu.VMEM(w.shape, BF16),
            pltpu.VMEM((BLOCK, HEADS * NOPE), BF16),
            pltpu.VMEM((ROWS * STEPS, HEADS * NOPE), BF16),
            pltpu.VMEM((HEADS * NOPE, LATENT), BF16),
            pltpu.VMEM((HEADS * NOPE, LATENT), BF16),
            pltpu.VMEM((HEADS, BLOCK, 256), BF16),
            pltpu.VMEM((HEADS * NOPE, 2 * BLOCK), BF16),
            pltpu.VMEM((HEADS * NOPE, 2 * BLOCK), BF16),
            pltpu.VMEM((HEADS, BLOCK, 128), F32),
            pltpu.VMEM((HEADS, BLOCK, 256), F32),
            pltpu.VMEM((lines, 640), BF16),
            pltpu.VMEM((lines, 640), BF16),
            pltpu.VMEM((lines, BLOCK), F32),
            pltpu.VMEM((lines, LATENT), F32),
            pltpu.VMEM((lines, LATENT), BF16),
            pltpu.VMEM((two, 640), BF16),
            pltpu.VMEM((N_CTX, two, BLOCK), F32),
            pltpu.VMEM((lines, LATENT), BF16),
            pltpu.VMEM((N_TP, 16, width // 4), BF16),
            pltpu.VMEM((N_TP, 16, width // 4), BF16),
            dma((8,)),
            dma((len(CHUNKS),)),
            dma((5, 2)),
            dma((5, 2)),
            dma((2, 4)),
            dma((2, 4)),
            dma((N_STATION + 1,)),
            dma((N_STATION + 1,)),
            dma((len(CHUNKS), N_TP)),
            dma((len(CHUNKS), N_TP)),
        ],
        compiler_params=pltpu.CompilerParams(collective_id=0, has_side_effects=True, vmem_limit_bytes=60 * MIB),
        name="latent_attention",
    )(lens, place, rlen, q, own, wk, wv, ct, dq, fresh, w)


def on_device(
    prefill_query,
    span_latent,
    prompt_lengths,
    key_weight,
    value_weight,
    placement,
    resident_cache,
    resident_lengths,
    decode_query,
    decode_latent,
    out_weight,
):
    cache_t = jnp.swapaxes(resident_cache, 1, 2).reshape(ROWS * WIDTH, BLOCK)
    return mega(
        prompt_lengths,
        placement,
        resident_lengths,
        prefill_query,
        span_latent.T,
        key_weight,
        value_weight,
        cache_t,
        decode_query,
        decode_latent,
        out_weight,
    )


def solution(mesh):
    placed = (
        P("ctx", "tp"),
        P("ctx", None),
        P(),
        P(None, "tp"),
        P(None, "tp"),
        P(),
        P("ctx", None, None),
        P("ctx"),
        P("ctx", None, "tp"),
        P("ctx", None, None),
        P("tp", None),
    )
    return jax.shard_map(
        on_device,
        mesh=mesh,
        in_specs=placed,
        out_specs=(P("ctx", "tp"), P(("ctx", "tp"), None, None)),
        check_vma=False,
    )
```
